128 devices in a mesh: outer: 4 (over x), inner: 32 (over y, z, core).
Axes of the slice: x: 4, y: 4, z: 4, core: 2. Of those that a mesh axis runs over, the one named last changes fastest.
Arguments:
- conv_input: bfloat16 [16384, 4096], P(('outer', 'inner')), may hold values from -6 to 6
- grad_out: bfloat16 [16384, 4096], P(('outer', 'inner')), may hold values from -6 to 6
- conv_w: float32 [4, 4096], replicated, may hold values from -3 to 3
- conv_b: float32 [4096], replicated, may hold values from -3 to 3
- w_x: bfloat16 [16, 256, 256], replicated, may hold values from -0.375 to 0.375
- b_x: float32 [4096], replicated, may hold values from -4 to 4
- w_a: bfloat16 [16, 256, 256], replicated, may hold values from -0.375 to 0.375
- b_a: float32 [4096], replicated, may hold values from -2 to 2
- a_param: float32 [4096], replicated, as said below
Outputs:
- grad_u: bfloat16 [16384, 4096], P(('outer', 'inner'))
- grad_w_x: float32 [16, 256, 256], replicated
- grad_w_a: float32 [16, 256, 256], replicated
- grad_b_x: float32 [4096], replicated
- grad_b_a: float32 [4096], replicated
- grad_a_param: float32 [4096], replicated
- grad_conv_w: float32 [4, 4096], replicated
- grad_conv_b: float32 [4096], replicated
The draws below stay inside these ranges and needn't reach their ends.
Inputs may be any that keep to these rules, and one draw needn't show every extreme that they name: `a_param`: each entry is the inverse softplus of a positive rate of at most 0.02.
All inputs are finite; a program needn't handle non-finite values.
Results may differ from the reference program's by a relative error of at most 0.0065.
Values may be sent and summed in bfloat16 or wider, within the bound.
No kernel may reach another device: no remote copies, remote signals or barrier semaphores. Data moves between devices by JAX's collectives and lax.ppermute only.
A program may use at most 128 MiB of HBM per device.

```python
import math
import jax
import jax.numpy as jnp
from jax import lax

D = 4096
HEADS = 16
CONV = 4
TOK_DEV = 128
HEAD_W = 256
LENGTH = 16384
N_OUTER = 4
N_INNER = 32


def draw_a_param(key, part):
    key = jax.random.fold_in(key, 11)
    pick_key, slow_key, fast_key = jax.random.split(key, 3)
    share = 0.5
    chooser = jax.random.uniform(pick_key, (D,), jnp.float32)
    slow = jnp.exp(jax.random.uniform(slow_key, (D,), jnp.float32, math.log(0.05 / LENGTH), math.log(0.5 / LENGTH)))
    fast = jnp.exp(jax.random.uniform(fast_key, (D,), jnp.float32, math.log(0.002), math.log(0.02)))
    rates = jnp.where(chooser < share, slow, fast)
    return jnp.log(jnp.expm1(rates))


def shard_levels(key, shape, pieces, low, top_value):
    gain, own = 1.0, jax.random.fold_in(key, 6)
    for axis_at, blocks in pieces:
        draws = jnp.exp(jax.random.uniform(jax.random.fold_in(own, axis_at), (blocks,), jnp.float32, low / len(pieces), top_value / len(pieces)))
        gain = gain * jnp.repeat(draws, shape[axis_at] // blocks).reshape([-1 if axis == axis_at else 1 for axis in range(len(shape))])
    return gain


def noise(rng, dims, spread, bound, cuts=(), held_as=jnp.bfloat16):
    values = spread * jax.random.normal(rng, dims, jnp.float32)
    if cuts:
        values = values * shard_levels(rng, dims, cuts, -0.22, 0.18)
    return jnp.clip(values, -bound, bound).astype(held_as)


def setup_inputs(seed: int = 0) -> dict:
    streams_of = jax.random.split(jax.random.key(seed), 10)
    return {
        "conv_input": noise(streams_of[0], (LENGTH, D), 1.0, 6.0, ((0, 128),)),
        "grad_out": noise(streams_of[1], (LENGTH, D), 1.0, 6.0, ((0, 128),)),
        "conv_w": noise(streams_of[2], (CONV, D), 0.5, 3.0, (), jnp.float32),
        "conv_b": noise(streams_of[3], (D,), 0.5, 3.0, (), jnp.float32),
        "w_x": noise(streams_of[4], (HEADS, HEAD_W, HEAD_W), HEAD_W ** -0.5, 0.375),
        "b_x": noise(streams_of[5], (D,), 1.0, 4.0, (), jnp.float32),
        "w_a": noise(streams_of[6], (HEADS, HEAD_W, HEAD_W), HEAD_W ** -0.5, 0.375),
        "b_a": jnp.clip(jax.random.uniform(streams_of[7], (D,), jnp.float32, -2.0, 2.0), -2.0, 2.0),
        "a_param": draw_a_param(jax.random.fold_in(streams_of[9], 71), 0),
    }


root_floor = 2.5e-07

def pair_combine(earlier, later):
    return (earlier[0] * later[0], later[0] * earlier[1] + later[1])

def block_gates(u_ext, conv_w, conv_b, w_x, b_x, w_a, b_a, rate):
    rows = u_ext.shape[0] - (CONV - 1)
    mixed = jnp.zeros((rows, D), jnp.float32) + conv_b[None, :]
    for k in range(CONV):
        mixed = mixed + conv_w[k][None, :] * u_ext[CONV - 1 - k:CONV - 1 - k + rows].astype(jnp.float32)
    mixed_b = mixed.astype(jnp.bfloat16)
    heads_in = mixed_b.astype(jnp.float32).reshape(rows, HEADS, HEAD_W)
    z_x = jnp.einsum('thi,hij->thj', heads_in, w_x.astype(jnp.float32)).reshape(rows, D) + b_x[None, :]
    z_a = jnp.einsum('thi,hij->thj', heads_in, w_a.astype(jnp.float32)).reshape(rows, D) + b_a[None, :]
    gate_x = jax.nn.sigmoid(z_x)
    gate_a = jax.nn.sigmoid(z_a)
    log_decay = -8.0 * gate_a * rate[None, :]
    decay = jnp.exp(log_decay)
    vari = -jnp.expm1(2.0 * log_decay)
    mult = jnp.sqrt(vari)
    drive = gate_x * mixed * mult
    return (mixed, mixed_b, gate_x, gate_a, decay, vari, mult, drive)

def reference(conv_input, grad_out, conv_w, conv_b, w_x, b_x, w_a, b_a, a_param):
    rate = jax.nn.softplus(a_param)
    blocks = N_OUTER * N_INNER
    u_pad = jnp.concatenate([jnp.zeros((CONV - 1, D), conv_input.dtype), conv_input], axis=0)
    indices = jnp.arange(blocks).astype(jnp.int32)

    def forward_step(carried, index):
        u_ext = lax.dynamic_slice_in_dim(u_pad, (index * TOK_DEV).astype(jnp.int32), TOK_DEV + CONV - 1, 0)
        parts = block_gates(u_ext, conv_w, conv_b, w_x, b_x, w_a, b_a, rate)
        prods, states = lax.associative_scan(pair_combine, (parts[4], parts[5 + 2]))
        return (prods[-1] * carried + states[-1], carried)
    _, starts = lax.scan(forward_step, jnp.zeros((D,), jnp.float32), indices)
    zero_w = jnp.zeros((HEADS, HEAD_W, HEAD_W), jnp.float32)
    zero_d = jnp.zeros((D,), jnp.float32)
    init = (zero_d, jnp.zeros((CONV - 1, D), jnp.float32), (zero_w, zero_w, zero_d, zero_d, zero_d, jnp.zeros((CONV, D), jnp.float32), zero_d))

    def backward_step(carried, inputs):
        entry, head_next, sums = carried
        index, start = inputs
        u_ext = lax.dynamic_slice_in_dim(u_pad, (index * TOK_DEV).astype(jnp.int32), TOK_DEV + CONV - 1, 0)
        mixed, mixed_b, gate_x, gate_a, decay, vari, mult, drive = block_gates(u_ext, conv_w, conv_b, w_x, b_x, w_a, b_a, rate)
        upstream = lax.dynamic_slice_in_dim(grad_out, (index * TOK_DEV).astype(jnp.int32), TOK_DEV, 0).astype(jnp.float32)
        prods, states = lax.associative_scan(pair_combine, (decay, drive))
        state = states + prods * start[None, :]
        state_prev = jnp.concatenate([start[None, :], state[:-1]], axis=0)
        factors = jnp.concatenate([decay[1:], jnp.ones((1, D), jnp.float32)], axis=0)
        back_prod, back_adj = lax.associative_scan(pair_combine, (jnp.flip(factors, 0), jnp.flip(upstream, 0)))
        adjoint = jnp.flip(back_adj, 0) + jnp.flip(back_prod, 0) * entry[None, :]
        grad_log = adjoint * state_prev * decay - adjoint * gate_x * mixed * decay * decay / jnp.sqrt(jnp.maximum(vari, root_floor))
        rate_terms = -8.0 * gate_a * grad_log
        dz_a = -8.0 * rate[None, :] * grad_log * gate_a * (1.0 - gate_a)
        dz_x = adjoint * mixed * mult * gate_x * (1.0 - gate_x)
        dz_a_b = dz_a.astype(jnp.bfloat16).astype(jnp.float32).reshape(TOK_DEV, HEADS, HEAD_W)
        dz_x_b = dz_x.astype(jnp.bfloat16).astype(jnp.float32).reshape(TOK_DEV, HEADS, HEAD_W)
        heads_in = mixed_b.astype(jnp.float32).reshape(TOK_DEV, HEADS, HEAD_W)
        grad_mixed = adjoint * gate_x * mult
        grad_mixed = grad_mixed + jnp.einsum('thj,hij->thi', dz_x_b, w_x.astype(jnp.float32)).reshape(TOK_DEV, D)
        grad_mixed = grad_mixed + jnp.einsum('thj,hij->thi', dz_a_b, w_a.astype(jnp.float32)).reshape(TOK_DEV, D)
        gwx = sums[0] + jnp.einsum('thi,thj->hij', heads_in, dz_x_b)
        gwa = sums[1] + jnp.einsum('thi,thj->hij', heads_in, dz_a_b)
        taps = jnp.stack([lax.optimization_barrier(jnp.sum(grad_mixed * u_ext[CONV - 1 - k:CONV - 1 - k + TOK_DEV].astype(jnp.float32), axis=0)) for k in range(CONV)], axis=0)
        new_sums = (gwx, gwa, sums[2] + lax.optimization_barrier(jnp.sum(dz_x, axis=0)), sums[3] + lax.optimization_barrier(jnp.sum(dz_a, axis=0)), sums[4] + lax.optimization_barrier(jnp.sum(rate_terms, axis=0)), sums[5] + taps, sums[6] + lax.optimization_barrier(jnp.sum(grad_mixed, axis=0)))
        extended = jnp.concatenate([grad_mixed, head_next], axis=0)
        grad_in = jnp.zeros((TOK_DEV, D), jnp.float32)
        for k in range(CONV):
            grad_in = grad_in + conv_w[k][None, :] * extended[k:k + TOK_DEV]
        new_entry = decay[0] * adjoint[0]
        return ((new_entry, grad_mixed[:CONV - 1], new_sums), grad_in.astype(jnp.bfloat16))
    final, grad_blocks = lax.scan(backward_step, init, (indices, starts), reverse=True)
    sums = final[2]
    grad_u = grad_blocks.reshape(LENGTH, D)
    grad_a_param = jax.nn.sigmoid(a_param) * sums[4]
    return (grad_u, sums[0], sums[1], sums[2], sums[3], grad_a_param, sums[5], sums[6])
```

```python
import functools

import jax
import jax.numpy as jnp
from jax import lax
from jax.experimental import pallas as pl
from jax.experimental.pallas import tpu as pltpu
from jax.sharding import PartitionSpec as P

AXES = ("outer", "inner")
F32, BF16 = jnp.float32, jnp.bfloat16
TOK = 128
CHIP_TOK = 256
GROUPS = CHIP_TOK // 8
WIDTH = 4096
HALF = 2048
HEAD_W = 256
HEADS = 8
MARGIN = 3
EDGE = 8 * MARGIN
ROOT_FLOOR = 2.5e-07
VMEM_LIMIT = 48 * 1024 * 1024


def place(index):
    return [index // 32, (index // 8) % 4, (index // 2) % 4, index % 2]


def number(coords):
    return coords[0] * 32 + coords[1] * 8 + coords[2] * 2 + coords[3]


def turned(axis, steps):
    size = 2 if axis == 3 else 4
    pairs = []
    for source in range(128):
        coords = place(source)
        coords[axis] = (coords[axis] + steps) % size
        pairs.append((source, number(coords)))
    return pairs


def send_on(value, axis, steps):
    return lax.ppermute(value, AXES, turned(axis, steps))


def swap_cores(value):
    return send_on(value, 3, 1)


def dot(a, b, dims):
    return lax.dot_general(a, b, (dims, ((), ())), preferred_element_type=F32)


def orders(core):
    row = lax.broadcasted_iota(jnp.int32, (CHIP_TOK, TOK), 0)
    col = lax.broadcasted_iota(jnp.int32, (CHIP_TOK, TOK), 1)
    token = (row % 8) * GROUPS + row // 8
    own = (token == col + core * TOK).astype(F32).astype(BF16)
    other = (token == col + (1 - core) * TOK).astype(F32).astype(BF16)
    return own, other


def wide(row, rows):
    return jnp.broadcast_to(row, (rows, row.shape[1]))


def load_conv_input(u_s, u, halo):
    sub = lax.broadcasted_iota(jnp.int32, (8, HEAD_W), 0)
    u_s[EDGE:, :] = u
    for k in range(1, MARGIN + 1):
        last = u_s[EDGE + CHIP_TOK - 8 * k : EDGE + CHIP_TOK - 8 * (k - 1), :]
        first = wide(halo[MARGIN - k : MARGIN - k + 1, :].astype(F32), 8)
        u_s[EDGE - 8 * k : EDGE - 8 * (k - 1), :] = jnp.where(
            sub == 0, first, pltpu.roll(last, 1, 0)
        )


def forward_kernel(
    at, u_own, g_own, other_in, halo_in, par, w_x, w_a,
    decay_o, drive_o, quot_o, ga_o, gx_o, gk_o, mixed_o, lead_o, total_o,
    u_s, g_s, mix_s, zx_s, za_s,
):
    own, other = orders(at[0])
    u = dot(own, u_own[...], ((1,), (0,))) + dot(other, other_in[:TOK, :], ((1,), (0,)))
    g_s[...] = dot(own, g_own[...], ((1,), (0,))) + dot(other, other_in[TOK:, :], ((1,), (0,)))
    load_conv_input(u_s, u, halo_in[...])
    step = 16
    taps = [wide(par[k : k + 1, :], step) for k in range(MARGIN + 1)]
    bias = wide(par[4:5, :], step)
    for c in range(0, CHIP_TOK, step):
        mixed = bias
        for k in range(MARGIN + 1):
            mixed = mixed + taps[k] * u_s[EDGE - 8 * k + c : EDGE - 8 * k + c + step, :]
        mix_s[c : c + step, :] = mixed
        mixed_o[c : c + step, :] = mixed.astype(BF16)
    mixed_b = mixed_o[...]
    zx_s[...] = dot(mixed_b, w_x[0], ((1,), (0,)))
    za_s[...] = dot(mixed_b, w_a[0], ((1,), (0,)))
    b_x, b_a = wide(par[5:6, :], step), wide(par[6:7, :], step)
    slope = wide(-8.0 * par[7:8, :], step)
    prod = jnp.ones((8, HEAD_W), F32)
    state = jnp.zeros((8, HEAD_W), F32)
    back = jnp.zeros((8, HEAD_W), F32)
    for c in range(0, CHIP_TOK, step):
        rows = slice(c, c + step)
        mixed = mix_s[rows, :]
        gate_x = jax.nn.sigmoid(zx_s[rows, :] + b_x)
        gate_a = jax.nn.sigmoid(za_s[rows, :] + b_a)
        x = slope * gate_a
        series = 1.0 / 120.0 + x * (1.0 / 720.0)
        for coef in (1.0 / 24.0, 1.0 / 6.0, 0.5, 1.0):
            series = coef + x * series
        less = x * series
        decay = 1.0 + less
        vari = -less * (2.0 + less)
        mult = jnp.sqrt(vari)
        gk = gate_x * mult
        drive = gk * mixed
        decay_o[rows, :] = decay
        drive_o[rows, :] = drive
        quot_o[rows, :] = (
            gate_x * mixed * (decay * decay) * lax.rsqrt(jnp.maximum(vari, ROOT_FLOOR))
        )
        ga_o[rows, :] = -8.0 * gate_a
        gx_o[rows, :] = gate_x
        gk_o[rows, :] = gk
        for h in (0, 8):
            part = decay[h : h + 8]
            prod = prod * part
            state = part * state + drive[h : h + 8]
            back = back + prod * g_s[c + h : c + h + 8, :]
    sub = lax.broadcasted_iota(jnp.int32, (8, HEAD_W), 0)
    fprod, fstate = prod, state
    bprod, bstate = prod, back
    for d in (1, 2, 4):
        up = sub >= d
        fstate = jnp.where(up, fprod * pltpu.roll(fstate, d, 0) + fstate, fstate)
        fprod = jnp.where(up, fprod * pltpu.roll(fprod, d, 0), fprod)
        down = sub < 8 - d
        bstate = jnp.where(down, bprod * pltpu.roll(bstate, 8 - d, 0) + bstate, bstate)
        bprod = jnp.where(down, bprod * pltpu.roll(bprod, 8 - d, 0), bprod)
    lead_o[0:8, :] = jnp.where(sub == 0, 1.0, pltpu.roll(fprod, 1, 0))
    lead_o[8:16, :] = jnp.where(sub == 0, 0.0, pltpu.roll(fstate, 1, 0))
    lead_o[16:24, :] = jnp.where(sub == 7, 1.0, pltpu.roll(bprod, 7, 0))
    lead_o[24:32, :] = jnp.where(sub == 7, 0.0, pltpu.roll(bstate, 7, 0))
    total_o[0:1, :] = fprod[7:8]
    total_o[1:2, :] = fstate[7:8]
    total_o[2:3, :] = bstate[0:1]


def forward_pass(at, conv_input, grad_out, other_in, halo, par, w_x, w_a):
    head = lambda h, at: (0, at[0] * HEADS + h)
    local = lambda h, at: (0, h)
    full = pl.BlockSpec((CHIP_TOK, HEAD_W), local)
    big = jax.ShapeDtypeStruct((CHIP_TOK, HALF), F32)
    return pl.pallas_call(
        forward_kernel,
        grid_spec=pltpu.PrefetchScalarGridSpec(
            num_scalar_prefetch=1,
            grid=(HEADS,),
            in_specs=[
                pl.BlockSpec((TOK, HEAD_W), head),
                pl.BlockSpec((TOK, HEAD_W), head),
                full,
                pl.BlockSpec((MARGIN, HEAD_W), local),
                pl.BlockSpec((8, HEAD_W), head),
                pl.BlockSpec((1, HEAD_W, HEAD_W), lambda h, at: (at[0] * HEADS + h, 0, 0)),
                pl.BlockSpec((1, HEAD_W, HEAD_W), lambda h, at: (at[0] * HEADS + h, 0, 0)),
            ],
            out_specs=[full] * 7
            + [pl.BlockSpec((32, HEAD_W), local), pl.BlockSpec((3, HEAD_W), local)],
            scratch_shapes=[pltpu.VMEM((EDGE + CHIP_TOK, HEAD_W), F32)]
            + [pltpu.VMEM((CHIP_TOK, HEAD_W), F32)] * 4,
        ),
        out_shape=[big] * 6
        + [
            jax.ShapeDtypeStruct((CHIP_TOK, HALF), BF16),
            jax.ShapeDtypeStruct((32, HALF), F32),
            jax.ShapeDtypeStruct((3, HALF), F32),
        ],
        compiler_params=pltpu.CompilerParams(vmem_limit_bytes=VMEM_LIMIT),
        name="gates",
    )(at, conv_input, grad_out, other_in, halo, par, w_x, w_a)


def join_kernel(axis, first, last, at, own, r1, r2, r3, *refs):
    before = None if first else refs[0]
    outs = refs if first else refs[1:]
    here = at[1 + axis]
    rows = lambda ref: [ref[i : i + 1, :] for i in range(3)]
    t0, f0, b0 = rows(own)
    pieces = [rows(r) for r in (r1, r2, r3)]
    one, zero = jnp.ones_like(t0), jnp.zeros_like(t0)
    early = [jnp.full(t0.shape, here + k >= 4) for k in (1, 2, 3)]
    pt, pf = one, zero
    for k in range(3):
        t, f, _ = pieces[k]
        pf = jnp.where(early[k], t * pf + f, pf)
        pt = jnp.where(early[k], t * pt, pt)
    bt, bs = one, zero
    for k in (2, 1, 0):
        t, _, b = pieces[k]
        bs = jnp.where(early[k], bs, t * bs + b)
        bt = jnp.where(early[k], bt, t * bt)
    if first:
        acc = [pt, pf, bt, bs]
    else:
        ep, es, fp, fs = [before[i : i + 1, :] for i in range(4)]
        acc = [ep * pt, ep * pf + es, fp * bt, fp * bs + fs]
    if last:
        outs[0][0:1, :] = acc[1]
        outs[0][1:2, :] = acc[3]
        return
    f = t0 * pf + f0
    for k in range(3):
        f = jnp.where(early[k], f, pieces[k][0] * f + pieces[k][1])
    b = t0 * bs + b0
    for k in (2, 1, 0):
        b = jnp.where(early[k], pieces[k][0] * b + pieces[k][2], b)
    outs[0][0:1, :] = pt * t0 * bt
    outs[0][1:2, :] = f
    outs[0][2:3, :] = b
    for i in range(4):
        outs[1][i : i + 1, :] = acc[i]


def whole(count):
    return [pl.BlockSpec(memory_space=pltpu.VMEM)] * count


def entering(at, total):
    acc = None
    value = total
    for axis in (2, 1, 0):
        first, last = axis == 2, axis == 0
        args = [value] + [send_on(value, axis, -k) for k in (1, 2, 3)]
        if not first:
            args.append(acc)
        if last:
            shapes = [jax.ShapeDtypeStruct((2, HALF), F32)]
        else:
            shapes = [jax.ShapeDtypeStruct((3, HALF), F32), jax.ShapeDtypeStruct((4, HALF), F32)]
        out = pl.pallas_call(
            functools.partial(join_kernel, axis, first, last),
            in_specs=[pl.BlockSpec(memory_space=pltpu.SMEM)] + whole(len(args)),
            out_specs=whole(len(shapes)),
            out_shape=shapes,
            name="join",
        )(at, *args)
        if last:
            return out[0]
        value, acc = out


def backward_kernel(
    keep, chained, at, u_own, other_in, g_own, halo_in, par, w_x, w_a,
    decay, drive, quot, ga, gx, gk, mixed_b, lead, carry, *refs
):
    if chained:
        refs = refs[3:]
    piece_o, own_o, send_o, edge_o, u_s, g_s, a_s, dx_s, da_s, gm_s = refs
    step_at = pl.program_id(0)
    own, other = orders(at[0])
    u = dot(own, u_own[...], ((1,), (0,))) + dot(other, other_in[:TOK, :], ((1,), (0,)))
    g_s[...] = dot(own, g_own[...], ((1,), (0,))) + dot(other, other_in[TOK:, :], ((1,), (0,)))
    load_conv_input(u_s, u, halo_in[...])
    state = lead[8:16, :] + lead[0:8, :] * wide(carry[0:1, :], 8)
    back = lead[24:32, :] + lead[16:24, :] * wide(carry[1:2, :], 8)
    for r in range(GROUPS - 1, -1, -1):
        rows = slice(8 * r, 8 * r + 8)
        adjoint = g_s[rows, :] + back
        a_s[rows, :] = adjoint
        back = decay[rows, :] * adjoint
    rate = wide(par[7:8, :], 8)
    eighth = 0.125 * rate
    zero = jnp.zeros((8, HEAD_W), F32)
    sum_x, sum_a, sum_rate = zero, zero, zero
    for r in range(0, GROUPS, 2):
        pair_x, pair_a = [], []
        for q in (r, r + 1):
            rows = slice(8 * q, 8 * q + 8)
            adjoint = a_s[rows, :]
            passed = state * decay[rows, :]
            drv = drive[rows, :]
            grad_log = adjoint * (passed - quot[rows, :])
            state = passed + drv
            gate = ga[rows, :]
            term = gate * grad_log
            dz_a = term * (rate + eighth * gate)
            dz_x = adjoint * drv * (1.0 - gx[rows, :])
            sum_rate = sum_rate + term
            sum_a = sum_a + dz_a
            sum_x = sum_x + dz_x
            gm_s[rows, :] = adjoint * gk[rows, :]
            pair_x.append(dz_x)
            pair_a.append(dz_a)
        rows = slice(8 * r, 8 * r + 16)
        dx_s[rows, :] = jnp.concatenate(pair_x, 0).astype(BF16)
        da_s[rows, :] = jnp.concatenate(pair_a, 0).astype(BF16)
    dz_x, dz_a = dx_s[...], da_s[...]
    gm_s[:CHIP_TOK, :] += dot(dz_x, w_x[0], ((1,), (1,))) + dot(dz_a, w_a[0], ((1,), (1,)))
    mixed = mixed_b[...]
    local_x = dot(mixed, dz_x, ((0,), (0,)))
    local_a = dot(mixed, dz_a, ((0,), (0,)))
    at_row = pl.ds(pl.multiple_of(step_at * HEAD_W, HEAD_W), HEAD_W)
    piece_o[at_row, 0:HEAD_W] = local_x.astype(piece_o.dtype)
    piece_o[at_row, HEAD_W : 2 * HEAD_W] = local_a.astype(piece_o.dtype)
    sub = lax.broadcasted_iota(jnp.int32, (8, HEAD_W), 0)
    for j in range(MARGIN):
        first = gm_s[8 * j : 8 * j + 8, :]
        gm_s[CHIP_TOK + 8 * j : CHIP_TOK + 8 * j + 8, :] = jnp.where(
            sub == 7, 0.0, pltpu.roll(first, 7, 0)
        )
        edge_o[MARGIN + j : MARGIN + j + 1, :] = first[0:1]
    taps = [wide(par[k : k + 1, :], 8) for k in range(MARGIN + 1)]
    sum_c, sum_k = zero, [zero] * (MARGIN + 1)
    for r in range(0, GROUPS, 2):
        pair = []
        for q in (r, r + 1):
            here = gm_s[8 * q : 8 * q + 8, :]
            sum_c = sum_c + here
            grad = taps[0] * here
            for k in range(1, MARGIN + 1):
                grad = grad + taps[k] * gm_s[8 * (q + k) : 8 * (q + k) + 8, :]
            for k in range(MARGIN + 1):
                lo = EDGE + 8 * (q - k)
                sum_k[k] = sum_k[k] + here * u_s[lo : lo + 8, :]
            if q >= GROUPS - MARGIN:
                edge_o[q - GROUPS + MARGIN : q - GROUPS + MARGIN + 1, :] = grad[7:8]
            pair.append(grad)
        dx_s[8 * r : 8 * r + 16, :] = jnp.concatenate(pair, 0).astype(BF16)
    grad_b = dx_s[...]
    own_o[...] = dot(own, grad_b, ((0,), (0,))).astype(BF16)
    send_o[...] = dot(other, grad_b, ((0,), (0,))).astype(BF16)
    sums = [sum_x, sum_a, sum_rate] + sum_k + [sum_c]
    small = jnp.concatenate([jnp.sum(s, axis=0, keepdims=True) for s in sums], 0)
    at_col = pl.ds(pl.multiple_of(step_at * HEAD_W, HEAD_W), HEAD_W)
    if keep:
        piece_o[2 * HEAD_W :, at_col] = small
    else:
        high = small.astype(BF16).astype(F32)
        piece_o[2 * HEAD_W :, at_col] = jnp.concatenate([high, small - high], 0).astype(BF16)


def backward_chunk(k, at, operands, blocks):
    keep = k == 0
    chained = blocks is not None
    head = lambda j, at: 2 * lax.rem(at[1] + k, 4) + j
    local = lambda j, at: (0, head(j, at))
    outer = lambda j, at: (0, at[0] * HEADS + head(j, at))
    matrix = lambda j, at: (at[0] * HEADS + head(j, at), 0, 0)
    full = pl.BlockSpec((CHIP_TOK, HEAD_W), local)
    in_specs = [
        pl.BlockSpec((TOK, HEAD_W), outer),
        full,
        pl.BlockSpec((TOK, HEAD_W), outer),
        pl.BlockSpec((MARGIN, HEAD_W), local),
        pl.BlockSpec((8, HEAD_W), outer),
        pl.BlockSpec((1, HEAD_W, HEAD_W), matrix),
        pl.BlockSpec((1, HEAD_W, HEAD_W), matrix),
    ] + [full] * 7 + [pl.BlockSpec((32, HEAD_W), local), pl.BlockSpec((2, HEAD_W), local)]
    aliases = {}
    if chained:
        aliases = {1 + len(in_specs) + i: 1 + i for i in range(3)}
        in_specs = in_specs + [pl.BlockSpec(memory_space=pl.ANY)] * 3
    piece = ((520, 512), F32) if keep else ((528, 512), BF16)
    out = pl.pallas_call(
        functools.partial(backward_kernel, keep, chained),
        grid_spec=pltpu.PrefetchScalarGridSpec(
            num_scalar_prefetch=1,
            grid=(2,),
            in_specs=in_specs,
            out_specs=[
                pl.BlockSpec(piece[0], lambda j, at: (0, 0)),
                pl.BlockSpec((TOK, HEAD_W), local),
                pl.BlockSpec((TOK, HEAD_W), local),
                pl.BlockSpec((8, HEAD_W), local),
            ],
            scratch_shapes=[
                pltpu.VMEM((EDGE + CHIP_TOK, HEAD_W), F32),
                pltpu.VMEM((CHIP_TOK, HEAD_W), F32),
                pltpu.VMEM((CHIP_TOK, HEAD_W), F32),
                pltpu.VMEM((CHIP_TOK, HEAD_W), BF16),
                pltpu.VMEM((CHIP_TOK, HEAD_W), BF16),
                pltpu.VMEM((EDGE + CHIP_TOK, HEAD_W), F32),
            ],
        ),
        out_shape=[
            jax.ShapeDtypeStruct(*piece),
            jax.ShapeDtypeStruct((TOK, HALF), BF16),
            jax.ShapeDtypeStruct((TOK, HALF), BF16),
            jax.ShapeDtypeStruct((8, HALF), F32),
        ],
        input_output_aliases=aliases,
        compiler_params=pltpu.CompilerParams(vmem_limit_bytes=VMEM_LIMIT),
        name="grads",
    )(at, *operands, *(blocks or ()))
    return out[0], tuple(out[1:])


def split_sum(small):
    high = small.astype(BF16).astype(F32)
    return jnp.concatenate([high, small - high], 0).astype(BF16)


def add_kernel(axis, rows, at, own, r1, r2, r3, *refs):
    total = own[0:rows, :]
    small = own[rows : rows + 8, :]
    for r in (r1, r2, r3):
        total = total + r[0:rows, :].astype(F32)
        parts = r[rows : rows + 16, :].astype(F32)
        small = small + (parts[0:8] + parts[8:16])
    if axis is None:
        refs[0][0:rows, :] = total.astype(BF16)
        refs[0][rows : rows + 16, :] = split_sum(small)
        return
    outs, acc = refs[:4], refs[4]
    acc[...] = total
    part = rows // 4
    for k in range(4):
        first = lax.rem(at[1 + axis] + k, 4) * part
        chunk = acc[pl.ds(pl.multiple_of(first, part), part), :]
        if k == 0:
            outs[0][0:part, :] = chunk
            outs[0][part : part + 8, :] = small
        else:
            outs[k][0:part, :] = chunk.astype(BF16)
            outs[k][part : part + 16, :] = split_sum(small)


def add_stage(axis, rows, at, own, arrived):
    if axis is None:
        shapes = [jax.ShapeDtypeStruct((rows + 16, 512), BF16)]
        scratch = []
    else:
        part = rows // 4
        shapes = [jax.ShapeDtypeStruct((part + 8, 512), F32)]
        shapes += [jax.ShapeDtypeStruct((part + 16, 512), BF16)] * 3
        scratch = [pltpu.VMEM((rows, 512), F32)]
    return pl.pallas_call(
        functools.partial(add_kernel, axis, rows),
        in_specs=[pl.BlockSpec(memory_space=pltpu.SMEM)] + whole(4),
        out_specs=whole(len(shapes)),
        out_shape=shapes,
        scratch_shapes=scratch,
        compiler_params=pltpu.CompilerParams(vmem_limit_bytes=VMEM_LIMIT),
        name="add",
    )(at, own, *arrived)


def lay_kernel(axis, rows, tail, at, own, r1, r2, r3, *refs):
    out = refs[-1]
    for k, ref in enumerate((own, r1, r2, r3)):
        first = lax.rem(at[1 + axis] + k, 4) * rows
        out[pl.ds(pl.multiple_of(first, rows), rows), :] = ref[0:rows, :]
    if tail:
        out[4 * rows : 4 * rows + 16, :] = refs[0][32:48, :]


def lay_out(axis, rows, at, pieces, tail=None):
    extra = [] if tail is None else [tail]
    return pl.pallas_call(
        functools.partial(lay_kernel, axis, rows, tail is not None),
        in_specs=[pl.BlockSpec(memory_space=pltpu.SMEM)] + whole(4 + len(extra)),
        out_specs=pl.BlockSpec(memory_space=pltpu.VMEM),
        out_shape=jax.ShapeDtypeStruct((4 * rows + 16 * len(extra), 512), BF16),
        compiler_params=pltpu.CompilerParams(vmem_limit_bytes=VMEM_LIMIT),
        name="lay",
    )(at, *pieces, *extra)


def final_kernel(at, a_param, *refs):
    pieces, outs = refs[:8], refs[8:]
    wx_o, wa_o, bx_o, ba_o, ap_o, taps_o, cb_o = outs
    step = pl.program_id(0)
    for i in range(8):
        owner = at[0] if i < 4 else 1 - at[0]
        chunk = lax.rem(at[1] + i % 4, 4)

        @pl.when(step // 2 == i)
        def _(ref=pieces[i]):
            row = pl.ds(pl.multiple_of(lax.rem(step, 2) * HEAD_W, HEAD_W), HEAD_W)
            wx_o[0] = ref[row, 0:HEAD_W].astype(F32)
            wa_o[0] = ref[row, HEAD_W : 2 * HEAD_W].astype(F32)

        @pl.when(step == 2 * i)
        def _(ref=pieces[i]):
            parts = ref[2 * HEAD_W : 2 * HEAD_W + 16, :].astype(F32)
            small = parts[0:8] + parts[8:16]
            cols = pl.ds(pl.multiple_of(owner * HALF + chunk * 512, 512), 512)
            bx_o[:, cols] = small[0:1]
            ba_o[:, cols] = small[1:2]
            ap_o[:, cols] = small[2:3] * jax.nn.sigmoid(a_param[:, cols])
            taps_o[:, cols] = small[3:7]
            cb_o[:, cols] = small[7:8]


def write_out(at, a_param, pieces):
    def head(step, at):
        i = step // 2
        owner = jnp.where(i < 4, at[0], 1 - at[0])
        return owner * HEADS + 2 * lax.rem(at[1] + i, 4) + lax.rem(step, 2)

    fixed = lambda step, at: (0, 0)
    matrix = pl.BlockSpec((1, HEAD_W, HEAD_W), lambda step, at: (head(step, at), 0, 0))
    row = pl.BlockSpec((1, WIDTH), fixed)
    big = jax.ShapeDtypeStruct((2 * HEADS, HEAD_W, HEAD_W), F32)
    line = jax.ShapeDtypeStruct((1, WIDTH), F32)
    return pl.pallas_call(
        final_kernel,
        grid_spec=pltpu.PrefetchScalarGridSpec(
            num_scalar_prefetch=1,
            grid=(2 * HEADS,),
            in_specs=whole(9),
            out_specs=[matrix, matrix, row, row, row, pl.BlockSpec((4, WIDTH), fixed), row],
        ),
        out_shape=[big, big, line, line, line, jax.ShapeDtypeStruct((4, WIDTH), F32), line],
        compiler_params=pltpu.CompilerParams(vmem_limit_bytes=VMEM_LIMIT),
        name="unpack",
    )(at, a_param, *pieces)


def assemble_kernel(at, own, other, fix, out):
    mine = pl.program_id(0) == at[0]

    @pl.when(mine)
    def _():
        out[...] = own[...]

        @pl.when(at[0] == 1)
        def _():
            tail = out[TOK - 16 :, :].astype(F32)
            out[TOK - 16 :, :] = jnp.concatenate([tail[: 16 - MARGIN], fix[0:MARGIN, :]], 0).astype(
                BF16
            )

    @pl.when(jnp.logical_not(mine))
    def _():
        out[...] = other[...]


def assemble(at, own, other, fix):
    return pl.pallas_call(
        assemble_kernel,
        grid_spec=pltpu.PrefetchScalarGridSpec(
            num_scalar_prefetch=1,
            grid=(2,),
            in_specs=whole(3),
            out_specs=pl.BlockSpec((TOK, HALF), lambda i, at: (0, i)),
        ),
        out_shape=jax.ShapeDtypeStruct((TOK, WIDTH), BF16),
        compiler_params=pltpu.CompilerParams(vmem_limit_bytes=VMEM_LIMIT),
        name="assemble",
    )(at, own, other, fix)


def on_device(conv_input, grad_out, conv_w, conv_b, w_x, b_x, w_a, b_a, a_param):
    outer, inner = lax.axis_index("outer"), lax.axis_index("inner")
    core = inner % 2
    at = jnp.stack([core, outer, inner // 8, (inner // 2) % 4]).astype(jnp.int32)
    theirs = (1 - core) * HALF
    give = jnp.concatenate(
        [
            lax.dynamic_slice(conv_input, (0, theirs), (TOK, HALF)),
            lax.dynamic_slice(grad_out, (0, theirs), (TOK, HALF)),
        ],
        axis=0,
    )
    other_in = swap_cores(give)
    tails = [
        lax.ppermute(
            conv_input[TOK - MARGIN :, c * HALF : (c + 1) * HALF],
            AXES,
            [(2 * chip + 1, 2 * chip + 2 + c) for chip in range(63)],
        )
        for c in range(2)
    ]
    halo = jnp.where(core == 0, tails[0], tails[1])
    rate = jax.nn.softplus(a_param)
    par = jnp.concatenate([conv_w, jnp.stack([conv_b, b_x, b_a, rate])], axis=0)

    *saved, total = forward_pass(at, conv_input, grad_out, other_in, halo, par, w_x, w_a)
    carry = entering(at, total)
    operands = (conv_input, other_in, grad_out, halo, par, w_x, w_a, *saved, carry)
    blocks = None
    arrived = []
    for k in (1, 2, 3):
        piece, blocks = backward_chunk(k, at, operands, blocks)
        arrived.append(send_on(piece, 0, k))
    own, blocks = backward_chunk(0, at, operands, blocks)

    own_u, send_u, edge = blocks
    after = lax.ppermute(
        edge[MARGIN : 2 * MARGIN].astype(BF16), AXES, [(i, i - 2) for i in range(2, 128)]
    ).astype(F32)
    cols = lax.dynamic_slice(conv_w, (0, core * HALF), (4, HALF))
    fixed = []
    for m in range(MARGIN):
        line = edge[m]
        for k in range(MARGIN - m, MARGIN + 1):
            line = line + cols[k] * after[m + k - MARGIN]
        fixed.append(line)
    fix = jnp.stack(fixed)
    tail_rows = jnp.where(core == 0, fix.astype(BF16), send_u[TOK - MARGIN :])
    send_u = lax.dynamic_update_slice(send_u, tail_rows, (TOK - MARGIN, 0))
    grad_u = assemble(at, own_u, swap_cores(send_u), fix)

    rows = 512
    for axis, following in ((0, 1), (1, 2)):
        own, *pieces = add_stage(following, rows, at, own, arrived)
        arrived = [send_on(piece, following, k) for k, piece in zip((1, 2, 3), pieces)]
        rows //= 4
    (done,) = add_stage(None, rows, at, own, arrived)
    short = done[:rows]
    part = lay_out(2, rows, at, [done] + [send_on(short, 2, -k) for k in (1, 2, 3)])
    part = lay_out(1, 128, at, [part] + [send_on(part, 1, -k) for k in (1, 2, 3)], done)
    mine = [part] + [send_on(part, 0, -k) for k in (1, 2, 3)]
    theirs = [swap_cores(piece) for piece in mine]
    wx, wa, bx, ba, ap, taps, cb = write_out(at, a_param.reshape(1, WIDTH), mine + theirs)
    flat = lambda line: line.reshape(WIDTH)
    return grad_u, wx, wa, flat(bx), flat(ba), flat(ap), taps, flat(cb)


def solution(mesh):
    split = P(AXES, None)
    return jax.shard_map(
        on_device,
        mesh=mesh,
        in_specs=(split, split) + (P(),) * 7,
        out_specs=(split,) + (P(),) * 7,
        check_vma=False,
    )
```

```python
import functools

import jax
import jax.numpy as jnp
from jax import lax
from jax.experimental import pallas as pl
from jax.experimental.pallas import tpu as pltpu
from jax.sharding import PartitionSpec as P

AXES = ("outer", "inner")
F32, BF16 = jnp.float32, jnp.bfloat16
TOK = 128
CHIP_TOK = 256
GROUPS = CHIP_TOK // 8
WIDTH = 4096
HALF = 2048
HEAD_W = 256
HEADS = 8
CHIPS = 64
PIECE = 16
SPAN = 1152
SAME_CORE = [list(range(c, 128, 2)) for c in range(2)]
MARGIN = 3
EDGE = 8 * MARGIN
ROOT_FLOOR = 2.5e-07
VMEM_LIMIT = 48 * 1024 * 1024


def place(index):
    return [index // 32, (index // 8) % 4, (index // 2) % 4, index % 2]


def number(coords):
    return coords[0] * 32 + coords[1] * 8 + coords[2] * 2 + coords[3]


def turned(axis, steps):
    size = 2 if axis == 3 else 4
    pairs = []
    for source in range(128):
        coords = place(source)
        coords[axis] = (coords[axis] + steps) % size
        pairs.append((source, number(coords)))
    return pairs


def send_on(value, axis, steps):
    return lax.ppermute(value, AXES, turned(axis, steps))


def swap_cores(value):
    return send_on(value, 3, 1)


def trade(pieces):
    return lax.all_to_all(pieces, AXES, 0, 0, axis_index_groups=SAME_CORE)


def dot(a, b, dims):
    return lax.dot_general(a, b, (dims, ((), ())), preferred_element_type=F32)


def orders(core):
    row = lax.broadcasted_iota(jnp.int32, (CHIP_TOK, TOK), 0)
    col = lax.broadcasted_iota(jnp.int32, (CHIP_TOK, TOK), 1)
    token = (row % 8) * GROUPS + row // 8
    own = (token == col + core * TOK).astype(F32).astype(BF16)
    other = (token == col + (1 - core) * TOK).astype(F32).astype(BF16)
    return own, other


def wide(row, rows):
    return jnp.broadcast_to(row, (rows, row.shape[1]))


def load_conv_input(u_s, u, halo):
    sub = lax.broadcasted_iota(jnp.int32, (8, HEAD_W), 0)
    u_s[EDGE:, :] = u
    for k in range(1, MARGIN + 1):
        last = u_s[EDGE + CHIP_TOK - 8 * k : EDGE + CHIP_TOK - 8 * (k - 1), :]
        first = wide(halo[MARGIN - k : MARGIN - k + 1, :].astype(F32), 8)
        u_s[EDGE - 8 * k : EDGE - 8 * (k - 1), :] = jnp.where(
            sub == 0, first, pltpu.roll(last, 1, 0)
        )


def whole(count):
    return [pl.BlockSpec(memory_space=pltpu.VMEM)] * count


def on_core(body, shapes, *args, scratch=(), name):
    return pl.pallas_call(
        body,
        in_specs=[pl.BlockSpec(memory_space=pltpu.SMEM)] + whole(len(args) - 1),
        out_specs=whole(len(shapes)),
        out_shape=[jax.ShapeDtypeStruct(shape, dtype) for shape, dtype in shapes],
        scratch_shapes=[pltpu.VMEM(shape, dtype) for shape, dtype in scratch],
        compiler_params=pltpu.CompilerParams(vmem_limit_bytes=VMEM_LIMIT),
        name=name,
    )(*args)


def columns(first, count=HEAD_W):
    return pl.ds(pl.multiple_of(first, count), count)


def cut_kernel(at, conv_input, grad_out, give):
    theirs = columns((1 - at[0]) * HALF, HALF)
    give[:TOK, :] = conv_input[:, theirs]
    give[TOK:, :] = grad_out[:, theirs]


def forward_kernel(
    at, u_own, g_own, other_in, halo_in, par, w_x, w_a,
    decay_o, drive_o, quot_o, ga_o, gx_o, gk_o, mixed_o, lead_o, total_o,
    u_s, g_s, mix_s, zx_s, za_s,
):
    own, other = orders(at[0])
    step = 16

    def one_head(h, _):
        head = at[0] * HEADS + h
        local, outer = columns(h * HEAD_W), columns(head * HEAD_W)
        u = dot(own, u_own[:, outer], ((1,), (0,))) + dot(
            other, other_in[:TOK, local], ((1,), (0,))
        )
        g_s[...] = dot(own, g_own[:, outer], ((1,), (0,))) + dot(
            other, other_in[TOK:, local], ((1,), (0,))
        )
        load_conv_input(u_s, u, halo_in[:, local])
        row = lambda k, rows: wide(par[k : k + 1, outer], rows)
        taps = [row(k, step) for k in range(MARGIN + 1)]
        bias = row(4, step)
        for c in range(0, CHIP_TOK, step):
            mixed = bias
            for k in range(MARGIN + 1):
                mixed = mixed + taps[k] * u_s[EDGE - 8 * k + c : EDGE - 8 * k + c + step, :]
            mix_s[c : c + step, :] = mixed
            mixed_o[h, c : c + step, :] = mixed.astype(BF16)
        mixed_b = mixed_o[h]
        zx_s[...] = dot(mixed_b, w_x[head], ((1,), (0,)))
        za_s[...] = dot(mixed_b, w_a[head], ((1,), (0,)))
        b_x, b_a = row(5, step), row(6, step)
        slope = -8.0 * row(7, step)
        prod = jnp.ones((8, HEAD_W), F32)
        state = jnp.zeros((8, HEAD_W), F32)
        back = jnp.zeros((8, HEAD_W), F32)
        for c in range(0, CHIP_TOK, step):
            rows = slice(c, c + step)
            mixed = mix_s[rows, :]
            gate_x = jax.nn.sigmoid(zx_s[rows, :] + b_x)
            gate_a = jax.nn.sigmoid(za_s[rows, :] + b_a)
            x = slope * gate_a
            series = 1.0 / 120.0 + x * (1.0 / 720.0)
            for coef in (1.0 / 24.0, 1.0 / 6.0, 0.5, 1.0):
                series = coef + x * series
            less = x * series
            decay = 1.0 + less
            vari = -less * (2.0 + less)
            mult = jnp.sqrt(vari)
            gk = gate_x * mult
            drive = gk * mixed
            decay_o[h, rows, :] = decay
            drive_o[h, rows, :] = drive
            quot_o[h, rows, :] = (
                gate_x * mixed * (decay * decay) * lax.rsqrt(jnp.maximum(vari, ROOT_FLOOR))
            )
            ga_o[h, rows, :] = -8.0 * gate_a
            gx_o[h, rows, :] = gate_x
            gk_o[h, rows, :] = gk
            for q in (0, 8):
                part = decay[q : q + 8]
                prod = prod * part
                state = part * state + drive[q : q + 8]
                back = back + prod * g_s[c + q : c + q + 8, :]
        sub = lax.broadcasted_iota(jnp.int32, (8, HEAD_W), 0)
        fprod, fstate = prod, state
        bprod, bstate = prod, back
        for d in (1, 2, 4):
            up = sub >= d
            fstate = jnp.where(up, fprod * pltpu.roll(fstate, d, 0) + fstate, fstate)
            fprod = jnp.where(up, fprod * pltpu.roll(fprod, d, 0), fprod)
            down = sub < 8 - d
            bstate = jnp.where(down, bprod * pltpu.roll(bstate, 8 - d, 0) + bstate, bstate)
            bprod = jnp.where(down, bprod * pltpu.roll(bprod, 8 - d, 0), bprod)
        lead_o[h, 0:8, :] = jnp.where(sub == 0, 1.0, pltpu.roll(fprod, 1, 0))
        lead_o[h, 8:16, :] = jnp.where(sub == 0, 0.0, pltpu.roll(fstate, 1, 0))
        lead_o[h, 16:24, :] = jnp.where(sub == 7, 1.0, pltpu.roll(bprod, 7, 0))
        lead_o[h, 24:32, :] = jnp.where(sub == 7, 0.0, pltpu.roll(bstate, 7, 0))
        for i, line in enumerate((fprod[7:8], fstate[7:8], bstate[0:1])):
            for part in range(2):
                total_o[i, pl.ds(2 * h + part, 1), :] = line[:, 128 * part : 128 * part + 128]
        return 0

    lax.fori_loop(0, HEADS, one_head, 0)


def forward_pass(at, conv_input, grad_out, other_in, halo, par, w_x, w_a):
    big = (HEADS, CHIP_TOK, HEAD_W)
    return on_core(
        forward_kernel,
        [(big, F32)] * 6 + [(big, BF16), ((HEADS, 32, HEAD_W), F32), ((3, 16, 128), F32)],
        at, conv_input, grad_out, other_in, halo, par, w_x, w_a,
        scratch=[((EDGE + CHIP_TOK, HEAD_W), F32)] + [((CHIP_TOK, HEAD_W), F32)] * 4,
        name="gates",
    )


def join_kernel(axis, first, last, at, own, r1, r2, r3, *refs):
    before = None if first else refs[0]
    outs = refs if first else refs[1:]
    here = at[1 + axis]
    rows = lambda ref: [ref[i] for i in range(3)]
    t0, f0, b0 = rows(own)
    pieces = [rows(r) for r in (r1, r2, r3)]
    one, zero = jnp.ones_like(t0), jnp.zeros_like(t0)
    early = [jnp.full(t0.shape, here + k >= 4) for k in (1, 2, 3)]
    pt, pf = one, zero
    for k in range(3):
        t, f, _ = pieces[k]
        pf = jnp.where(early[k], t * pf + f, pf)
        pt = jnp.where(early[k], t * pt, pt)
    bt, bs = one, zero
    for k in (2, 1, 0):
        t, _, b = pieces[k]
        bs = jnp.where(early[k], bs, t * bs + b)
        bt = jnp.where(early[k], bt, t * bt)
    if first:
        acc = [pt, pf, bt, bs]
    else:
        ep, es, fp, fs = [before[i] for i in range(4)]
        acc = [ep * pt, ep * pf + es, fp * bt, fp * bs + fs]
    if last:
        outs[0][0] = acc[1]
        outs[0][1] = acc[3]
        return
    f = t0 * pf + f0
    for k in range(3):
        f = jnp.where(early[k], f, pieces[k][0] * f + pieces[k][1])
    b = t0 * bs + b0
    for k in (2, 1, 0):
        b = jnp.where(early[k], pieces[k][0] * b + pieces[k][2], b)
    outs[0][0] = pt * t0 * bt
    outs[0][1] = f
    outs[0][2] = b
    for i in range(4):
        outs[1][i] = acc[i]


def entering(at, total):
    acc = None
    value = total
    for axis in (2, 1, 0):
        first, last = axis == 2, axis == 0
        args = [value] + [send_on(value, axis, -k) for k in (1, 2, 3)]
        if not first:
            args.append(acc)
        shapes = [((2, 16, 128), F32)] if last else [((3, 16, 128), F32), ((4, 16, 128), F32)]
        out = on_core(
            functools.partial(join_kernel, axis, first, last), shapes, at, *args, name="join"
        )
        if last:
            return out[0]
        value, acc = out


def backward_kernel(
    at, u_own, g_own, other_in, halo_in, par, w_x, w_a,
    decay, drive, quot, ga, gx, gk, mixed_b, lead, carry,
    piece_o, own_o, send_o, edge_o,
    u_s, g_s, a_s, dx_s, da_s, gm_s,
):
    own, other = orders(at[0])

    def one_head(h, _):
        head = at[0] * HEADS + h
        local, outer = columns(h * HEAD_W), columns(head * HEAD_W)
        u = dot(own, u_own[:, outer], ((1,), (0,))) + dot(
            other, other_in[:TOK, local], ((1,), (0,))
        )
        g_s[...] = dot(own, g_own[:, outer], ((1,), (0,))) + dot(
            other, other_in[TOK:, local], ((1,), (0,))
        )
        load_conv_input(u_s, u, halo_in[:, local])
        row = lambda k: wide(par[k : k + 1, outer], 8)
        entry = [
            wide(
                jnp.concatenate([carry[i, pl.ds(2 * h + p, 1), :] for p in range(2)], axis=1), 8
            )
            for i in range(2)
        ]
        state = lead[h, 8:16, :] + lead[h, 0:8, :] * entry[0]
        back = lead[h, 24:32, :] + lead[h, 16:24, :] * entry[1]
        for r in range(GROUPS - 1, -1, -1):
            rows = slice(8 * r, 8 * r + 8)
            adjoint = g_s[rows, :] + back
            a_s[rows, :] = adjoint
            back = decay[h, rows, :] * adjoint
        rate = row(7)
        eighth = 0.125 * rate
        zero = jnp.zeros((8, HEAD_W), F32)
        sum_x, sum_a, sum_rate = zero, zero, zero
        for r in range(0, GROUPS, 2):
            pair_x, pair_a = [], []
            for q in (r, r + 1):
                rows = slice(8 * q, 8 * q + 8)
                adjoint = a_s[rows, :]
                passed = state * decay[h, rows, :]
                drv = drive[h, rows, :]
                grad_log = adjoint * (passed - quot[h, rows, :])
                state = passed + drv
                gate = ga[h, rows, :]
                term = gate * grad_log
                dz_a = term * (rate + eighth * gate)
                dz_x = adjoint * drv * (1.0 - gx[h, rows, :])
                sum_rate = sum_rate + term
                sum_a = sum_a + dz_a
                sum_x = sum_x + dz_x
                gm_s[rows, :] = adjoint * gk[h, rows, :]
                pair_x.append(dz_x)
                pair_a.append(dz_a)
            rows = slice(8 * r, 8 * r + 16)
            dx_s[rows, :] = jnp.concatenate(pair_x, 0).astype(BF16)
            da_s[rows, :] = jnp.concatenate(pair_a, 0).astype(BF16)
        dz_x, dz_a = dx_s[...], da_s[...]
        gm_s[:CHIP_TOK, :] += dot(dz_x, w_x[head], ((1,), (1,))) + dot(
            dz_a, w_a[head], ((1,), (1,))
        )
        mixed = mixed_b[h]
        for first, dz in ((0, dz_x), (HEAD_W, dz_a)):
            local_w = dot(mixed, dz, ((0,), (0,))).astype(BF16)
            for m in range(8):
                for part in range(2):
                    lo = 32 * m + PIECE * part
                    piece_o[8 * h + m, :, 512 * part + first : 512 * part + first + HEAD_W] = (
                        local_w[lo : lo + PIECE]
                    )
        sub = lax.broadcasted_iota(jnp.int32, (8, HEAD_W), 0)
        for j in range(MARGIN):
            first = gm_s[8 * j : 8 * j + 8, :]
            gm_s[CHIP_TOK + 8 * j : CHIP_TOK + 8 * j + 8, :] = jnp.where(
                sub == 7, 0.0, pltpu.roll(first, 7, 0)
            )
            edge_o[MARGIN + j : MARGIN + j + 1, local] = first[0:1]
        taps = [row(k) for k in range(MARGIN + 1)]
        sum_c, sum_k = zero, [zero] * (MARGIN + 1)
        for r in range(0, GROUPS, 2):
            pair = []
            for q in (r, r + 1):
                here = gm_s[8 * q : 8 * q + 8, :]
                sum_c = sum_c + here
                grad = taps[0] * here
                for k in range(1, MARGIN + 1):
                    grad = grad + taps[k] * gm_s[8 * (q + k) : 8 * (q + k) + 8, :]
                for k in range(MARGIN + 1):
                    lo = EDGE + 8 * (q - k)
                    sum_k[k] = sum_k[k] + here * u_s[lo : lo + 8, :]
                if q >= GROUPS - MARGIN:
                    at_edge = q - GROUPS + MARGIN
                    edge_o[at_edge : at_edge + 1, local] = grad[7:8]
                pair.append(grad)
            dx_s[8 * r : 8 * r + 16, :] = jnp.concatenate(pair, 0).astype(BF16)
        grad_b = dx_s[...]
        own_o[:, local] = dot(own, grad_b, ((0,), (0,))).astype(BF16)
        send_o[:, local] = dot(other, grad_b, ((0,), (0,))).astype(BF16)
        sums = [sum_x, sum_a, sum_rate] + sum_k + [sum_c]
        small = jnp.concatenate([jnp.sum(s, axis=0, keepdims=True) for s in sums], 0)
        parts = in_two(small)
        for m in range(8):
            turned_parts = parts if m == 0 else pltpu.roll(parts, HEAD_W - 32 * m, 1)
            piece_o[8 * h + m, :, 1024:SPAN] = turned_parts[:, :128].astype(BF16)
        return 0

    lax.fori_loop(0, HEADS, one_head, 0)


def in_two(small):
    high = small.astype(BF16).astype(F32)
    return jnp.concatenate([high, small - high], 0)


def backward_pass(at, *operands):
    return on_core(
        backward_kernel,
        [((CHIPS, PIECE, SPAN), BF16), ((TOK, HALF), BF16), ((TOK, HALF), BF16), ((8, HALF), F32)],
        at, *operands,
        scratch=[
            ((EDGE + CHIP_TOK, HEAD_W), F32),
            ((CHIP_TOK, HEAD_W), F32),
            ((CHIP_TOK, HEAD_W), F32),
            ((CHIP_TOK, HEAD_W), BF16),
            ((CHIP_TOK, HEAD_W), BF16),
            ((EDGE + CHIP_TOK, HEAD_W), F32),
        ],
        name="grads",
    )


def sum_kernel(at, pieces, out):
    def add(i, total):
        return total + pieces[i].astype(F32)

    total = lax.fori_loop(0, CHIPS, add, jnp.zeros((PIECE, SPAN), F32), unroll=8)
    small = total[0:8, 1024:] + total[8:16, 1024:]
    done = jnp.concatenate([total[:, :1024], in_two(small)], 1).astype(BF16)

    def lay(i, _):
        out[i] = done
        return 0

    lax.fori_loop(0, CHIPS, lay, 0, unroll=8)


def unpack_weights(owner, pieces, wx_o, wa_o, buf, sems):
    copies = []
    for j in range(HEADS):
        for m in range(8):
            for part in range(2):
                lo = 32 * m + PIECE * part
                for i in range(2):
                    first = 512 * part + HEAD_W * i
                    buf[j, i, lo : lo + PIECE, :] = pieces[
                        8 * j + m, :, first : first + HEAD_W
                    ].astype(F32)
        for i, out in enumerate((wx_o, wa_o)):
            copies.append(
                pltpu.make_async_copy(
                    buf.at[j, i], out.at[owner * HEADS + j], sems.at[2 * j + i]
                )
            )
            copies[-1].start()
    return copies


def unpack_own_kernel(at, pieces, wx_o, wa_o, buf, sems):
    for copy in unpack_weights(at[0], pieces, wx_o, wa_o, buf, sems):
        copy.wait()


def unpack_rest_kernel(
    at, mine, theirs, a_param, wx_in, wa_in,
    wx_o, wa_o, bx_o, ba_o, ap_o, taps_o, cb_o, buf, sems,
):
    copies = unpack_weights(1 - at[0], theirs, wx_o, wa_o, buf, sems)
    lane = lax.broadcasted_iota(jnp.int32, (8, HEAD_W), 1)
    for owner, pieces in ((at[0], mine), (1 - at[0], theirs)):
        for j in range(HEADS):
            small = jnp.zeros((8, HEAD_W), F32)
            for m in range(8):
                parts = pieces[8 * j + m, :, 1024:SPAN].astype(F32)
                both = parts[0:8] + parts[8:16]
                both = jnp.concatenate([both, both], 1)
                both = both if m == 0 else pltpu.roll(both, 32 * m, 1)
                small = jnp.where(lane // 32 == m, both, small)
            cols = columns(owner * HALF + j * HEAD_W)
            bx_o[:, cols] = small[0:1]
            ba_o[:, cols] = small[1:2]
            ap_o[:, cols] = small[2:3] * jax.nn.sigmoid(a_param[:, cols])
            taps_o[:, cols] = small[3:7]
            cb_o[:, cols] = small[7:8]
    for copy in copies:
        copy.wait()


def write_out(at, a_param, mine, theirs):
    away = pl.BlockSpec(memory_space=pl.ANY)
    smem = pl.BlockSpec(memory_space=pltpu.SMEM)
    big = jax.ShapeDtypeStruct((2 * HEADS, HEAD_W, HEAD_W), F32)
    line = jax.ShapeDtypeStruct((1, WIDTH), F32)
    scratch = [pltpu.VMEM((HEADS, 2, HEAD_W, HEAD_W), F32), pltpu.SemaphoreType.DMA((16,))]
    params = pltpu.CompilerParams(vmem_limit_bytes=VMEM_LIMIT)
    wx, wa = pl.pallas_call(
        unpack_own_kernel,
        in_specs=[smem] + whole(1),
        out_specs=[away] * 2,
        out_shape=[big, big],
        scratch_shapes=scratch,
        compiler_params=params,
        name="unpack_own",
    )(at, mine)
    return pl.pallas_call(
        unpack_rest_kernel,
        in_specs=[smem] + whole(3) + [away] * 2,
        out_specs=[away] * 2 + whole(5),
        out_shape=[big, big, line, line, line, jax.ShapeDtypeStruct((4, WIDTH), F32), line],
        input_output_aliases={4: 0, 5: 1},
        scratch_shapes=scratch,
        compiler_params=params,
        name="unpack_rest",
    )(at, mine, theirs, a_param, wx, wa)


def assemble_kernel(at, own, other, fix, out):
    mine, rest = columns(at[0] * HALF, HALF), columns((1 - at[0]) * HALF, HALF)
    out[:, mine] = own[...]
    out[:, rest] = other[...]

    @pl.when(at[0] == 1)
    def _():
        tail = own[TOK - 16 :, :].astype(F32)
        tail = jnp.concatenate([tail[: 16 - MARGIN], fix[0:MARGIN, :]], 0)
        out[TOK - 16 :, HALF:] = tail.astype(BF16)


def on_device(conv_input, grad_out, conv_w, conv_b, w_x, b_x, w_a, b_a, a_param):
    outer, inner = lax.axis_index("outer"), lax.axis_index("inner")
    core = inner % 2
    at = jnp.stack([core, outer, inner // 8, (inner // 2) % 4]).astype(jnp.int32)
    (give,) = on_core(
        cut_kernel, [((2 * TOK, HALF), BF16)], at, conv_input, grad_out, name="cut"
    )
    other_in = swap_cores(give)
    tails = [
        lax.ppermute(
            conv_input[TOK - MARGIN :, c * HALF : (c + 1) * HALF],
            AXES,
            [(2 * chip + 1, 2 * chip + 2 + c) for chip in range(63)],
        )
        for c in range(2)
    ]
    halo = jnp.where(core == 0, tails[0], tails[1])
    rate = jax.nn.softplus(a_param)
    par = jnp.concatenate([conv_w, jnp.stack([conv_b, b_x, b_a, rate])], axis=0)

    inputs = (conv_input, grad_out, other_in, halo, par, w_x, w_a)
    *saved, total = forward_pass(at, *inputs)
    carry = entering(at, total)
    pieces, own_u, send_u, edge = backward_pass(at, *inputs, *saved, carry)
    arrived = trade(pieces)

    after = lax.ppermute(
        edge[MARGIN : 2 * MARGIN].astype(BF16), AXES, [(i, i - 2) for i in range(2, 128)]
    ).astype(F32)
    cols = lax.dynamic_slice(conv_w, (0, core * HALF), (4, HALF))
    fixed = []
    for m in range(MARGIN):
        line = edge[m]
        for k in range(MARGIN - m, MARGIN + 1):
            line = line + cols[k] * after[m + k - MARGIN]
        fixed.append(line)
    fix = jnp.stack(fixed)
    tail_rows = jnp.where(core == 0, fix.astype(BF16), send_u[TOK - MARGIN :])
    send_u = lax.dynamic_update_slice(send_u, tail_rows, (TOK - MARGIN, 0))
    (grad_u,) = on_core(
        assemble_kernel,
        [((TOK, WIDTH), BF16)],
        at, own_u, swap_cores(send_u), fix,
        name="assemble",
    )

    (done,) = on_core(
        sum_kernel, [((CHIPS, PIECE, SPAN), BF16)], at, arrived, name="sum_chips"
    )
    mine = trade(done)
    theirs = swap_cores(mine)
    wx, wa, bx, ba, ap, taps, cb = write_out(at, a_param.reshape(1, WIDTH), mine, theirs)
    flat = lambda line: line.reshape(WIDTH)
    return grad_u, wx, wa, flat(bx), flat(ba), flat(ap), taps, flat(cb)


def solution(mesh):
    split = P(AXES, None)
    return jax.shard_map(
        on_device,
        mesh=mesh,
        in_specs=(split, split) + (P(),) * 7,
        out_specs=(split,) + (P(),) * 7,
        check_vma=False,
    )
```

```python
import functools

import jax
import jax.numpy as jnp
from jax import lax
from jax.experimental import pallas as pl
from jax.experimental.pallas import tpu as pltpu
from jax.sharding import PartitionSpec as P

AXES = ("outer", "inner")
F32, BF16 = jnp.float32, jnp.bfloat16
TOK = 128
CHIP_TOK = 256
GROUPS = CHIP_TOK // 8
WIDTH = 4096
HALF = 2048
HEAD_W = 256
HEADS = 8
PLANE = 16
SHARE = 32
BOTH = 2 * HEAD_W
MARGIN = 3
EDGE = 8 * MARGIN
ROOT_FLOOR = 2.5e-07
VMEM_LIMIT = 16 * 1024 * 1024
CHEAP = pl.CostEstimate(flops=1000, bytes_accessed=1000, transcendentals=0)


def place(index):
    return [index // 32, (index // 8) % 4, (index // 2) % 4, index % 2]


def number(coords):
    return coords[0] * 32 + coords[1] * 8 + coords[2] * 2 + coords[3]


def turned(axis, steps):
    size = 2 if axis == 3 else 4
    pairs = []
    for source in range(128):
        coords = place(source)
        coords[axis] = (coords[axis] + steps) % size
        pairs.append((source, number(coords)))
    return pairs


def send_on(value, axis, steps):
    return lax.ppermute(value, AXES, turned(axis, steps))


def swap_cores(value):
    return send_on(value, 3, 1)


def dot(a, b, dims):
    return lax.dot_general(a, b, (dims, ((), ())), preferred_element_type=F32)


def orders(core):
    row = lax.broadcasted_iota(jnp.int32, (CHIP_TOK, TOK), 0)
    col = lax.broadcasted_iota(jnp.int32, (CHIP_TOK, TOK), 1)
    token = (row % 8) * GROUPS + row // 8
    own = (token == col + core * TOK).astype(F32).astype(BF16)
    other = (token == col + (1 - core) * TOK).astype(F32).astype(BF16)
    return own, other


def wide(row, rows):
    return jnp.broadcast_to(row, (rows, row.shape[1]))


def load_conv_input(u_s, u, halo):
    sub = lax.broadcasted_iota(jnp.int32, (8, HEAD_W), 0)
    u_s[EDGE:, :] = u
    for k in range(1, MARGIN + 1):
        last = u_s[EDGE + CHIP_TOK - 8 * k : EDGE + CHIP_TOK - 8 * (k - 1), :]
        first = wide(halo[MARGIN - k : MARGIN - k + 1, :].astype(F32), 8)
        u_s[EDGE - 8 * k : EDGE - 8 * (k - 1), :] = jnp.where(
            sub == 0, first, pltpu.roll(last, 1, 0)
        )


def whole(count):
    return [pl.BlockSpec(memory_space=pltpu.VMEM)] * count


def on_core(body, shapes, *args, scratch=(), away=(), name):
    specs = [pl.BlockSpec(memory_space=pltpu.SMEM)] + whole(len(args) - 1)
    for i in away:
        specs[i] = pl.BlockSpec(memory_space=pl.ANY)
    return pl.pallas_call(
        body,
        in_specs=specs,
        out_specs=whole(len(shapes)),
        out_shape=[jax.ShapeDtypeStruct(shape, dtype) for shape, dtype in shapes],
        scratch_shapes=[
            s if not isinstance(s, tuple) else pltpu.VMEM(s[0], s[1]) for s in scratch
        ],
        compiler_params=pltpu.CompilerParams(vmem_limit_bytes=VMEM_LIMIT),
        cost_estimate=CHEAP,
        name=name,
    )(*args)


def columns(first, count=HEAD_W):
    return pl.ds(pl.multiple_of(first, count), count)


def early_kernel(at, conv_input, grad_out, w_x, w_a, out):
    for i in range(4):
        out[i] = at[i]


def early(at, *arrays):
    smem = pl.BlockSpec(memory_space=pltpu.SMEM)
    return pl.pallas_call(
        early_kernel,
        in_specs=[smem] + [pl.BlockSpec(memory_space=pl.ANY)] * len(arrays),
        out_specs=smem,
        out_shape=jax.ShapeDtypeStruct((4,), jnp.int32),
        compiler_params=pltpu.CompilerParams(vmem_limit_bytes=VMEM_LIMIT),
        name="early",
    )(at, *arrays)


def forward_kernel(
    at, u_other, g_other, halo_in, par, u_own, g_own, w_x, w_a,
    decay_o, drive_o, quot_o, ga_o, gx_o, gk_o, mixed_o, u_o, g_o, lead_o, total_o,
    u_s, g_s, mix_s, zx_s, za_s,
):
    own, other = orders(at[0])
    step = 16

    h = pl.program_id(0)

    u = dot(own, u_own[...], ((1,), (0,))) + dot(other, u_other[...], ((1,), (0,)))
    g = dot(own, g_own[...], ((1,), (0,))) + dot(other, g_other[...], ((1,), (0,)))
    u_o[0] = u.astype(BF16)
    g_o[0] = g.astype(BF16)
    g_s[...] = g
    load_conv_input(u_s, u, halo_in[...])
    row = lambda k, rows: wide(par[k : k + 1, :], rows)
    taps = [row(k, step) for k in range(MARGIN + 1)]
    bias = row(4, step)
    for c in range(0, CHIP_TOK, step):
        mixed = bias
        for k in range(MARGIN + 1):
            mixed = mixed + taps[k] * u_s[EDGE - 8 * k + c : EDGE - 8 * k + c + step, :]
        mix_s[c : c + step, :] = mixed
        mixed_o[0, c : c + step, :] = mixed.astype(BF16)
    mixed_b = mixed_o[0]
    zx_s[...] = dot(mixed_b, w_x[0], ((1,), (0,)))
    za_s[...] = dot(mixed_b, w_a[0], ((1,), (0,)))
    b_x, b_a = row(5, step), row(6, step)
    slope = -8.0 * row(7, step)
    prod = jnp.ones((8, HEAD_W), F32)
    state = jnp.zeros((8, HEAD_W), F32)
    back = jnp.zeros((8, HEAD_W), F32)
    for c in range(0, CHIP_TOK, step):
        rows = slice(c, c + step)
        mixed = mix_s[rows, :]
        gate_x = jax.nn.sigmoid(zx_s[rows, :] + b_x)
        gate_a = jax.nn.sigmoid(za_s[rows, :] + b_a)
        x = slope * gate_a
        series = 1.0 / 120.0 + x * (1.0 / 720.0)
        for coef in (1.0 / 24.0, 1.0 / 6.0, 0.5, 1.0):
            series = coef + x * series
        less = x * series
        decay = 1.0 + less
        vari = -less * (2.0 + less)
        mult = jnp.sqrt(vari)
        gk = gate_x * mult
        drive = gk * mixed
        decay_o[0, rows, :] = decay
        drive_o[0, rows, :] = drive
        quot_o[0, rows, :] = (
            gate_x * mixed * (decay * decay) * lax.rsqrt(jnp.maximum(vari, ROOT_FLOOR))
        )
        ga_o[0, rows, :] = -8.0 * gate_a
        gx_o[0, rows, :] = gate_x
        gk_o[0, rows, :] = gk
        for q in (0, 8):
            part = decay[q : q + 8]
            prod = prod * part
            state = part * state + drive[q : q + 8]
            back = back + prod * g_s[c + q : c + q + 8, :]
    sub = lax.broadcasted_iota(jnp.int32, (8, HEAD_W), 0)
    fprod, fstate = prod, state
    bprod, bstate = prod, back
    for d in (1, 2, 4):
        up = sub >= d
        fstate = jnp.where(up, fprod * pltpu.roll(fstate, d, 0) + fstate, fstate)
        fprod = jnp.where(up, fprod * pltpu.roll(fprod, d, 0), fprod)
        down = sub < 8 - d
        bstate = jnp.where(down, bprod * pltpu.roll(bstate, 8 - d, 0) + bstate, bstate)
        bprod = jnp.where(down, bprod * pltpu.roll(bprod, 8 - d, 0), bprod)
    lead_o[0, 0:8, :] = jnp.where(sub == 0, 1.0, pltpu.roll(fprod, 1, 0))
    lead_o[0, 8:16, :] = jnp.where(sub == 0, 0.0, pltpu.roll(fstate, 1, 0))
    lead_o[0, 16:24, :] = jnp.where(sub == 7, 1.0, pltpu.roll(bprod, 7, 0))
    lead_o[0, 24:32, :] = jnp.where(sub == 7, 0.0, pltpu.roll(bstate, 7, 0))
    for i, line in enumerate((fprod[7:8], fstate[7:8], bstate[0:1])):
        for part in range(2):
            total_o[i, pl.ds(2 * h + part, 1), :] = line[:, 128 * part : 128 * part + 128]


def forward_pass(at, *inputs):
    head = lambda h, at: (0, at[0] * HEADS + h)
    saved = pl.BlockSpec((1, CHIP_TOK, HEAD_W), lambda h, at: (h, 0, 0))
    big = (HEADS, CHIP_TOK, HEAD_W)
    return pl.pallas_call(
        forward_kernel,
        grid_spec=pltpu.PrefetchScalarGridSpec(
            num_scalar_prefetch=1,
            grid=(HEADS,),
            in_specs=[pl.BlockSpec((TOK, HEAD_W), head)] * 2
            + [pl.BlockSpec((MARGIN, HEAD_W), lambda h, at: (0, h)), pl.BlockSpec((8, HEAD_W), head)]
            + [pl.BlockSpec((TOK, HEAD_W), head)] * 2
            + [pl.BlockSpec((1, HEAD_W, HEAD_W), lambda h, at: (at[0] * HEADS + h, 0, 0))] * 2,
            out_specs=[saved] * 9
            + [
                pl.BlockSpec((1, 32, HEAD_W), lambda h, at: (h, 0, 0)),
                pl.BlockSpec((3, 16, 128), lambda h, at: (0, 0, 0)),
            ],
            scratch_shapes=[pltpu.VMEM((EDGE + CHIP_TOK, HEAD_W), F32)]
            + [pltpu.VMEM((CHIP_TOK, HEAD_W), F32)] * 4,
        ),
        out_shape=[jax.ShapeDtypeStruct(big, F32)] * 6
        + [jax.ShapeDtypeStruct(big, BF16)] * 3
        + [
            jax.ShapeDtypeStruct((HEADS, 32, HEAD_W), F32),
            jax.ShapeDtypeStruct((3, 16, 128), F32),
        ],
        compiler_params=pltpu.CompilerParams(vmem_limit_bytes=VMEM_LIMIT),
        cost_estimate=CHEAP,
        name="gates",
    )(at, *inputs)


def join_kernel(axis, first, last, at, own, r1, r2, r3, *refs):
    before = None if first else refs[0]
    outs = refs if first else refs[1:]
    here = at[1 + axis]
    rows = lambda ref: [ref[i] for i in range(3)]
    t0, f0, b0 = rows(own)
    pieces = [rows(r) for r in (r1, r2, r3)]
    one, zero = jnp.ones_like(t0), jnp.zeros_like(t0)
    early = [jnp.full(t0.shape, here + k >= 4) for k in (1, 2, 3)]
    pt, pf = one, zero
    for k in range(3):
        t, f, _ = pieces[k]
        pf = jnp.where(early[k], t * pf + f, pf)
        pt = jnp.where(early[k], t * pt, pt)
    bt, bs = one, zero
    for k in (2, 1, 0):
        t, _, b = pieces[k]
        bs = jnp.where(early[k], bs, t * bs + b)
        bt = jnp.where(early[k], bt, t * bt)
    if first:
        acc = [pt, pf, bt, bs]
    else:
        ep, es, fp, fs = [before[i] for i in range(4)]
        acc = [ep * pt, ep * pf + es, fp * bt, fp * bs + fs]
    if last:
        outs[0][0] = acc[1]
        outs[0][1] = acc[3]
        return
    f = t0 * pf + f0
    for k in range(3):
        f = jnp.where(early[k], f, pieces[k][0] * f + pieces[k][1])
    b = t0 * bs + b0
    for k in (2, 1, 0):
        b = jnp.where(early[k], pieces[k][0] * b + pieces[k][2], b)
    outs[0][0] = pt * t0 * bt
    outs[0][1] = f
    outs[0][2] = b
    for i in range(4):
        outs[1][i] = acc[i]


def entering(at, total):
    acc = None
    value = total
    for axis in (2, 1, 0):
        first, last = axis == 2, axis == 0
        args = [value] + [send_on(value, axis, -k) for k in (1, 2, 3)]
        if not first:
            args.append(acc)
        shapes = [((2, 16, 128), F32)] if last else [((3, 16, 128), F32), ((4, 16, 128), F32)]
        out = on_core(
            functools.partial(join_kernel, axis, first, last), shapes, at, *args, name="join"
        )
        if last:
            return out[0]
        value, acc = out


def backward_kernel(
    k, at, halo_in, par, w_x, w_a,
    decay, drive, quot, ga, gx, gk, mixed_b, u_b, g_b, lead, carry,
    *refs,
):
    pieces, (gm_o, u_s, a_s, dx_s, da_s) = refs[:-5], refs[-5:]
    j = pl.program_id(0)
    h = 2 * lax.rem(at[1] + k, 4) + j
    load_conv_input(u_s, u_b[0].astype(F32), halo_in[...])
    row = lambda k: wide(par[k : k + 1, :], 8)
    entry = [
        wide(
            jnp.concatenate([carry[i, pl.ds(2 * h + p, 1), :] for p in range(2)], axis=1), 8
        )
        for i in range(2)
    ]
    state = lead[0, 8:16, :] + lead[0, 0:8, :] * entry[0]
    back = lead[0, 24:32, :] + lead[0, 16:24, :] * entry[1]
    for r in range(GROUPS - 2, -1, -2):
        grads = g_b[0, 8 * r : 8 * r + 16, :].astype(F32)
        for q in (1, 0):
            rows = slice(8 * (r + q), 8 * (r + q) + 8)
            adjoint = grads[8 * q : 8 * q + 8] + back
            a_s[rows, :] = adjoint
            back = decay[0, rows, :] * adjoint
    rate = row(7)
    eighth = 0.125 * rate
    zero = jnp.zeros((8, HEAD_W), F32)
    sum_x, sum_a, sum_rate = zero, zero, zero
    for r in range(0, GROUPS, 2):
        pair_x, pair_a = [], []
        for q in (r, r + 1):
            rows = slice(8 * q, 8 * q + 8)
            adjoint = a_s[rows, :]
            passed = state * decay[0, rows, :]
            drv = drive[0, rows, :]
            grad_log = adjoint * (passed - quot[0, rows, :])
            state = passed + drv
            gate = ga[0, rows, :]
            term = gate * grad_log
            dz_a = term * (rate + eighth * gate)
            dz_x = adjoint * drv * (1.0 - gx[0, rows, :])
            sum_rate = sum_rate + term
            sum_a = sum_a + dz_a
            sum_x = sum_x + dz_x
            gm_o[0, rows, :] = adjoint * gk[0, rows, :]
            pair_x.append(dz_x)
            pair_a.append(dz_a)
        rows = slice(8 * r, 8 * r + 16)
        dx_s[rows, :] = jnp.concatenate(pair_x, 0).astype(BF16)
        da_s[rows, :] = jnp.concatenate(pair_a, 0).astype(BF16)
    dz_x, dz_a = dx_s[...], da_s[...]
    gm_o[0] += dot(dz_x, w_x[0], ((1,), (1,))) + dot(dz_a, w_a[0], ((1,), (1,)))
    mixed = mixed_b[0]
    grad_w = [dot(mixed, dz, ((0,), (0,))) for dz in (dz_x, dz_a)]
    if len(pieces) == 2:
        for n in range(2):

            @pl.when(j == n)
            def _(half=pieces[n]):
                half[:HEAD_W, :HEAD_W] = grad_w[0].astype(BF16)
                half[:HEAD_W, HEAD_W:] = grad_w[1].astype(BF16)
    else:
        at_row = pl.ds(pl.multiple_of(j * HEAD_W, HEAD_W), HEAD_W)
        pieces[0][at_row, :HEAD_W] = grad_w[0]
        pieces[0][at_row, HEAD_W:] = grad_w[1]
    sum_c, sum_k = zero, [zero] * (MARGIN + 1)
    for q in range(GROUPS):
        here = gm_o[0, 8 * q : 8 * q + 8, :]
        sum_c = sum_c + here
        for t in range(MARGIN + 1):
            lo = EDGE + 8 * (q - t)
            sum_k[t] = sum_k[t] + here * u_s[lo : lo + 8, :]
    sums = [sum_x, sum_a, sum_rate] + sum_k + [sum_c]
    small = jnp.concatenate([jnp.sum(s, axis=0, keepdims=True) for s in sums], 0)
    if len(pieces) == 2:
        pieces[1][HEAD_W:, columns(j * HEAD_W)] = in_two(small)
    else:
        pieces[0][BOTH:, columns(j * HEAD_W)] = small


def in_two(small):
    high = small.astype(BF16).astype(F32)
    return jnp.concatenate([high, small - high], 0).astype(BF16)


def backward_chunk(k, at, *operands):
    local = lambda j, at: 2 * lax.rem(at[1] + k, 4) + j
    outer = lambda j, at: at[0] * HEADS + local(j, at)
    saved = pl.BlockSpec((1, CHIP_TOK, HEAD_W), lambda j, at: (local(j, at), 0, 0))
    matrix = pl.BlockSpec((1, HEAD_W, HEAD_W), lambda j, at: (outer(j, at), 0, 0))
    pieces = [((BOTH + 8, BOTH), F32)]
    if k == 2:
        pieces = [((HEAD_W, BOTH), BF16), ((HEAD_W + 16, BOTH), BF16)]
    return pl.pallas_call(
        functools.partial(backward_kernel, k),
        grid_spec=pltpu.PrefetchScalarGridSpec(
            num_scalar_prefetch=1,
            grid=(2,),
            in_specs=[
                pl.BlockSpec((MARGIN, HEAD_W), lambda j, at: (0, local(j, at))),
                pl.BlockSpec((8, HEAD_W), lambda j, at: (0, outer(j, at))),
                matrix,
                matrix,
            ]
            + [saved] * 9
            + [
                pl.BlockSpec((1, 32, HEAD_W), lambda j, at: (local(j, at), 0, 0)),
                pl.BlockSpec((2, 16, 128), lambda j, at: (0, 0, 0)),
            ],
            out_specs=[pl.BlockSpec(shape, lambda j, at: (0, 0)) for shape, _ in pieces]
            + [pl.BlockSpec((1, CHIP_TOK, HEAD_W), lambda j, at: (j, 0, 0))],
            scratch_shapes=[
                pltpu.VMEM((EDGE + CHIP_TOK, HEAD_W), F32),
                pltpu.VMEM((CHIP_TOK, HEAD_W), F32),
                pltpu.VMEM((CHIP_TOK, HEAD_W), BF16),
                pltpu.VMEM((CHIP_TOK, HEAD_W), BF16),
            ],
        ),
        out_shape=[jax.ShapeDtypeStruct(*piece) for piece in pieces]
        + [jax.ShapeDtypeStruct((2, CHIP_TOK, HEAD_W), F32)],
        compiler_params=pltpu.CompilerParams(vmem_limit_bytes=VMEM_LIMIT),
        cost_estimate=CHEAP,
        name="grads",
    )(at, *operands)


def input_kernel(at, gm0, gm1, gm2, gm3, par, own_o, send_o, edge_o, gm_s, dx_s):
    own, other = orders(at[0])
    sub = lax.broadcasted_iota(jnp.int32, (8, HEAD_W), 0)
    for k, gm in enumerate((gm0, gm1, gm2, gm3)):

        def one_head(j, _):
            h = 2 * lax.rem(at[1] + k, 4) + j
            head = at[0] * HEADS + h
            local, outer = columns(h * HEAD_W), columns(head * HEAD_W)
            for i in range(MARGIN):
                first = gm[j, 8 * i : 8 * i + 8, :]
                edge_o[MARGIN + i : MARGIN + i + 1, local] = first[0:1]
                gm_s[8 * i : 8 * i + 8, :] = jnp.where(sub == 7, 0.0, pltpu.roll(first, 7, 0))
            taps = [wide(par[t : t + 1, outer], 8) for t in range(MARGIN + 1)]
            for r in range(0, GROUPS, 2):
                pair = []
                for q in (r, r + 1):
                    grad = taps[0] * gm[j, 8 * q : 8 * q + 8, :]
                    for t in range(1, MARGIN + 1):
                        lo = 8 * (q + t)
                        if q + t < GROUPS:
                            grad = grad + taps[t] * gm[j, lo : lo + 8, :]
                        else:
                            lo -= CHIP_TOK
                            grad = grad + taps[t] * gm_s[lo : lo + 8, :]
                    if q >= GROUPS - MARGIN:
                        at_edge = q - GROUPS + MARGIN
                        edge_o[at_edge : at_edge + 1, local] = grad[7:8]
                    pair.append(grad)
                dx_s[8 * r : 8 * r + 16, :] = jnp.concatenate(pair, 0).astype(BF16)
            grad_b = dx_s[...]
            own_o[:, local] = dot(own, grad_b, ((0,), (0,))).astype(BF16)
            send_o[:, local] = dot(other, grad_b, ((0,), (0,))).astype(BF16)
            return 0

        lax.fori_loop(0, 2, one_head, 0)


def input_pass(at, par, gms):
    return on_core(
        input_kernel,
        [((TOK, HALF), BF16), ((TOK, HALF), BF16), ((8, HALF), F32)],
        at, *gms, par,
        scratch=[((EDGE, HEAD_W), F32), ((CHIP_TOK, HEAD_W), BF16)],
        name="grad_input",
    )


def merge_kernel(low, at, own, half, out):
    first = 0 if low else HEAD_W
    rest = slice(HEAD_W, BOTH) if low else slice(0, HEAD_W)
    out[rest, :] = own[rest, :].astype(BF16)
    total = own[first : first + HEAD_W, :] + half[:HEAD_W, :].astype(F32)
    out[first : first + HEAD_W, :] = total.astype(BF16)
    small = own[BOTH:, :]
    if not low:
        parts = half[HEAD_W:, :].astype(F32)
        small = small + (parts[0:8] + parts[8:16])
    out[BOTH:, :] = in_two(small)


def merge(low, at, own, half):
    (out,) = on_core(
        functools.partial(merge_kernel, low),
        [((BOTH + 16, BOTH), BF16)],
        at, own, half,
        name="merge",
    )
    return out


def spread_kernel(at, own, r1, r2, out):
    total = own[0:BOTH, :] + r1[0:BOTH, :].astype(F32) + r2[0:BOTH, :].astype(F32)
    small = own[BOTH:, :]
    for r in (r1, r2):
        parts = r[BOTH:, :].astype(F32)
        small = small + (parts[0:8] + parts[8:16])
    tail = in_two(small)
    for p in range(PLANE):
        out[p, :SHARE, :] = total[SHARE * p : SHARE * (p + 1)].astype(BF16)
        out[p, SHARE:, :] = tail


def plane_kernel(at, pieces, out, tail):
    total = pieces[0].astype(F32)
    for p in range(1, PLANE):
        total = total + pieces[p].astype(F32)
    done = total[:SHARE].astype(BF16)
    for p in range(PLANE):
        out[p] = done
    tail[...] = in_two(total[SHARE : SHARE + 8] + total[SHARE + 8 :])


def trade(pieces):
    groups = [list(range(c, 32, 2)) for c in range(2)]
    return lax.all_to_all(pieces, "inner", 0, 0, axis_index_groups=groups)


def lay_kernel(at, body, tail, out):
    for p in range(PLANE):
        out[SHARE * p : SHARE * (p + 1), :] = body[p]
    out[BOTH:, :] = tail[...]


def unpack_kernel(items, count, lines, at, *refs):
    pieces, refs = refs[:count], refs[count:]
    buf, sems = refs[-2:]
    if lines:
        a_param, tails, refs = refs[0], refs[1:9], refs[9:]
        lines_o, refs = refs[-7:-2], refs[:-7] + refs[-2:]
    wx_o, wa_o = refs[-4:-2]
    copies = []
    for operand, row, k, j, mine in items:
        owner = at[0] if mine else 1 - at[0]
        head = owner * HEADS + 2 * lax.rem(at[1] + k, 4) + j
        for i, out in enumerate((wx_o, wa_o)):
            n = len(copies)
            buf[n] = pieces[operand][row : row + HEAD_W, HEAD_W * i : HEAD_W * (i + 1)].astype(F32)
            copies.append(pltpu.make_async_copy(buf.at[n], out.at[head], sems.at[n]))
            copies[n].start()
    if lines:
        bx_o, ba_o, ap_o, taps_o, cb_o = lines_o
        for n, piece in enumerate(tails):
            owner = at[0] if n < 4 else 1 - at[0]
            parts = piece[piece.shape[0] - 16 :, :].astype(F32)
            small = parts[0:8] + parts[8:16]
            cols = columns(owner * HALF + lax.rem(at[1] + n % 4, 4) * BOTH, BOTH)
            bx_o[:, cols] = small[0:1]
            ba_o[:, cols] = small[1:2]
            ap_o[:, cols] = small[2:3] * jax.nn.sigmoid(a_param[:, cols])
            taps_o[:, cols] = small[3:7]
            cb_o[:, cols] = small[7:8]
    for copy in copies:
        copy.wait()


def unpack(at, pieces, items, done, lines=()):
    away = pl.BlockSpec(memory_space=pl.ANY)
    big = jax.ShapeDtypeStruct((2 * HEADS, HEAD_W, HEAD_W), F32)
    line = jax.ShapeDtypeStruct((1, WIDTH), F32)
    taps = jax.ShapeDtypeStruct((MARGIN + 1, WIDTH), F32)
    count, before = len(pieces), 1 + len(pieces) + len(lines)
    return pl.pallas_call(
        functools.partial(unpack_kernel, items, count, bool(lines)),
        in_specs=[pl.BlockSpec(memory_space=pltpu.SMEM)]
        + whole(before - 1)
        + [away] * len(done),
        out_specs=[away] * 2 + whole(5 if lines else 0),
        out_shape=[big, big] + ([line, line, line, taps, line] if lines else []),
        input_output_aliases={before + i: i for i in range(len(done))},
        scratch_shapes=[
            pltpu.VMEM((2 * len(items), HEAD_W, HEAD_W), F32),
            pltpu.SemaphoreType.DMA((2 * len(items),)),
        ],
        compiler_params=pltpu.CompilerParams(vmem_limit_bytes=VMEM_LIMIT),
        cost_estimate=CHEAP,
        name="unpack",
    )(at, *pieces, *lines, *done)


def assemble_kernel(at, own, other, fix, out):
    mine, rest = columns(at[0] * HALF, HALF), columns((1 - at[0]) * HALF, HALF)
    out[:, mine] = own[...]
    out[:, rest] = other[...]

    @pl.when(at[0] == 1)
    def _():
        tail = own[TOK - 16 :, :].astype(F32)
        tail = jnp.concatenate([tail[: 16 - MARGIN], fix[0:MARGIN, :]], 0)
        out[TOK - 16 :, HALF:] = tail.astype(BF16)


def on_device(conv_input, grad_out, conv_w, conv_b, w_x, b_x, w_a, b_a, a_param):
    outer, inner = lax.axis_index("outer"), lax.axis_index("inner")
    core = inner % 2
    at = jnp.stack([core, outer, inner // 8, (inner // 2) % 4]).astype(jnp.int32)
    tails = [
        lax.ppermute(
            conv_input[TOK - MARGIN :, c * HALF : (c + 1) * HALF],
            AXES,
            [(2 * chip + 1, 2 * chip + 2 + c) for chip in range(63)],
        )
        for c in range(2)
    ]
    halo = jnp.where(core == 0, tails[0], tails[1])
    rate = jax.nn.softplus(a_param)
    par = jnp.concatenate([conv_w, jnp.stack([conv_b, b_x, b_a, rate])], axis=0)

    inputs = (swap_cores(conv_input), swap_cores(grad_out), halo, par)
    at_gates = early(at, conv_input, grad_out, w_x, w_a)
    *saved, total = forward_pass(at_gates, *inputs, conv_input, grad_out, w_x, w_a)
    carry = entering(at, total)
    operands = (halo, par, w_x, w_a, *saved, carry)
    gms = [None] * 4
    low, high, gms[2] = backward_chunk(2, at, *operands)
    low, high = send_on(low, 0, 1), send_on(high, 0, -1)
    right, gms[1] = backward_chunk(1, at, *operands)
    left, gms[3] = backward_chunk(3, at, *operands)
    own, gms[0] = backward_chunk(0, at, *operands)
    arrived = [
        send_on(merge(True, at, right, low), 0, 1),
        send_on(merge(False, at, left, high), 0, -1),
    ]

    own_u, send_u, edge = input_pass(at, par, gms)
    own, own_u, send_u, edge = lax.optimization_barrier((own, own_u, send_u, edge))

    (pieces,) = on_core(
        spread_kernel, [((PLANE, SHARE + 16, BOTH), BF16)], at, own, *arrived, name="spread"
    )
    pieces, edge = lax.optimization_barrier((pieces, edge))
    traded = trade(pieces)
    after = lax.ppermute(
        edge[MARGIN : 2 * MARGIN].astype(BF16), AXES, [(i, i - 2) for i in range(2, 128)]
    ).astype(F32)
    cols = lax.dynamic_slice(conv_w, (0, core * HALF), (4, HALF))
    fixed = []
    for m in range(MARGIN):
        line = edge[m]
        for k in range(MARGIN - m, MARGIN + 1):
            line = line + cols[k] * after[m + k - MARGIN]
        fixed.append(line)
    fix = jnp.stack(fixed)
    tail_rows = jnp.where(core == 0, fix.astype(BF16), send_u[TOK - MARGIN :])
    send_u = lax.dynamic_update_slice(send_u, tail_rows, (TOK - MARGIN, 0))
    traded, send_u, fix = lax.optimization_barrier((traded, send_u, fix))
    shared, tail = on_core(
        plane_kernel,
        [((PLANE, SHARE, BOTH), BF16), ((16, BOTH), BF16)],
        at, traded,
        name="plane",
    )
    traded = trade(shared)
    (grad_u,) = on_core(
        assemble_kernel,
        [((TOK, WIDTH), BF16)],
        at, own_u, swap_cores(send_u), fix,
        name="assemble",
    )
    traded, grad_u = lax.optimization_barrier((traded, grad_u))
    (part,) = on_core(lay_kernel, [((BOTH + 16, BOTH), BF16)], at, traded, tail, name="lay")

    from_left, from_right = send_on(part, 0, 1), send_on(part, 0, -1)
    part_other = swap_cores(part)
    items = [(n, HEAD_W * j, 0, j, n == 0) for n in range(2) for j in range(2)]
    weights = unpack(at, (part, part_other), items, ())
    from_left, from_right, weights = lax.optimization_barrier((from_left, from_right, weights))
    far_low = send_on(from_left[:HEAD_W], 0, 1)
    far_high = send_on(from_right[HEAD_W:], 0, -1)
    near = [from_right, from_left]
    near_other = [swap_cores(piece) for piece in near]
    items = [(n, HEAD_W * j, (1, 3)[n % 2], j, n < 2) for n in range(4) for j in range(2)]
    weights = unpack(at, near + near_other, items, weights)
    far_low, far_high, weights = lax.optimization_barrier((far_low, far_high, weights))
    far = [far_low, far_high]
    far_other = [swap_cores(piece) for piece in far]
    items = [(2 * c + j, 0, 2, j, c == 0) for c in range(2) for j in range(2)]
    mine = [part, from_right, far_high, from_left]
    theirs = [part_other, near_other[0], far_other[1], near_other[1]]
    lines = (a_param.reshape(1, WIDTH), *mine, *theirs)
    *weights, bx, ba, ap, taps, cb = unpack(at, far + far_other, items, weights, lines)
    flat = lambda line: line.reshape(WIDTH)
    return (grad_u, *weights, flat(bx), flat(ba), flat(ap), taps, flat(cb))


def solution(mesh):
    split = P(AXES, None)
    return jax.shard_map(
        on_device,
        mesh=mesh,
        in_specs=(split, split) + (P(),) * 7,
        out_specs=(split,) + (P(),) * 7,
        check_vma=False,
    )
```

```python
import functools

import jax
import jax.numpy as jnp
from jax import lax
from jax.experimental import pallas as pl
from jax.experimental.pallas import tpu as pltpu
from jax.sharding import PartitionSpec as P

AXES = ("outer", "inner")
F32, BF16 = jnp.float32, jnp.bfloat16
TOK = 128
CHIP_TOK = 256
GROUPS = CHIP_TOK // 8
WIDTH = 4096
HALF = 2048
HEAD_W = 256
HEADS = 8
PLANE = 16
SHARE = 32
BOTH = 2 * HEAD_W
MARGIN = 3
EDGE = 8 * MARGIN
ROOT_FLOOR = 2.5e-07
VMEM_LIMIT = 16 * 1024 * 1024
CHEAP = pl.CostEstimate(flops=1000, bytes_accessed=1000, transcendentals=0)


def place(index):
    return [index // 32, (index // 8) % 4, (index // 2) % 4, index % 2]


def number(coords):
    return coords[0] * 32 + coords[1] * 8 + coords[2] * 2 + coords[3]


def turned(axis, steps):
    size = 2 if axis == 3 else 4
    pairs = []
    for source in range(128):
        coords = place(source)
        coords[axis] = (coords[axis] + steps) % size
        pairs.append((source, number(coords)))
    return pairs


def send_on(value, axis, steps):
    return lax.ppermute(value, AXES, turned(axis, steps))


def swap_cores(value):
    return send_on(value, 3, 1)


def dot(a, b, dims):
    return lax.dot_general(a, b, (dims, ((), ())), preferred_element_type=F32)


def orders(core):
    row = lax.broadcasted_iota(jnp.int32, (CHIP_TOK, TOK), 0)
    col = lax.broadcasted_iota(jnp.int32, (CHIP_TOK, TOK), 1)
    token = (row % 8) * GROUPS + row // 8
    own = (token == col + core * TOK).astype(F32).astype(BF16)
    other = (token == col + (1 - core) * TOK).astype(F32).astype(BF16)
    return own, other


def wide(row, rows):
    return jnp.broadcast_to(row, (rows, row.shape[1]))


def load_conv_input(u_s, u, halo):
    sub = lax.broadcasted_iota(jnp.int32, (8, HEAD_W), 0)
    u_s[EDGE:, :] = u
    for k in range(1, MARGIN + 1):
        last = u_s[EDGE + CHIP_TOK - 8 * k : EDGE + CHIP_TOK - 8 * (k - 1), :]
        first = wide(halo[MARGIN - k : MARGIN - k + 1, :].astype(F32), 8)
        u_s[EDGE - 8 * k : EDGE - 8 * (k - 1), :] = jnp.where(
            sub == 0, first, pltpu.roll(last, 1, 0)
        )


def whole(count):
    return [pl.BlockSpec(memory_space=pltpu.VMEM)] * count


def on_core(body, shapes, *args, scratch=(), away=(), name):
    specs = [pl.BlockSpec(memory_space=pltpu.SMEM)] + whole(len(args) - 1)
    for i in away:
        specs[i] = pl.BlockSpec(memory_space=pl.ANY)
    return pl.pallas_call(
        body,
        in_specs=specs,
        out_specs=whole(len(shapes)),
        out_shape=[jax.ShapeDtypeStruct(shape, dtype) for shape, dtype in shapes],
        scratch_shapes=[
            s if not isinstance(s, tuple) else pltpu.VMEM(s[0], s[1]) for s in scratch
        ],
        compiler_params=pltpu.CompilerParams(vmem_limit_bytes=VMEM_LIMIT),
        cost_estimate=CHEAP,
        name=name,
    )(*args)


def columns(first, count=HEAD_W):
    return pl.ds(pl.multiple_of(first, count), count)


def forward_kernel(
    at, u_other, g_other, u_own, g_own, halo_in, par, w_x, w_a,
    decay_o, drive_o, quot_o, ga_o, gx_o, gk_o, mixed_o, u_o, g_o, lead_o, total_o,
    u_s, g_s, mix_s, zx_s, za_s,
):
    own, other = orders(at[0])
    step = 16

    h = pl.program_id(0)


    u = dot(own, u_own[...], ((1,), (0,))) + dot(other, u_other[...], ((1,), (0,)))
    g = dot(own, g_own[...], ((1,), (0,))) + dot(other, g_other[...], ((1,), (0,)))
    u_o[0] = u.astype(BF16)
    g_o[0] = g.astype(BF16)
    g_s[...] = g
    load_conv_input(u_s, u, halo_in[...])
    row = lambda k, rows: wide(par[k : k + 1, :], rows)
    taps = [row(k, step) for k in range(MARGIN + 1)]
    bias = row(4, step)
    for c in range(0, CHIP_TOK, step):
        mixed = bias
        for k in range(MARGIN + 1):
            mixed = mixed + taps[k] * u_s[EDGE - 8 * k + c : EDGE - 8 * k + c + step, :]
        mix_s[c : c + step, :] = mixed
        mixed_o[0, c : c + step, :] = mixed.astype(BF16)
    mixed_b = mixed_o[0]
    zx_s[...] = dot(mixed_b, w_x[0], ((1,), (0,)))
    za_s[...] = dot(mixed_b, w_a[0], ((1,), (0,)))
    b_x, b_a = row(5, step), row(6, step)
    slope = -8.0 * row(7, step)
    prod = jnp.ones((8, HEAD_W), F32)
    state = jnp.zeros((8, HEAD_W), F32)
    back = jnp.zeros((8, HEAD_W), F32)
    for c in range(0, CHIP_TOK, step):
        rows = slice(c, c + step)
        mixed = mix_s[rows, :]
        gate_x = jax.nn.sigmoid(zx_s[rows, :] + b_x)
        gate_a = jax.nn.sigmoid(za_s[rows, :] + b_a)
        x = slope * gate_a
        series = 1.0 / 120.0 + x * (1.0 / 720.0)
        for coef in (1.0 / 24.0, 1.0 / 6.0, 0.5, 1.0):
            series = coef + x * series
        less = x * series
        decay = 1.0 + less
        vari = -less * (2.0 + less)
        mult = jnp.sqrt(vari)
        gk = gate_x * mult
        drive = gk * mixed
        decay_o[0, rows, :] = decay
        drive_o[0, rows, :] = drive
        quot_o[0, rows, :] = (
            gate_x * mixed * (decay * decay) * lax.rsqrt(jnp.maximum(vari, ROOT_FLOOR))
        )
        ga_o[0, rows, :] = -8.0 * gate_a
        gx_o[0, rows, :] = gate_x
        gk_o[0, rows, :] = gk
        for q in (0, 8):
            part = decay[q : q + 8]
            prod = prod * part
            state = part * state + drive[q : q + 8]
            back = back + prod * g_s[c + q : c + q + 8, :]
    sub = lax.broadcasted_iota(jnp.int32, (8, HEAD_W), 0)
    fprod, fstate = prod, state
    bprod, bstate = prod, back
    for d in (1, 2, 4):
        up = sub >= d
        fstate = jnp.where(up, fprod * pltpu.roll(fstate, d, 0) + fstate, fstate)
        fprod = jnp.where(up, fprod * pltpu.roll(fprod, d, 0), fprod)
        down = sub < 8 - d
        bstate = jnp.where(down, bprod * pltpu.roll(bstate, 8 - d, 0) + bstate, bstate)
        bprod = jnp.where(down, bprod * pltpu.roll(bprod, 8 - d, 0), bprod)
    lead_o[0, 0:8, :] = jnp.where(sub == 0, 1.0, pltpu.roll(fprod, 1, 0))
    lead_o[0, 8:16, :] = jnp.where(sub == 0, 0.0, pltpu.roll(fstate, 1, 0))
    lead_o[0, 16:24, :] = jnp.where(sub == 7, 1.0, pltpu.roll(bprod, 7, 0))
    lead_o[0, 24:32, :] = jnp.where(sub == 7, 0.0, pltpu.roll(bstate, 7, 0))
    for i, line in enumerate((fprod[7:8], fstate[7:8], bstate[0:1])):
        for part in range(2):
            total_o[i, pl.ds(2 * h + part, 1), :] = line[:, 128 * part : 128 * part + 128]


def forward_pass(at, *inputs):
    head = lambda h, at: (0, at[0] * HEADS + h)
    saved = pl.BlockSpec((1, CHIP_TOK, HEAD_W), lambda h, at: (h, 0, 0))
    matrix = pl.BlockSpec((1, HEAD_W, HEAD_W), lambda h, at: (h, 0, 0))
    big = (HEADS, CHIP_TOK, HEAD_W)
    return pl.pallas_call(
        forward_kernel,
        grid_spec=pltpu.PrefetchScalarGridSpec(
            num_scalar_prefetch=1,
            grid=(HEADS,),
            in_specs=[pl.BlockSpec((TOK, HEAD_W), head)] * 4
            + [pl.BlockSpec((MARGIN, HEAD_W), lambda h, at: (0, h)), pl.BlockSpec((8, HEAD_W), head)]
            + [matrix] * 2,
            out_specs=[saved] * 9
            + [
                pl.BlockSpec((1, 32, HEAD_W), lambda h, at: (h, 0, 0)),
                pl.BlockSpec((3, 16, 128), lambda h, at: (0, 0, 0)),
            ],
            scratch_shapes=[pltpu.VMEM((EDGE + CHIP_TOK, HEAD_W), F32)]
            + [pltpu.VMEM((CHIP_TOK, HEAD_W), F32)] * 4,
        ),
        out_shape=[jax.ShapeDtypeStruct(big, F32)] * 6
        + [jax.ShapeDtypeStruct(big, BF16)] * 3
        + [
            jax.ShapeDtypeStruct((HEADS, 32, HEAD_W), F32),
            jax.ShapeDtypeStruct((3, 16, 128), F32),
        ],
        compiler_params=pltpu.CompilerParams(vmem_limit_bytes=VMEM_LIMIT),
        cost_estimate=CHEAP,
        name="gates",
    )(at, *inputs)


def join_kernel(axis, first, last, at, own, r1, r2, r3, *refs):
    before = None if first else refs[0]
    outs = refs if first else refs[1:]
    here = at[1 + axis]
    rows = lambda ref: [ref[i] for i in range(3)]
    t0, f0, b0 = rows(own)
    pieces = [rows(r) for r in (r1, r2, r3)]
    one, zero = jnp.ones_like(t0), jnp.zeros_like(t0)
    early = [jnp.full(t0.shape, here + k >= 4) for k in (1, 2, 3)]
    pt, pf = one, zero
    for k in range(3):
        t, f, _ = pieces[k]
        pf = jnp.where(early[k], t * pf + f, pf)
        pt = jnp.where(early[k], t * pt, pt)
    bt, bs = one, zero
    for k in (2, 1, 0):
        t, _, b = pieces[k]
        bs = jnp.where(early[k], bs, t * bs + b)
        bt = jnp.where(early[k], bt, t * bt)
    if first:
        acc = [pt, pf, bt, bs]
    else:
        ep, es, fp, fs = [before[i] for i in range(4)]
        acc = [ep * pt, ep * pf + es, fp * bt, fp * bs + fs]
    if last:
        outs[0][0] = acc[1]
        outs[0][1] = acc[3]
        return
    f = t0 * pf + f0
    for k in range(3):
        f = jnp.where(early[k], f, pieces[k][0] * f + pieces[k][1])
    b = t0 * bs + b0
    for k in (2, 1, 0):
        b = jnp.where(early[k], pieces[k][0] * b + pieces[k][2], b)
    outs[0][0] = pt * t0 * bt
    outs[0][1] = f
    outs[0][2] = b
    for i in range(4):
        outs[1][i] = acc[i]


def entering(at, total):
    acc = None
    value = total
    for axis in (2, 1, 0):
        first, last = axis == 2, axis == 0
        args = [value] + [send_on(value, axis, -k) for k in (1, 2, 3)]
        if not first:
            args.append(acc)
        shapes = [((2, 16, 128), F32)] if last else [((3, 16, 128), F32), ((4, 16, 128), F32)]
        out = on_core(
            functools.partial(join_kernel, axis, first, last), shapes, at, *args, name="join"
        )
        if last:
            return out[0]
        value, acc = out


def backward_kernel(
    k, at, halo_in, par,
    decay, drive, quot, ga, gx, gk, mixed_b, u_b, g_b, w_x, w_a, lead, carry,
    *refs,
):
    pieces, (gm_o, u_s, a_s, dx_s, da_s) = refs[:-5], refs[-5:]
    j = pl.program_id(0)
    h = 2 * lax.rem(at[1] + k, 4) + j
    load_conv_input(u_s, u_b[0].astype(F32), halo_in[...])
    row = lambda k: wide(par[k : k + 1, :], 8)
    entry = [
        wide(
            jnp.concatenate([carry[i, pl.ds(2 * h + p, 1), :] for p in range(2)], axis=1), 8
        )
        for i in range(2)
    ]
    state = lead[0, 8:16, :] + lead[0, 0:8, :] * entry[0]
    back = lead[0, 24:32, :] + lead[0, 16:24, :] * entry[1]
    for r in range(GROUPS - 2, -1, -2):
        grads = g_b[0, 8 * r : 8 * r + 16, :].astype(F32)
        for q in (1, 0):
            rows = slice(8 * (r + q), 8 * (r + q) + 8)
            adjoint = grads[8 * q : 8 * q + 8] + back
            a_s[rows, :] = adjoint
            back = decay[0, rows, :] * adjoint
    rate = row(7)
    eighth = 0.125 * rate
    zero = jnp.zeros((8, HEAD_W), F32)
    sum_x, sum_a, sum_rate = zero, zero, zero
    for r in range(0, GROUPS, 2):
        pair_x, pair_a = [], []
        for q in (r, r + 1):
            rows = slice(8 * q, 8 * q + 8)
            adjoint = a_s[rows, :]
            passed = state * decay[0, rows, :]
            drv = drive[0, rows, :]
            grad_log = adjoint * (passed - quot[0, rows, :])
            state = passed + drv
            gate = ga[0, rows, :]
            term = gate * grad_log
            dz_a = term * (rate + eighth * gate)
            dz_x = adjoint * drv * (1.0 - gx[0, rows, :])
            sum_rate = sum_rate + term
            sum_a = sum_a + dz_a
            sum_x = sum_x + dz_x
            gm_o[0, rows, :] = adjoint * gk[0, rows, :]
            pair_x.append(dz_x)
            pair_a.append(dz_a)
        rows = slice(8 * r, 8 * r + 16)
        dx_s[rows, :] = jnp.concatenate(pair_x, 0).astype(BF16)
        da_s[rows, :] = jnp.concatenate(pair_a, 0).astype(BF16)
    dz_x, dz_a = dx_s[...], da_s[...]
    gm_o[0] += dot(dz_x, w_x[0], ((1,), (1,))) + dot(dz_a, w_a[0], ((1,), (1,)))
    mixed = mixed_b[0]
    grad_w = [dot(mixed, dz, ((0,), (0,))) for dz in (dz_x, dz_a)]
    for n in range(2):

        @pl.when(j == n)
        def _(half=pieces[n]):
            half[:HEAD_W, :HEAD_W] = grad_w[0].astype(half.dtype)
            half[:HEAD_W, HEAD_W:] = grad_w[1].astype(half.dtype)

    sum_c, sum_k = zero, [zero] * (MARGIN + 1)
    for q in range(GROUPS):
        here = gm_o[0, 8 * q : 8 * q + 8, :]
        sum_c = sum_c + here
        for t in range(MARGIN + 1):
            lo = EDGE + 8 * (q - t)
            sum_k[t] = sum_k[t] + here * u_s[lo : lo + 8, :]
    sums = [sum_x, sum_a, sum_rate] + sum_k + [sum_c]
    small = jnp.concatenate([jnp.sum(s, axis=0, keepdims=True) for s in sums], 0)
    if pieces[1].dtype == BF16:
        small = in_two(small)
    pieces[1][HEAD_W:, columns(j * HEAD_W)] = small


def in_two(small):
    high = small.astype(BF16).astype(F32)
    return jnp.concatenate([high, small - high], 0).astype(BF16)


def backward_chunk(k, at, *operands):
    local = lambda j, at: 2 * lax.rem(at[1] + k, 4) + j
    outer = lambda j, at: at[0] * HEADS + local(j, at)
    saved = pl.BlockSpec((1, CHIP_TOK, HEAD_W), lambda j, at: (local(j, at), 0, 0))
    low = ((HEAD_W, BOTH), BF16 if k in (2, 3) else F32)
    high = ((HEAD_W + 16, BOTH), BF16) if k in (1, 2) else ((HEAD_W + 8, BOTH), F32)
    pieces = [low, high]
    return pl.pallas_call(
        functools.partial(backward_kernel, k),
        grid_spec=pltpu.PrefetchScalarGridSpec(
            num_scalar_prefetch=1,
            grid=(2,),
            in_specs=[
                pl.BlockSpec((MARGIN, HEAD_W), lambda j, at: (0, local(j, at))),
                pl.BlockSpec((8, HEAD_W), lambda j, at: (0, outer(j, at))),
            ]
            + [saved] * 11
            + [
                pl.BlockSpec((1, 32, HEAD_W), lambda j, at: (local(j, at), 0, 0)),
                pl.BlockSpec((2, 16, 128), lambda j, at: (0, 0, 0)),
            ],
            out_specs=[pl.BlockSpec(shape, lambda j, at: (0, 0)) for shape, _ in pieces]
            + [pl.BlockSpec((1, CHIP_TOK, HEAD_W), lambda j, at: (j, 0, 0))],
            scratch_shapes=[
                pltpu.VMEM((EDGE + CHIP_TOK, HEAD_W), F32),
                pltpu.VMEM((CHIP_TOK, HEAD_W), F32),
                pltpu.VMEM((CHIP_TOK, HEAD_W), BF16),
                pltpu.VMEM((CHIP_TOK, HEAD_W), BF16),
            ],
        ),
        out_shape=[jax.ShapeDtypeStruct(*piece) for piece in pieces]
        + [jax.ShapeDtypeStruct((2, CHIP_TOK, HEAD_W), F32)],
        compiler_params=pltpu.CompilerParams(vmem_limit_bytes=VMEM_LIMIT),
        cost_estimate=CHEAP,
        name="grads",
    )(at, *operands)


def input_kernel(at, gm0, gm1, gm2, gm3, par, own_o, send_o, edge_o, gm_s, dx_s):
    own, other = orders(at[0])
    sub = lax.broadcasted_iota(jnp.int32, (8, HEAD_W), 0)
    for k, gm in enumerate((gm0, gm1, gm2, gm3)):

        def one_head(j, _):
            h = 2 * lax.rem(at[1] + k, 4) + j
            head = at[0] * HEADS + h
            local, outer = columns(h * HEAD_W), columns(head * HEAD_W)
            for i in range(MARGIN):
                first = gm[j, 8 * i : 8 * i + 8, :]
                edge_o[MARGIN + i : MARGIN + i + 1, local] = first[0:1]
                gm_s[8 * i : 8 * i + 8, :] = jnp.where(sub == 7, 0.0, pltpu.roll(first, 7, 0))
            taps = [wide(par[t : t + 1, outer], 8) for t in range(MARGIN + 1)]
            for r in range(0, GROUPS, 2):
                pair = []
                for q in (r, r + 1):
                    grad = taps[0] * gm[j, 8 * q : 8 * q + 8, :]
                    for t in range(1, MARGIN + 1):
                        lo = 8 * (q + t)
                        if q + t < GROUPS:
                            grad = grad + taps[t] * gm[j, lo : lo + 8, :]
                        else:
                            lo -= CHIP_TOK
                            grad = grad + taps[t] * gm_s[lo : lo + 8, :]
                    if q >= GROUPS - MARGIN:
                        at_edge = q - GROUPS + MARGIN
                        edge_o[at_edge : at_edge + 1, local] = grad[7:8]
                    pair.append(grad)
                dx_s[8 * r : 8 * r + 16, :] = jnp.concatenate(pair, 0).astype(BF16)
            grad_b = dx_s[...]
            own_o[:, local] = dot(own, grad_b, ((0,), (0,))).astype(BF16)
            send_o[:, local] = dot(other, grad_b, ((0,), (0,))).astype(BF16)
            return 0

        lax.fori_loop(0, 2, one_head, 0)


def input_pass(at, par, gms):
    return on_core(
        input_kernel,
        [((TOK, HALF), BF16), ((TOK, HALF), BF16), ((8, HALF), F32)],
        at, *gms, par,
        scratch=[((EDGE, HEAD_W), F32), ((CHIP_TOK, HEAD_W), BF16)],
        name="grad_input",
    )


def merge_kernel(at, mine, half, out):
    out[:HEAD_W, :] = (mine[:HEAD_W, :] + half[:HEAD_W, :].astype(F32)).astype(BF16)
    if out.shape[0] > HEAD_W:
        parts = half[HEAD_W:, :].astype(F32)
        out[HEAD_W:, :] = in_two(mine[HEAD_W:, :] + (parts[0:8] + parts[8:16]))


def merge(at, mine, half):
    (out,) = on_core(merge_kernel, [(half.shape, BF16)], at, mine, half, name="merge")
    return out


def spread_kernel(at, low, high, low1, high1, low2, high2, out):
    small = high[HEAD_W:, :]
    for r in (high1, high2):
        parts = r[HEAD_W:, :].astype(F32)
        small = small + (parts[0:8] + parts[8:16])
    tail = in_two(small)
    for n, (a, b, c) in enumerate(((low, low1, low2), (high, high1, high2))):
        total = a[:HEAD_W, :] + b[:HEAD_W, :].astype(F32) + c[:HEAD_W, :].astype(F32)
        for p in range(PLANE // 2):
            at_chip = n * (PLANE // 2) + p
            out[at_chip, :SHARE, :] = total[SHARE * p : SHARE * (p + 1)].astype(BF16)
            out[at_chip, SHARE:, :] = tail


def plane_kernel(at, pieces, out, tail):
    total = pieces[0].astype(F32)
    for p in range(1, PLANE):
        total = total + pieces[p].astype(F32)
    done = total[:SHARE].astype(BF16)
    for p in range(PLANE):
        out[p] = done
    tail[...] = in_two(total[SHARE : SHARE + 8] + total[SHARE + 8 :])


def trade(pieces):
    groups = [list(range(c, 32, 2)) for c in range(2)]
    return lax.all_to_all(pieces, "inner", 0, 0, axis_index_groups=groups)


def lay_kernel(at, body, tail, low, high):
    for p in range(PLANE // 2):
        rows = slice(SHARE * p, SHARE * (p + 1))
        low[rows, :] = body[p]
        high[rows, :] = body[PLANE // 2 + p]
    high[HEAD_W:, :] = tail[...]


def unpack_kernel(items, count, lines, at, *refs):
    pieces, refs = refs[:count], refs[count:]
    buf, sems = refs[-2:]
    if lines:
        a_param, tails, refs = refs[0], refs[1:9], refs[9:]
        lines_o, refs = refs[-7:-2], refs[:-7] + refs[-2:]
    wx_o, wa_o = refs[-4:-2]
    copies = []
    for parts, k, j, mine in items:
        owner = at[0] if mine else 1 - at[0]
        chunk = j // 2 if k is None else lax.rem(at[1] + k, 4)
        head = owner * HEADS + 2 * chunk + j % 2
        for i, out in enumerate((wx_o, wa_o)):
            n, place = len(copies), 0
            for operand, lead, first, rows in parts:
                ref = pieces[operand] if lead is None else pieces[operand].at[lead]
                buf[n, place : place + rows, :] = ref[
                    first : first + rows, HEAD_W * i : HEAD_W * (i + 1)
                ].astype(F32)
                place += rows
            copies.append(pltpu.make_async_copy(buf.at[n], out.at[head], sems.at[n]))
            copies[n].start()
    if lines:
        bx_o, ba_o, ap_o, taps_o, cb_o = lines_o
        for n, piece in enumerate(tails):
            owner = at[0] if n < 4 else 1 - at[0]
            parts = piece[piece.shape[0] - 16 :, :].astype(F32)
            small = parts[0:8] + parts[8:16]
            cols = columns(owner * HALF + lax.rem(at[1] + n % 4, 4) * BOTH, BOTH)
            bx_o[:, cols] = small[0:1]
            ba_o[:, cols] = small[1:2]
            ap_o[:, cols] = small[2:3] * jax.nn.sigmoid(a_param[:, cols])
            taps_o[:, cols] = small[3:7]
            cb_o[:, cols] = small[7:8]
    for copy in copies:
        copy.wait()


def unpack(at, pieces, items, done, lines=()):
    away = pl.BlockSpec(memory_space=pl.ANY)
    big = jax.ShapeDtypeStruct((2 * HEADS, HEAD_W, HEAD_W), F32)
    line = jax.ShapeDtypeStruct((1, WIDTH), F32)
    taps = jax.ShapeDtypeStruct((MARGIN + 1, WIDTH), F32)
    count, before = len(pieces), 1 + len(pieces) + len(lines)
    return pl.pallas_call(
        functools.partial(unpack_kernel, items, count, bool(lines)),
        in_specs=[pl.BlockSpec(memory_space=pltpu.SMEM)]
        + whole(before - 1)
        + [away] * len(done),
        out_specs=[away] * 2 + whole(5 if lines else 0),
        out_shape=[big, big] + ([line, line, line, taps, line] if lines else []),
        input_output_aliases={before + i: i for i in range(len(done))},
        scratch_shapes=[
            pltpu.VMEM((2 * len(items), HEAD_W, HEAD_W), F32),
            pltpu.SemaphoreType.DMA((2 * len(items),)),
        ],
        compiler_params=pltpu.CompilerParams(vmem_limit_bytes=VMEM_LIMIT),
        cost_estimate=CHEAP,
        name="unpack",
    )(at, *pieces, *lines, *done)


def assemble_kernel(at, own, other, fix, fix_other, out):
    mine, rest = columns(at[0] * HALF, HALF), columns((1 - at[0]) * HALF, HALF)
    out[:, mine] = own[...]
    out[:, rest] = other[...]

    @pl.when(at[0] == 1)
    def _():
        for half, lines, cols in ((own, fix, mine), (other, fix_other, rest)):
            tail = half[TOK - 16 :, :].astype(F32)
            tail = jnp.concatenate([tail[: 16 - MARGIN], lines[0:MARGIN, :].astype(F32)], 0)
            out[TOK - 16 :, cols] = tail.astype(BF16)


def on_device(conv_input, grad_out, conv_w, conv_b, w_x, b_x, w_a, b_a, a_param):
    outer, inner = lax.axis_index("outer"), lax.axis_index("inner")
    core = inner % 2
    at = jnp.stack([core, outer, inner // 8, (inner // 2) % 4]).astype(jnp.int32)
    rate = jax.nn.softplus(a_param)
    par = jnp.concatenate([conv_w, jnp.stack([conv_b, b_x, b_a, rate])], axis=0)
    heads = [lax.dynamic_slice_in_dim(w, core * HEADS, HEADS, 0) for w in (w_x, w_a)]
    u_other, g_other = swap_cores(conv_input), swap_cores(grad_out)
    end = jnp.where(core == 0, u_other[TOK - MARGIN :, :HALF], conv_input[TOK - MARGIN :, HALF:])
    halo = lax.ppermute(end, AXES, [(i, i + 2) for i in range(126)])
    *saved, lead, total = forward_pass(
        at, u_other, g_other, conv_input, grad_out, halo, par, *heads
    )
    operands = (halo, par, *saved, *heads, lead, entering(at, total))
    gms = [None] * 4
    far_low, far_high, gms[2] = backward_chunk(2, at, *operands)
    far_low, far_high = send_on(far_low, 0, 1), send_on(far_high, 0, -1)
    right_low, right_high, gms[1] = backward_chunk(1, at, *operands)
    from_left = send_on(right_high, 0, 1)
    left_low, left_high, gms[3] = backward_chunk(3, at, *operands)
    from_right = send_on(left_low, 0, -1)
    own_low, own_high, gms[0] = backward_chunk(0, at, *operands)
    arrived = (
        send_on(merge(at, right_low, far_low), 0, 1),
        from_left,
        from_right,
        send_on(merge(at, left_high, far_high), 0, -1),
    )

    (pieces,) = on_core(
        spread_kernel,
        [((PLANE, SHARE + 16, BOTH), BF16)],
        at, own_low, own_high, *arrived,
        name="spread",
    )
    pieces, gms = lax.optimization_barrier((pieces, gms))
    traded = trade(pieces)
    own_u, send_u, edge = input_pass(at, par, gms)
    other_u = swap_cores(send_u)
    traded, own_u, other_u, edge = lax.optimization_barrier((traded, own_u, other_u, edge))
    shared, tail = on_core(
        plane_kernel,
        [((PLANE, SHARE, BOTH), BF16), ((16, BOTH), BF16)],
        at, traded,
        name="plane",
    )
    traded = trade(shared)
    low, high = on_core(
        lay_kernel,
        [((HEAD_W, BOTH), BF16), ((HEAD_W + 16, BOTH), BF16)],
        at, traded, tail,
        name="lay",
    )

    left_low, right_high = send_on(low, 0, 1), send_on(high, 0, -1)
    left_high, right_low = send_on(high, 0, 1), send_on(low, 0, -1)
    theirs = [swap_cores(low), swap_cores(high)]
    one = lambda n: ((n, None, 0, HEAD_W),)
    items = [(one(2 * c + j), 0, j, c == 0) for c in range(2) for j in range(2)]
    weights = unpack(at, [low, high] + theirs, items, ())
    edge, theirs = lax.optimization_barrier((edge, theirs))
    far = [send_on(left_low, 0, 1), send_on(right_high, 0, -1)]

    after = lax.ppermute(
        edge[MARGIN : 2 * MARGIN].astype(BF16), AXES, [(i, i - 2) for i in range(2, 128)]
    ).astype(F32)
    cols = lax.dynamic_slice(conv_w, (0, core * HALF), (4, HALF))
    fixed = []
    for m in range(MARGIN):
        line = edge[m]
        for k in range(MARGIN - m, MARGIN + 1):
            line = line + cols[k] * after[m + k - MARGIN]
        fixed.append(line)
    fix = jnp.stack(fixed).astype(BF16)
    (grad_u,) = on_core(
        assemble_kernel,
        [((TOK, WIDTH), BF16)],
        at, own_u, other_u, fix, swap_cores(fix),
        name="assemble",
    )
    near = [right_low, right_high, left_low, left_high]
    near_items = [(one(n), (1, 3)[n // 2], n % 2, True) for n in range(4)]
    weights = unpack(at, near, near_items, weights)
    far, near, weights, grad_u = lax.optimization_barrier((far, near, weights, grad_u))
    far_other = [swap_cores(piece) for piece in far]
    near_other = [swap_cores(piece) for piece in near]
    weights = unpack(at, far, [(one(j), 2, j, True) for j in range(2)], weights)
    items = [(one(n), (1, 3, 2)[n // 2], n % 2, False) for n in range(6)]
    tails = [high, near[1], far[1], near[3]]
    tails += [theirs[1], near_other[1], far_other[1], near_other[3]]
    lines = (a_param.reshape(1, WIDTH), *tails)
    *weights, bx, ba, ap, taps, cb = unpack(at, near_other + far_other, items, weights, lines)
    flat = lambda line: line.reshape(WIDTH)
    return (grad_u, *weights, flat(bx), flat(ba), flat(ap), taps, flat(cb))


def solution(mesh):
    split = P(AXES, None)
    return jax.shard_map(
        on_device,
        mesh=mesh,
        in_specs=(split, split) + (P(),) * 7,
        out_specs=(split,) + (P(),) * 7,
        check_vma=False,
    )
```

```python
import functools

import jax
import jax.numpy as jnp
from jax import lax
from jax.experimental import pallas as pl
from jax.experimental.pallas import tpu as pltpu
from jax.sharding import PartitionSpec as P

AXES = ("outer", "inner")
F32, BF16 = jnp.float32, jnp.bfloat16
TOK = 128
CHIP_TOK = 256
GROUPS = CHIP_TOK // 8
WIDTH = 4096
HALF = 2048
HEAD_W = 256
HEADS = 8
PLANE = 16
SHARE = 32
BOTH = 2 * HEAD_W
MARGIN = 3
EDGE = 8 * MARGIN
ROOT_FLOOR = 2.5e-07
VMEM_LIMIT = 16 * 1024 * 1024
CHEAP = pl.CostEstimate(flops=1000, bytes_accessed=1000, transcendentals=0)


def place(index):
    return [index // 32, (index // 8) % 4, (index // 2) % 4, index % 2]


def number(coords):
    return coords[0] * 32 + coords[1] * 8 + coords[2] * 2 + coords[3]


def turned(axis, steps):
    size = 2 if axis == 3 else 4
    pairs = []
    for source in range(128):
        coords = place(source)
        coords[axis] = (coords[axis] + steps) % size
        pairs.append((source, number(coords)))
    return pairs


def send_on(value, axis, steps):
    return lax.ppermute(value, AXES, turned(axis, steps))


def swap_cores(value):
    return send_on(value, 3, 1)


def dot(a, b, dims):
    return lax.dot_general(a, b, (dims, ((), ())), preferred_element_type=F32)


def orders(core):
    row = lax.broadcasted_iota(jnp.int32, (CHIP_TOK, TOK), 0)
    col = lax.broadcasted_iota(jnp.int32, (CHIP_TOK, TOK), 1)
    token = (row % 8) * GROUPS + row // 8
    own = (token == col + core * TOK).astype(F32).astype(BF16)
    other = (token == col + (1 - core) * TOK).astype(F32).astype(BF16)
    return own, other


def wide(row, rows):
    return jnp.broadcast_to(row, (rows, row.shape[1]))


def load_conv_input(u_s, u, halo):
    sub = lax.broadcasted_iota(jnp.int32, (8, HEAD_W), 0)
    u_s[EDGE:, :] = u
    for k in range(1, MARGIN + 1):
        last = u_s[EDGE + CHIP_TOK - 8 * k : EDGE + CHIP_TOK - 8 * (k - 1), :]
        first = wide(halo[MARGIN - k : MARGIN - k + 1, :].astype(F32), 8)
        u_s[EDGE - 8 * k : EDGE - 8 * (k - 1), :] = jnp.where(
            sub == 0, first, pltpu.roll(last, 1, 0)
        )


def whole(count):
    return [pl.BlockSpec(memory_space=pltpu.VMEM)] * count


def on_core(body, shapes, *args, scratch=(), away=(), name):
    specs = [pl.BlockSpec(memory_space=pltpu.SMEM)] + whole(len(args) - 1)
    for i in away:
        specs[i] = pl.BlockSpec(memory_space=pl.ANY)
    return pl.pallas_call(
        body,
        in_specs=specs,
        out_specs=whole(len(shapes)),
        out_shape=[jax.ShapeDtypeStruct(shape, dtype) for shape, dtype in shapes],
        scratch_shapes=[
            s if not isinstance(s, tuple) else pltpu.VMEM(s[0], s[1]) for s in scratch
        ],
        compiler_params=pltpu.CompilerParams(vmem_limit_bytes=VMEM_LIMIT),
        cost_estimate=CHEAP,
        name=name,
    )(*args)


def columns(first, count=HEAD_W):
    return pl.ds(pl.multiple_of(first, count), count)


def forward_kernel(
    at, u_other, g_other, u_own, g_own, halo_in, par, w_x, w_a,
    decay_o, drive_o, quot_o, ga_o, gx_o, gk_o, mixed_o, u_o, g_o, lead_o, total_o,
    u_s, g_s, mix_s, zx_s, za_s,
):
    own, other = orders(at[0])
    step = 16

    h = pl.program_id(0)


    u = dot(own, u_own[...], ((1,), (0,))) + dot(other, u_other[...], ((1,), (0,)))
    g = dot(own, g_own[...], ((1,), (0,))) + dot(other, g_other[...], ((1,), (0,)))
    u_o[0] = u.astype(BF16)
    g_o[0] = g.astype(BF16)
    g_s[...] = g
    load_conv_input(u_s, u, halo_in[...])
    row = lambda k, rows: wide(par[k : k + 1, :], rows)
    taps = [row(k, step) for k in range(MARGIN + 1)]
    bias = row(4, step)
    for c in range(0, CHIP_TOK, step):
        mixed = bias
        for k in range(MARGIN + 1):
            mixed = mixed + taps[k] * u_s[EDGE - 8 * k + c : EDGE - 8 * k + c + step, :]
        mix_s[c : c + step, :] = mixed
        mixed_o[0, c : c + step, :] = mixed.astype(BF16)
    mixed_b = mixed_o[0]
    zx_s[...] = dot(mixed_b, w_x[0], ((1,), (0,)))
    za_s[...] = dot(mixed_b, w_a[0], ((1,), (0,)))
    b_x, b_a = row(5, step), row(6, step)
    slope = -8.0 * row(7, step)
    prod = jnp.ones((8, HEAD_W), F32)
    state = jnp.zeros((8, HEAD_W), F32)
    back = jnp.zeros((8, HEAD_W), F32)
    for c in range(0, CHIP_TOK, step):
        rows = slice(c, c + step)
        mixed = mix_s[rows, :]
        gate_x = jax.nn.sigmoid(zx_s[rows, :] + b_x)
        gate_a = jax.nn.sigmoid(za_s[rows, :] + b_a)
        x = slope * gate_a
        series = 1.0 / 120.0 + x * (1.0 / 720.0)
        for coef in (1.0 / 24.0, 1.0 / 6.0, 0.5, 1.0):
            series = coef + x * series
        less = x * series
        decay = 1.0 + less
        vari = -less * (2.0 + less)
        mult = jnp.sqrt(vari)
        gk = gate_x * mult
        drive = gk * mixed
        decay_o[0, rows, :] = decay
        drive_o[0, rows, :] = drive
        quot_o[0, rows, :] = (
            gate_x * mixed * (decay * decay) * lax.rsqrt(jnp.maximum(vari, ROOT_FLOOR))
        )
        ga_o[0, rows, :] = -8.0 * gate_a
        gx_o[0, rows, :] = gate_x
        gk_o[0, rows, :] = gk
        for q in (0, 8):
            part = decay[q : q + 8]
            prod = prod * part
            state = part * state + drive[q : q + 8]
            back = back + prod * g_s[c + q : c + q + 8, :]
    sub = lax.broadcasted_iota(jnp.int32, (8, HEAD_W), 0)
    fprod, fstate = prod, state
    bprod, bstate = prod, back
    for d in (1, 2, 4):
        up = sub >= d
        fstate = jnp.where(up, fprod * pltpu.roll(fstate, d, 0) + fstate, fstate)
        fprod = jnp.where(up, fprod * pltpu.roll(fprod, d, 0), fprod)
        down = sub < 8 - d
        bstate = jnp.where(down, bprod * pltpu.roll(bstate, 8 - d, 0) + bstate, bstate)
        bprod = jnp.where(down, bprod * pltpu.roll(bprod, 8 - d, 0), bprod)
    lead_o[0, 0:8, :] = jnp.where(sub == 0, 1.0, pltpu.roll(fprod, 1, 0))
    lead_o[0, 8:16, :] = jnp.where(sub == 0, 0.0, pltpu.roll(fstate, 1, 0))
    lead_o[0, 16:24, :] = jnp.where(sub == 7, 1.0, pltpu.roll(bprod, 7, 0))
    lead_o[0, 24:32, :] = jnp.where(sub == 7, 0.0, pltpu.roll(bstate, 7, 0))
    for i, line in enumerate((fprod[7:8], fstate[7:8], bstate[0:1])):
        for part in range(2):
            total_o[i, pl.ds(2 * h + part, 1), :] = line[:, 128 * part : 128 * part + 128]


def forward_pass(at, *inputs):
    head = lambda h, at: (0, at[0] * HEADS + h)
    saved = pl.BlockSpec((1, CHIP_TOK, HEAD_W), lambda h, at: (h, 0, 0))
    matrix = pl.BlockSpec((1, HEAD_W, HEAD_W), lambda h, at: (h, 0, 0))
    big = (HEADS, CHIP_TOK, HEAD_W)
    return pl.pallas_call(
        forward_kernel,
        grid_spec=pltpu.PrefetchScalarGridSpec(
            num_scalar_prefetch=1,
            grid=(HEADS,),
            in_specs=[pl.BlockSpec((TOK, HEAD_W), head)] * 4
            + [pl.BlockSpec((MARGIN, HEAD_W), lambda h, at: (0, h)), pl.BlockSpec((8, HEAD_W), head)]
            + [matrix] * 2,
            out_specs=[saved] * 9
            + [
                pl.BlockSpec((1, 32, HEAD_W), lambda h, at: (h, 0, 0)),
                pl.BlockSpec((3, 16, 128), lambda h, at: (0, 0, 0)),
            ],
            scratch_shapes=[pltpu.VMEM((EDGE + CHIP_TOK, HEAD_W), F32)]
            + [pltpu.VMEM((CHIP_TOK, HEAD_W), F32)] * 4,
        ),
        out_shape=[jax.ShapeDtypeStruct(big, F32)] * 6
        + [jax.ShapeDtypeStruct(big, BF16)] * 3
        + [
            jax.ShapeDtypeStruct((HEADS, 32, HEAD_W), F32),
            jax.ShapeDtypeStruct((3, 16, 128), F32),
        ],
        compiler_params=pltpu.CompilerParams(vmem_limit_bytes=VMEM_LIMIT),
        cost_estimate=CHEAP,
        name="gates",
    )(at, *inputs)


def join_kernel(axis, first, last, at, own, r1, r2, r3, *refs):
    before = None if first else refs[0]
    outs = refs if first else refs[1:]
    here = at[1 + axis]
    rows = lambda ref: [ref[i] for i in range(3)]
    t0, f0, b0 = rows(own)
    pieces = [rows(r) for r in (r1, r2, r3)]
    one, zero = jnp.ones_like(t0), jnp.zeros_like(t0)
    early = [jnp.full(t0.shape, here + k >= 4) for k in (1, 2, 3)]
    pt, pf = one, zero
    for k in range(3):
        t, f, _ = pieces[k]
        pf = jnp.where(early[k], t * pf + f, pf)
        pt = jnp.where(early[k], t * pt, pt)
    bt, bs = one, zero
    for k in (2, 1, 0):
        t, _, b = pieces[k]
        bs = jnp.where(early[k], bs, t * bs + b)
        bt = jnp.where(early[k], bt, t * bt)
    if first:
        acc = [pt, pf, bt, bs]
    else:
        ep, es, fp, fs = [before[i] for i in range(4)]
        acc = [ep * pt, ep * pf + es, fp * bt, fp * bs + fs]
    if last:
        outs[0][0] = acc[1]
        outs[0][1] = acc[3]
        return
    f = t0 * pf + f0
    for k in range(3):
        f = jnp.where(early[k], f, pieces[k][0] * f + pieces[k][1])
    b = t0 * bs + b0
    for k in (2, 1, 0):
        b = jnp.where(early[k], pieces[k][0] * b + pieces[k][2], b)
    outs[0][0] = pt * t0 * bt
    outs[0][1] = f
    outs[0][2] = b
    for i in range(4):
        outs[1][i] = acc[i]


def entering(at, total):
    acc = None
    value = total
    for axis in (2, 1, 0):
        first, last = axis == 2, axis == 0
        args = [value] + [send_on(value, axis, -k) for k in (1, 2, 3)]
        if not first:
            args.append(acc)
        shapes = [((2, 16, 128), F32)] if last else [((3, 16, 128), F32), ((4, 16, 128), F32)]
        out = on_core(
            functools.partial(join_kernel, axis, first, last), shapes, at, *args, name="join"
        )
        if last:
            return out[0]
        value, acc = out


def backward_kernel(
    k, at, halo_in, par,
    decay, drive, quot, ga, gx, gk, mixed_b, u_b, g_b, w_x, w_a, lead, carry,
    *refs,
):
    pieces, (gm_o, u_s, a_s, dx_s, da_s) = refs[:-5], refs[-5:]
    j = pl.program_id(0)
    h = 2 * lax.rem(at[1] + k, 4) + j
    load_conv_input(u_s, u_b[0].astype(F32), halo_in[...])
    row = lambda k: wide(par[k : k + 1, :], 8)
    entry = [
        wide(
            jnp.concatenate([carry[i, pl.ds(2 * h + p, 1), :] for p in range(2)], axis=1), 8
        )
        for i in range(2)
    ]
    state = lead[0, 8:16, :] + lead[0, 0:8, :] * entry[0]
    back = lead[0, 24:32, :] + lead[0, 16:24, :] * entry[1]
    for r in range(GROUPS - 2, -1, -2):
        grads = g_b[0, 8 * r : 8 * r + 16, :].astype(F32)
        for q in (1, 0):
            rows = slice(8 * (r + q), 8 * (r + q) + 8)
            adjoint = grads[8 * q : 8 * q + 8] + back
            a_s[rows, :] = adjoint
            back = decay[0, rows, :] * adjoint
    rate = row(7)
    eighth = 0.125 * rate
    zero = jnp.zeros((8, HEAD_W), F32)
    sum_x, sum_a, sum_rate = zero, zero, zero
    for r in range(0, GROUPS, 2):
        pair_x, pair_a = [], []
        for q in (r, r + 1):
            rows = slice(8 * q, 8 * q + 8)
            adjoint = a_s[rows, :]
            passed = state * decay[0, rows, :]
            drv = drive[0, rows, :]
            grad_log = adjoint * (passed - quot[0, rows, :])
            state = passed + drv
            gate = ga[0, rows, :]
            term = gate * grad_log
            dz_a = term * (rate + eighth * gate)
            dz_x = adjoint * drv * (1.0 - gx[0, rows, :])
            sum_rate = sum_rate + term
            sum_a = sum_a + dz_a
            sum_x = sum_x + dz_x
            gm_o[0, rows, :] = adjoint * gk[0, rows, :]
            pair_x.append(dz_x)
            pair_a.append(dz_a)
        rows = slice(8 * r, 8 * r + 16)
        dx_s[rows, :] = jnp.concatenate(pair_x, 0).astype(BF16)
        da_s[rows, :] = jnp.concatenate(pair_a, 0).astype(BF16)
    dz_x, dz_a = dx_s[...], da_s[...]
    gm_o[0] += dot(dz_x, w_x[0], ((1,), (1,))) + dot(dz_a, w_a[0], ((1,), (1,)))
    mixed = mixed_b[0]
    grad_w = [dot(mixed, dz, ((0,), (0,))) for dz in (dz_x, dz_a)]
    for n in range(2):

        @pl.when(j == n)
        def _(half=pieces[n]):
            half[:HEAD_W, :HEAD_W] = grad_w[0].astype(half.dtype)
            half[:HEAD_W, HEAD_W:] = grad_w[1].astype(half.dtype)

    sum_c, sum_k = zero, [zero] * (MARGIN + 1)
    for q in range(GROUPS):
        here = gm_o[0, 8 * q : 8 * q + 8, :]
        sum_c = sum_c + here
        for t in range(MARGIN + 1):
            lo = EDGE + 8 * (q - t)
            sum_k[t] = sum_k[t] + here * u_s[lo : lo + 8, :]
    sums = [sum_x, sum_a, sum_rate] + sum_k + [sum_c]
    small = jnp.concatenate([jnp.sum(s, axis=0, keepdims=True) for s in sums], 0)
    if pieces[1].dtype == BF16:
        small = in_two(small)
    pieces[1][HEAD_W:, columns(j * HEAD_W)] = small


def in_two(small):
    high = small.astype(BF16).astype(F32)
    return jnp.concatenate([high, small - high], 0).astype(BF16)


def backward_chunk(k, at, *operands):
    local = lambda j, at: 2 * lax.rem(at[1] + k, 4) + j
    outer = lambda j, at: at[0] * HEADS + local(j, at)
    saved = pl.BlockSpec((1, CHIP_TOK, HEAD_W), lambda j, at: (local(j, at), 0, 0))
    low = ((HEAD_W, BOTH), BF16 if k in (2, 3) else F32)
    high = ((HEAD_W + 16, BOTH), BF16) if k in (1, 2) else ((HEAD_W + 8, BOTH), F32)
    pieces = [low, high]
    return pl.pallas_call(
        functools.partial(backward_kernel, k),
        grid_spec=pltpu.PrefetchScalarGridSpec(
            num_scalar_prefetch=1,
            grid=(2,),
            in_specs=[
                pl.BlockSpec((MARGIN, HEAD_W), lambda j, at: (0, local(j, at))),
                pl.BlockSpec((8, HEAD_W), lambda j, at: (0, outer(j, at))),
            ]
            + [saved] * 11
            + [
                pl.BlockSpec((1, 32, HEAD_W), lambda j, at: (local(j, at), 0, 0)),
                pl.BlockSpec((2, 16, 128), lambda j, at: (0, 0, 0)),
            ],
            out_specs=[pl.BlockSpec(shape, lambda j, at: (0, 0)) for shape, _ in pieces]
            + [pl.BlockSpec((1, CHIP_TOK, HEAD_W), lambda j, at: (j, 0, 0))],
            scratch_shapes=[
                pltpu.VMEM((EDGE + CHIP_TOK, HEAD_W), F32),
                pltpu.VMEM((CHIP_TOK, HEAD_W), F32),
                pltpu.VMEM((CHIP_TOK, HEAD_W), BF16),
                pltpu.VMEM((CHIP_TOK, HEAD_W), BF16),
            ],
        ),
        out_shape=[jax.ShapeDtypeStruct(*piece) for piece in pieces]
        + [jax.ShapeDtypeStruct((2, CHIP_TOK, HEAD_W), F32)],
        compiler_params=pltpu.CompilerParams(vmem_limit_bytes=VMEM_LIMIT),
        cost_estimate=CHEAP,
        name="grads",
    )(at, *operands)


def input_kernel(at, gm0, gm1, gm2, gm3, par, own_o, send_o, edge_o, gm_s, dx_s):
    own, other = orders(at[0])
    sub = lax.broadcasted_iota(jnp.int32, (8, HEAD_W), 0)
    for k, gm in enumerate((gm0, gm1, gm2, gm3)):

        def one_head(j, _):
            h = 2 * lax.rem(at[1] + k, 4) + j
            head = at[0] * HEADS + h
            local, outer = columns(h * HEAD_W), columns(head * HEAD_W)
            for i in range(MARGIN):
                first = gm[j, 8 * i : 8 * i + 8, :]
                edge_o[MARGIN + i : MARGIN + i + 1, local] = first[0:1]
                gm_s[8 * i : 8 * i + 8, :] = jnp.where(sub == 7, 0.0, pltpu.roll(first, 7, 0))
            taps = [wide(par[t : t + 1, outer], 8) for t in range(MARGIN + 1)]
            for r in range(0, GROUPS, 2):
                pair = []
                for q in (r, r + 1):
                    grad = taps[0] * gm[j, 8 * q : 8 * q + 8, :]
                    for t in range(1, MARGIN + 1):
                        lo = 8 * (q + t)
                        if q + t < GROUPS:
                            grad = grad + taps[t] * gm[j, lo : lo + 8, :]
                        else:
                            lo -= CHIP_TOK
                            grad = grad + taps[t] * gm_s[lo : lo + 8, :]
                    if q >= GROUPS - MARGIN:
                        at_edge = q - GROUPS + MARGIN
                        edge_o[at_edge : at_edge + 1, local] = grad[7:8]
                    pair.append(grad)
                dx_s[8 * r : 8 * r + 16, :] = jnp.concatenate(pair, 0).astype(BF16)
            grad_b = dx_s[...]
            own_o[:, local] = dot(own, grad_b, ((0,), (0,))).astype(BF16)
            send_o[:, local] = dot(other, grad_b, ((0,), (0,))).astype(BF16)
            return 0

        lax.fori_loop(0, 2, one_head, 0)


def input_pass(at, par, gms):
    return on_core(
        input_kernel,
        [((TOK, HALF), BF16), ((TOK, HALF), BF16), ((8, HALF), F32)],
        at, *gms, par,
        scratch=[((EDGE, HEAD_W), F32), ((CHIP_TOK, HEAD_W), BF16)],
        name="grad_input",
    )


def merge_kernel(at, mine, half, out):
    out[:HEAD_W, :] = (mine[:HEAD_W, :] + half[:HEAD_W, :].astype(F32)).astype(BF16)
    if out.shape[0] > HEAD_W:
        parts = half[HEAD_W:, :].astype(F32)
        out[HEAD_W:, :] = in_two(mine[HEAD_W:, :] + (parts[0:8] + parts[8:16]))


def merge(at, mine, half):
    (out,) = on_core(merge_kernel, [(half.shape, BF16)], at, mine, half, name="merge")
    return out


def spread_kernel(at, low, high, low1, high1, low2, high2, out):
    small = high[HEAD_W:, :]
    for r in (high1, high2):
        parts = r[HEAD_W:, :].astype(F32)
        small = small + (parts[0:8] + parts[8:16])
    tail = in_two(small)
    for n, (a, b, c) in enumerate(((low, low1, low2), (high, high1, high2))):
        total = a[:HEAD_W, :] + b[:HEAD_W, :].astype(F32) + c[:HEAD_W, :].astype(F32)
        for p in range(PLANE // 2):
            at_chip = n * (PLANE // 2) + p
            out[at_chip, :SHARE, :] = total[SHARE * p : SHARE * (p + 1)].astype(BF16)
            out[at_chip, SHARE:, :] = tail


def plane_kernel(at, pieces, out, tail):
    total = pieces[0].astype(F32)
    for p in range(1, PLANE):
        total = total + pieces[p].astype(F32)
    done = total[:SHARE].astype(BF16)
    for p in range(PLANE):
        out[p] = done
    tail[...] = in_two(total[SHARE : SHARE + 8] + total[SHARE + 8 :])


def trade(pieces):
    groups = [list(range(c, 32, 2)) for c in range(2)]
    return lax.all_to_all(pieces, "inner", 0, 0, axis_index_groups=groups)


def lay_kernel(at, body, tail, low, high):
    for p in range(PLANE // 2):
        rows = slice(SHARE * p, SHARE * (p + 1))
        low[rows, :] = body[p]
        high[rows, :] = body[PLANE // 2 + p]
    high[HEAD_W:, :] = tail[...]


def unpack_kernel(items, count, lines, at, *refs):
    pieces, refs = refs[:count], refs[count:]
    buf, sems = refs[-2:]
    if lines:
        a_param, tails, refs = refs[0], refs[1:9], refs[9:]
        lines_o, refs = refs[-7:-2], refs[:-7] + refs[-2:]
    wx_o, wa_o = refs[-4:-2]
    copies = []
    for parts, k, j, mine in items:
        owner = at[0] if mine else 1 - at[0]
        chunk = j // 2 if k is None else lax.rem(at[1] + k, 4)
        head = owner * HEADS + 2 * chunk + j % 2
        for i, out in enumerate((wx_o, wa_o)):
            n, place = len(copies), 0
            for operand, lead, first, rows in parts:
                ref = pieces[operand] if lead is None else pieces[operand].at[lead]
                buf[n, place : place + rows, :] = ref[
                    first : first + rows, HEAD_W * i : HEAD_W * (i + 1)
                ].astype(F32)
                place += rows
            copies.append(pltpu.make_async_copy(buf.at[n], out.at[head], sems.at[n]))
            copies[n].start()
    if lines:
        bx_o, ba_o, ap_o, taps_o, cb_o = lines_o
        for n, piece in enumerate(tails):
            owner = at[0] if n < 4 else 1 - at[0]
            parts = piece[piece.shape[0] - 16 :, :].astype(F32)
            small = parts[0:8] + parts[8:16]
            cols = columns(owner * HALF + lax.rem(at[1] + n % 4, 4) * BOTH, BOTH)
            bx_o[:, cols] = small[0:1]
            ba_o[:, cols] = small[1:2]
            ap_o[:, cols] = small[2:3] * jax.nn.sigmoid(a_param[:, cols])
            taps_o[:, cols] = small[3:7]
            cb_o[:, cols] = small[7:8]
    for copy in copies:
        copy.wait()


def unpack(at, pieces, items, done, lines=()):
    away = pl.BlockSpec(memory_space=pl.ANY)
    big = jax.ShapeDtypeStruct((2 * HEADS, HEAD_W, HEAD_W), F32)
    line = jax.ShapeDtypeStruct((1, WIDTH), F32)
    taps = jax.ShapeDtypeStruct((MARGIN + 1, WIDTH), F32)
    count, before = len(pieces), 1 + len(pieces) + len(lines)
    return pl.pallas_call(
        functools.partial(unpack_kernel, items, count, bool(lines)),
        in_specs=[pl.BlockSpec(memory_space=pltpu.SMEM)]
        + whole(before - 1)
        + [away] * len(done),
        out_specs=[away] * 2 + whole(5 if lines else 0),
        out_shape=[big, big] + ([line, line, line, taps, line] if lines else []),
        input_output_aliases={before + i: i for i in range(len(done))},
        scratch_shapes=[
            pltpu.VMEM((2 * len(items), HEAD_W, HEAD_W), F32),
            pltpu.SemaphoreType.DMA((2 * len(items),)),
        ],
        compiler_params=pltpu.CompilerParams(vmem_limit_bytes=VMEM_LIMIT),
        cost_estimate=CHEAP,
        name="unpack",
    )(at, *pieces, *lines, *done)


def assemble_kernel(at, own, other, fix, fix_other, out):
    mine, rest = columns(at[0] * HALF, HALF), columns((1 - at[0]) * HALF, HALF)
    out[:, mine] = own[...]
    out[:, rest] = other[...]

    @pl.when(at[0] == 1)
    def _():
        for half, lines, cols in ((own, fix, mine), (other, fix_other, rest)):
            tail = half[TOK - 16 :, :].astype(F32)
            tail = jnp.concatenate([tail[: 16 - MARGIN], lines[0:MARGIN, :].astype(F32)], 0)
            out[TOK - 16 :, cols] = tail.astype(BF16)


def on_device(conv_input, grad_out, conv_w, conv_b, w_x, b_x, w_a, b_a, a_param):
    outer, inner = lax.axis_index("outer"), lax.axis_index("inner")
    core = inner % 2
    at = jnp.stack([core, outer, inner // 8, (inner // 2) % 4]).astype(jnp.int32)
    rate = jax.nn.softplus(a_param)
    par = jnp.concatenate([conv_w, jnp.stack([conv_b, b_x, b_a, rate])], axis=0)
    heads = [lax.dynamic_slice_in_dim(w, core * HEADS, HEADS, 0) for w in (w_x, w_a)]
    u_other, g_other = swap_cores(conv_input), swap_cores(grad_out)
    ends = lax.ppermute(
        conv_input[TOK - MARGIN :, :], AXES, [(2 * chip + 1, 2 * chip + 3) for chip in range(63)]
    )
    passed_on = lax.ppermute(
        ends[:, :HALF], AXES, [(2 * chip + 1, 2 * chip) for chip in range(64)]
    )
    halo = jnp.where(core == 0, passed_on, ends[:, HALF:])
    *saved, lead, total = forward_pass(
        at, u_other, g_other, conv_input, grad_out, halo, par, *heads
    )
    operands = (halo, par, *saved, *heads, lead, entering(at, total))
    gms = [None] * 4
    far_low, far_high, gms[2] = backward_chunk(2, at, *operands)
    far_low, far_high = send_on(far_low, 0, 1), send_on(far_high, 0, -1)
    right_low, right_high, gms[1] = backward_chunk(1, at, *operands)
    from_left = send_on(right_high, 0, 1)
    left_low, left_high, gms[3] = backward_chunk(3, at, *operands)
    from_right = send_on(left_low, 0, -1)
    own_low, own_high, gms[0] = backward_chunk(0, at, *operands)
    arrived = (
        send_on(merge(at, right_low, far_low), 0, 1),
        from_left,
        from_right,
        send_on(merge(at, left_high, far_high), 0, -1),
    )

    (pieces,) = on_core(
        spread_kernel,
        [((PLANE, SHARE + 16, BOTH), BF16)],
        at, own_low, own_high, *arrived,
        name="spread",
    )
    pieces, gms = lax.optimization_barrier((pieces, gms))
    traded = trade(pieces)
    own_u, send_u, edge = input_pass(at, par, gms)
    other_u = swap_cores(send_u)
    traded, own_u, other_u, edge = lax.optimization_barrier((traded, own_u, other_u, edge))
    shared, tail = on_core(
        plane_kernel,
        [((PLANE, SHARE, BOTH), BF16), ((16, BOTH), BF16)],
        at, traded,
        name="plane",
    )
    traded = trade(shared)
    low, high = on_core(
        lay_kernel,
        [((HEAD_W, BOTH), BF16), ((HEAD_W + 16, BOTH), BF16)],
        at, traded, tail,
        name="lay",
    )

    left_low, right_high = send_on(low, 0, 1), send_on(high, 0, -1)
    left_high, right_low = send_on(high, 0, 1), send_on(low, 0, -1)
    theirs = [swap_cores(low), swap_cores(high)]
    one = lambda n: ((n, None, 0, HEAD_W),)
    items = [(one(2 * c + j), 0, j, c == 0) for c in range(2) for j in range(2)]
    weights = unpack(at, [low, high] + theirs, items, ())
    edge, theirs = lax.optimization_barrier((edge, theirs))
    far = [send_on(left_low, 0, 1), send_on(right_high, 0, -1)]

    after = lax.ppermute(
        edge[MARGIN : 2 * MARGIN].astype(BF16), AXES, [(i, i - 2) for i in range(2, 128)]
    ).astype(F32)
    cols = lax.dynamic_slice(conv_w, (0, core * HALF), (4, HALF))
    fixed = []
    for m in range(MARGIN):
        line = edge[m]
        for k in range(MARGIN - m, MARGIN + 1):
            line = line + cols[k] * after[m + k - MARGIN]
        fixed.append(line)
    fix = jnp.stack(fixed).astype(BF16)
    (grad_u,) = on_core(
        assemble_kernel,
        [((TOK, WIDTH), BF16)],
        at, own_u, other_u, fix, swap_cores(fix),
        name="assemble",
    )
    first = [right_high, left_low]
    first_other = [swap_cores(piece) for piece in first]
    second = [right_low, left_high]
    items = [(one(0), 1, 1, True), (one(1), 3, 0, True), (one(2), 1, 0, True), (one(3), 3, 1, True)]
    weights = unpack(at, first + second, items, weights)
    far, second, weights, grad_u = lax.optimization_barrier((far, second, weights, grad_u))
    far_other = [swap_cores(piece) for piece in far]
    second_other = [swap_cores(piece) for piece in second]
    items = [(one(0), 2, 0, True), (one(1), 2, 1, True), (one(2), 1, 1, False), (one(3), 3, 0, False)]
    weights = unpack(at, far + first_other, items, weights)
    items = [(one(0), 2, 0, False), (one(1), 2, 1, False), (one(2), 1, 0, False), (one(3), 3, 1, False)]
    tails = [high, right_high, far[1], second[1]]
    tails += [theirs[1], first_other[0], far_other[1], second_other[1]]
    lines = (a_param.reshape(1, WIDTH), *tails)
    *weights, bx, ba, ap, taps, cb = unpack(at, far_other + second_other, items, weights, lines)
    flat = lambda line: line.reshape(WIDTH)
    return (grad_u, *weights, flat(bx), flat(ba), flat(ap), taps, flat(cb))


def solution(mesh):
    split = P(AXES, None)
    return jax.shard_map(
        on_device,
        mesh=mesh,
        in_specs=(split, split) + (P(),) * 7,
        out_specs=(split,) + (P(),) * 7,
        check_vma=False,
    )
```

```python
import functools

import jax
import jax.numpy as jnp
from jax import lax
from jax.experimental import pallas as pl
from jax.experimental.pallas import tpu as pltpu
from jax.sharding import PartitionSpec as P

AXES = ("outer", "inner")
F32, BF16 = jnp.float32, jnp.bfloat16
TOK = 128
CHIP_TOK = 256
GROUPS = CHIP_TOK // 8
WIDTH = 4096
HALF = 2048
HEAD_W = 256
HEADS = 8
PLANE = 16
SHARE = 32
BOTH = 2 * HEAD_W
MARGIN = 3
EDGE = 8 * MARGIN
ROOT_FLOOR = 2.5e-07
VMEM_LIMIT = 16 * 1024 * 1024
CHEAP = pl.CostEstimate(flops=1000, bytes_accessed=1000, transcendentals=0)


def place(index):
    return [index // 32, (index // 8) % 4, (index // 2) % 4, index % 2]


def number(coords):
    return coords[0] * 32 + coords[1] * 8 + coords[2] * 2 + coords[3]


def turned(axis, steps):
    size = 2 if axis == 3 else 4
    pairs = []
    for source in range(128):
        coords = place(source)
        coords[axis] = (coords[axis] + steps) % size
        pairs.append((source, number(coords)))
    return pairs


def send_on(value, axis, steps):
    return lax.ppermute(value, AXES, turned(axis, steps))


def swap_cores(value):
    return send_on(value, 3, 1)


def dot(a, b, dims):
    return lax.dot_general(a, b, (dims, ((), ())), preferred_element_type=F32)


def orders(core):
    row = lax.broadcasted_iota(jnp.int32, (CHIP_TOK, TOK), 0)
    col = lax.broadcasted_iota(jnp.int32, (CHIP_TOK, TOK), 1)
    token = (row % 8) * GROUPS + row // 8
    own = (token == col + core * TOK).astype(F32).astype(BF16)
    other = (token == col + (1 - core) * TOK).astype(F32).astype(BF16)
    return own, other


def wide(row, rows):
    return jnp.broadcast_to(row, (rows, row.shape[1]))


def load_conv_input(u_s, u, halo):
    sub = lax.broadcasted_iota(jnp.int32, (8, HEAD_W), 0)
    u_s[EDGE:, :] = u
    for k in range(1, MARGIN + 1):
        last = u_s[EDGE + CHIP_TOK - 8 * k : EDGE + CHIP_TOK - 8 * (k - 1), :]
        first = wide(halo[MARGIN - k : MARGIN - k + 1, :].astype(F32), 8)
        u_s[EDGE - 8 * k : EDGE - 8 * (k - 1), :] = jnp.where(
            sub == 0, first, pltpu.roll(last, 1, 0)
        )


def whole(count):
    return [pl.BlockSpec(memory_space=pltpu.VMEM)] * count


def on_core(body, shapes, *args, scratch=(), away=(), name):
    specs = [pl.BlockSpec(memory_space=pltpu.SMEM)] + whole(len(args) - 1)
    for i in away:
        specs[i] = pl.BlockSpec(memory_space=pl.ANY)
    return pl.pallas_call(
        body,
        in_specs=specs,
        out_specs=whole(len(shapes)),
        out_shape=[jax.ShapeDtypeStruct(shape, dtype) for shape, dtype in shapes],
        scratch_shapes=[
            s if not isinstance(s, tuple) else pltpu.VMEM(s[0], s[1]) for s in scratch
        ],
        compiler_params=pltpu.CompilerParams(vmem_limit_bytes=VMEM_LIMIT),
        cost_estimate=CHEAP,
        name=name,
    )(*args)


def columns(first, count=HEAD_W):
    return pl.ds(pl.multiple_of(first, count), count)


def forward_kernel(
    at, u_other, g_other, u_own, g_own, halo_in, par, w_x, w_a,
    decay_o, drive_o, quot_o, ga_o, gx_o, gk_o, mixed_o, u_o, g_o, lead_o, total_o,
    u_s, g_s, mix_s, zx_s, za_s,
):
    own, other = orders(at[0])
    step = 16

    h = pl.program_id(0)


    u = dot(own, u_own[...], ((1,), (0,))) + dot(other, u_other[...], ((1,), (0,)))
    g = dot(own, g_own[...], ((1,), (0,))) + dot(other, g_other[...], ((1,), (0,)))
    u_o[0] = u.astype(BF16)
    g_o[0] = g.astype(BF16)
    g_s[...] = g
    load_conv_input(u_s, u, halo_in[...])
    row = lambda k, rows: wide(par[k : k + 1, :], rows)
    taps = [row(k, step) for k in range(MARGIN + 1)]
    bias = row(4, step)
    for c in range(0, CHIP_TOK, step):
        mixed = bias
        for k in range(MARGIN + 1):
            mixed = mixed + taps[k] * u_s[EDGE - 8 * k + c : EDGE - 8 * k + c + step, :]
        mix_s[c : c + step, :] = mixed
        mixed_o[0, c : c + step, :] = mixed.astype(BF16)
    mixed_b = mixed_o[0]
    zx_s[...] = dot(mixed_b, w_x[0], ((1,), (0,)))
    za_s[...] = dot(mixed_b, w_a[0], ((1,), (0,)))
    b_x, b_a = row(5, step), row(6, step)
    slope = -8.0 * row(7, step)
    prod = jnp.ones((8, HEAD_W), F32)
    state = jnp.zeros((8, HEAD_W), F32)
    back = jnp.zeros((8, HEAD_W), F32)
    for c in range(0, CHIP_TOK, step):
        rows = slice(c, c + step)
        mixed = mix_s[rows, :]
        gate_x = jax.nn.sigmoid(zx_s[rows, :] + b_x)
        gate_a = jax.nn.sigmoid(za_s[rows, :] + b_a)
        x = slope * gate_a
        series = 1.0 / 120.0 + x * (1.0 / 720.0)
        for coef in (1.0 / 24.0, 1.0 / 6.0, 0.5, 1.0):
            series = coef + x * series
        less = x * series
        decay = 1.0 + less
        vari = -less * (2.0 + less)
        mult = jnp.sqrt(vari)
        gk = gate_x * mult
        drive = gk * mixed
        decay_o[0, rows, :] = decay
        drive_o[0, rows, :] = drive
        quot_o[0, rows, :] = (
            gate_x * mixed * (decay * decay) * lax.rsqrt(jnp.maximum(vari, ROOT_FLOOR))
        )
        ga_o[0, rows, :] = -8.0 * gate_a
        gx_o[0, rows, :] = gate_x
        gk_o[0, rows, :] = gk
        for q in (0, 8):
            part = decay[q : q + 8]
            prod = prod * part
            state = part * state + drive[q : q + 8]
            back = back + prod * g_s[c + q : c + q + 8, :]
    sub = lax.broadcasted_iota(jnp.int32, (8, HEAD_W), 0)
    fprod, fstate = prod, state
    bprod, bstate = prod, back
    for d in (1, 2, 4):
        up = sub >= d
        fstate = jnp.where(up, fprod * pltpu.roll(fstate, d, 0) + fstate, fstate)
        fprod = jnp.where(up, fprod * pltpu.roll(fprod, d, 0), fprod)
        down = sub < 8 - d
        bstate = jnp.where(down, bprod * pltpu.roll(bstate, 8 - d, 0) + bstate, bstate)
        bprod = jnp.where(down, bprod * pltpu.roll(bprod, 8 - d, 0), bprod)
    lead_o[0, 0:8, :] = jnp.where(sub == 0, 1.0, pltpu.roll(fprod, 1, 0))
    lead_o[0, 8:16, :] = jnp.where(sub == 0, 0.0, pltpu.roll(fstate, 1, 0))
    lead_o[0, 16:24, :] = jnp.where(sub == 7, 1.0, pltpu.roll(bprod, 7, 0))
    lead_o[0, 24:32, :] = jnp.where(sub == 7, 0.0, pltpu.roll(bstate, 7, 0))
    for i, line in enumerate((fprod[7:8], fstate[7:8], bstate[0:1])):
        for part in range(2):
            total_o[i, pl.ds(2 * h + part, 1), :] = line[:, 128 * part : 128 * part + 128]


def forward_pass(at, *inputs):
    head = lambda h, at: (0, at[0] * HEADS + h)
    saved = pl.BlockSpec((1, CHIP_TOK, HEAD_W), lambda h, at: (h, 0, 0))
    matrix = pl.BlockSpec((1, HEAD_W, HEAD_W), lambda h, at: (h, 0, 0))
    big = (HEADS, CHIP_TOK, HEAD_W)
    return pl.pallas_call(
        forward_kernel,
        grid_spec=pltpu.PrefetchScalarGridSpec(
            num_scalar_prefetch=1,
            grid=(HEADS,),
            in_specs=[pl.BlockSpec((TOK, HEAD_W), head)] * 4
            + [pl.BlockSpec((MARGIN, HEAD_W), lambda h, at: (0, h)), pl.BlockSpec((8, HEAD_W), head)]
            + [matrix] * 2,
            out_specs=[saved] * 9
            + [
                pl.BlockSpec((1, 32, HEAD_W), lambda h, at: (h, 0, 0)),
                pl.BlockSpec((3, 16, 128), lambda h, at: (0, 0, 0)),
            ],
            scratch_shapes=[pltpu.VMEM((EDGE + CHIP_TOK, HEAD_W), F32)]
            + [pltpu.VMEM((CHIP_TOK, HEAD_W), F32)] * 4,
        ),
        out_shape=[jax.ShapeDtypeStruct(big, F32)] * 6
        + [jax.ShapeDtypeStruct(big, BF16)] * 3
        + [
            jax.ShapeDtypeStruct((HEADS, 32, HEAD_W), F32),
            jax.ShapeDtypeStruct((3, 16, 128), F32),
        ],
        compiler_params=pltpu.CompilerParams(vmem_limit_bytes=VMEM_LIMIT),
        cost_estimate=CHEAP,
        name="gates",
    )(at, *inputs)


def join_kernel(axis, first, last, at, own, r1, r2, r3, *refs):
    before = None if first else refs[0]
    outs = refs if first else refs[1:]
    here = at[1 + axis]
    rows = lambda ref: [ref[i] for i in range(3)]
    t0, f0, b0 = rows(own)
    pieces = [rows(r) for r in (r1, r2, r3)]
    one, zero = jnp.ones_like(t0), jnp.zeros_like(t0)
    early = [jnp.full(t0.shape, here + k >= 4) for k in (1, 2, 3)]
    pt, pf = one, zero
    for k in range(3):
        t, f, _ = pieces[k]
        pf = jnp.where(early[k], t * pf + f, pf)
        pt = jnp.where(early[k], t * pt, pt)
    bt, bs = one, zero
    for k in (2, 1, 0):
        t, _, b = pieces[k]
        bs = jnp.where(early[k], bs, t * bs + b)
        bt = jnp.where(early[k], bt, t * bt)
    if first:
        acc = [pt, pf, bt, bs]
    else:
        ep, es, fp, fs = [before[i] for i in range(4)]
        acc = [ep * pt, ep * pf + es, fp * bt, fp * bs + fs]
    if last:
        outs[0][0] = acc[1]
        outs[0][1] = acc[3]
        return
    f = t0 * pf + f0
    for k in range(3):
        f = jnp.where(early[k], f, pieces[k][0] * f + pieces[k][1])
    b = t0 * bs + b0
    for k in (2, 1, 0):
        b = jnp.where(early[k], pieces[k][0] * b + pieces[k][2], b)
    outs[0][0] = pt * t0 * bt
    outs[0][1] = f
    outs[0][2] = b
    for i in range(4):
        outs[1][i] = acc[i]


def entering(at, total):
    acc = None
    value = total
    for axis in (2, 1, 0):
        first, last = axis == 2, axis == 0
        args = [value] + [send_on(value, axis, -k) for k in (1, 2, 3)]
        if not first:
            args.append(acc)
        shapes = [((2, 16, 128), F32)] if last else [((3, 16, 128), F32), ((4, 16, 128), F32)]
        out = on_core(
            functools.partial(join_kernel, axis, first, last), shapes, at, *args, name="join"
        )
        if last:
            return out[0]
        value, acc = out


def backward_kernel(
    k, at, halo_in, par,
    decay, drive, quot, ga, gx, gk, mixed_b, u_b, g_b, w_x, w_a, lead, carry,
    *refs,
):
    pieces, (gm_o, u_s, a_s, dx_s, da_s) = refs[:-5], refs[-5:]
    j = pl.program_id(0)
    h = 2 * lax.rem(at[1] + k, 4) + j
    load_conv_input(u_s, u_b[0].astype(F32), halo_in[...])
    row = lambda k: wide(par[k : k + 1, :], 8)
    entry = [
        wide(
            jnp.concatenate([carry[i, pl.ds(2 * h + p, 1), :] for p in range(2)], axis=1), 8
        )
        for i in range(2)
    ]
    state = lead[0, 8:16, :] + lead[0, 0:8, :] * entry[0]
    back = lead[0, 24:32, :] + lead[0, 16:24, :] * entry[1]
    for r in range(GROUPS - 2, -1, -2):
        grads = g_b[0, 8 * r : 8 * r + 16, :].astype(F32)
        for q in (1, 0):
            rows = slice(8 * (r + q), 8 * (r + q) + 8)
            adjoint = grads[8 * q : 8 * q + 8] + back
            a_s[rows, :] = adjoint
            back = decay[0, rows, :] * adjoint
    rate = row(7)
    eighth = 0.125 * rate
    zero = jnp.zeros((8, HEAD_W), F32)
    sum_x, sum_a, sum_rate = zero, zero, zero
    for r in range(0, GROUPS, 2):
        pair_x, pair_a = [], []
        for q in (r, r + 1):
            rows = slice(8 * q, 8 * q + 8)
            adjoint = a_s[rows, :]
            passed = state * decay[0, rows, :]
            drv = drive[0, rows, :]
            grad_log = adjoint * (passed - quot[0, rows, :])
            state = passed + drv
            gate = ga[0, rows, :]
            term = gate * grad_log
            dz_a = term * (rate + eighth * gate)
            dz_x = adjoint * drv * (1.0 - gx[0, rows, :])
            sum_rate = sum_rate + term
            sum_a = sum_a + dz_a
            sum_x = sum_x + dz_x
            gm_o[0, rows, :] = adjoint * gk[0, rows, :]
            pair_x.append(dz_x)
            pair_a.append(dz_a)
        rows = slice(8 * r, 8 * r + 16)
        dx_s[rows, :] = jnp.concatenate(pair_x, 0).astype(BF16)
        da_s[rows, :] = jnp.concatenate(pair_a, 0).astype(BF16)
    dz_x, dz_a = dx_s[...], da_s[...]
    gm_o[0] += dot(dz_x, w_x[0], ((1,), (1,))) + dot(dz_a, w_a[0], ((1,), (1,)))
    mixed = mixed_b[0]
    grad_w = [dot(mixed, dz, ((0,), (0,))) for dz in (dz_x, dz_a)]
    for n in range(2):

        @pl.when(j == n)
        def _(half=pieces[n]):
            half[:HEAD_W, :HEAD_W] = grad_w[0].astype(half.dtype)
            half[:HEAD_W, HEAD_W:] = grad_w[1].astype(half.dtype)

    sum_c, sum_k = zero, [zero] * (MARGIN + 1)
    for q in range(GROUPS):
        here = gm_o[0, 8 * q : 8 * q + 8, :]
        sum_c = sum_c + here
        for t in range(MARGIN + 1):
            lo = EDGE + 8 * (q - t)
            sum_k[t] = sum_k[t] + here * u_s[lo : lo + 8, :]
    sums = [sum_x, sum_a, sum_rate] + sum_k + [sum_c]
    small = jnp.concatenate([jnp.sum(s, axis=0, keepdims=True) for s in sums], 0)
    if pieces[1].dtype == BF16:
        small = in_two(small)
    pieces[1][HEAD_W:, columns(j * HEAD_W)] = small


def in_two(small):
    high = small.astype(BF16).astype(F32)
    return jnp.concatenate([high, small - high], 0).astype(BF16)


def backward_chunk(k, at, *operands):
    local = lambda j, at: 2 * lax.rem(at[1] + k, 4) + j
    outer = lambda j, at: at[0] * HEADS + local(j, at)
    saved = pl.BlockSpec((1, CHIP_TOK, HEAD_W), lambda j, at: (local(j, at), 0, 0))
    low = ((HEAD_W, BOTH), BF16 if k in (2, 3) else F32)
    high = ((HEAD_W + 16, BOTH), BF16) if k in (1, 2) else ((HEAD_W + 8, BOTH), F32)
    pieces = [low, high]
    return pl.pallas_call(
        functools.partial(backward_kernel, k),
        grid_spec=pltpu.PrefetchScalarGridSpec(
            num_scalar_prefetch=1,
            grid=(2,),
            in_specs=[
                pl.BlockSpec((MARGIN, HEAD_W), lambda j, at: (0, local(j, at))),
                pl.BlockSpec((8, HEAD_W), lambda j, at: (0, outer(j, at))),
            ]
            + [saved] * 11
            + [
                pl.BlockSpec((1, 32, HEAD_W), lambda j, at: (local(j, at), 0, 0)),
                pl.BlockSpec((2, 16, 128), lambda j, at: (0, 0, 0)),
            ],
            out_specs=[pl.BlockSpec(shape, lambda j, at: (0, 0)) for shape, _ in pieces]
            + [pl.BlockSpec((1, CHIP_TOK, HEAD_W), lambda j, at: (j, 0, 0))],
            scratch_shapes=[
                pltpu.VMEM((EDGE + CHIP_TOK, HEAD_W), F32),
                pltpu.VMEM((CHIP_TOK, HEAD_W), F32),
                pltpu.VMEM((CHIP_TOK, HEAD_W), BF16),
                pltpu.VMEM((CHIP_TOK, HEAD_W), BF16),
            ],
        ),
        out_shape=[jax.ShapeDtypeStruct(*piece) for piece in pieces]
        + [jax.ShapeDtypeStruct((2, CHIP_TOK, HEAD_W), F32)],
        compiler_params=pltpu.CompilerParams(vmem_limit_bytes=VMEM_LIMIT),
        cost_estimate=CHEAP,
        name="grads",
    )(at, *operands)


def input_kernel(at, gm0, gm1, gm2, gm3, par, own_o, send_o, edge_o, gm_s, dx_s):
    own, other = orders(at[0])
    sub = lax.broadcasted_iota(jnp.int32, (8, HEAD_W), 0)
    for k, gm in enumerate((gm0, gm1, gm2, gm3)):

        def one_head(j, _):
            h = 2 * lax.rem(at[1] + k, 4) + j
            head = at[0] * HEADS + h
            local, outer = columns(h * HEAD_W), columns(head * HEAD_W)
            for i in range(MARGIN):
                first = gm[j, 8 * i : 8 * i + 8, :]
                edge_o[MARGIN + i : MARGIN + i + 1, local] = first[0:1]
                gm_s[8 * i : 8 * i + 8, :] = jnp.where(sub == 7, 0.0, pltpu.roll(first, 7, 0))
            taps = [wide(par[t : t + 1, outer], 8) for t in range(MARGIN + 1)]
            for r in range(0, GROUPS, 2):
                pair = []
                for q in (r, r + 1):
                    grad = taps[0] * gm[j, 8 * q : 8 * q + 8, :]
                    for t in range(1, MARGIN + 1):
                        lo = 8 * (q + t)
                        if q + t < GROUPS:
                            grad = grad + taps[t] * gm[j, lo : lo + 8, :]
                        else:
                            lo -= CHIP_TOK
                            grad = grad + taps[t] * gm_s[lo : lo + 8, :]
                    if q >= GROUPS - MARGIN:
                        at_edge = q - GROUPS + MARGIN
                        edge_o[at_edge : at_edge + 1, local] = grad[7:8]
                    pair.append(grad)
                dx_s[8 * r : 8 * r + 16, :] = jnp.concatenate(pair, 0).astype(BF16)
            grad_b = dx_s[...]
            own_o[:, local] = dot(own, grad_b, ((0,), (0,))).astype(BF16)
            send_o[:, local] = dot(other, grad_b, ((0,), (0,))).astype(BF16)
            return 0

        lax.fori_loop(0, 2, one_head, 0)


def input_pass(at, par, gms):
    return on_core(
        input_kernel,
        [((TOK, HALF), BF16), ((TOK, HALF), BF16), ((8, HALF), F32)],
        at, *gms, par,
        scratch=[((EDGE, HEAD_W), F32), ((CHIP_TOK, HEAD_W), BF16)],
        name="grad_input",
    )


def merge_kernel(at, mine, half, out):
    out[:HEAD_W, :] = (mine[:HEAD_W, :] + half[:HEAD_W, :].astype(F32)).astype(BF16)
    if out.shape[0] > HEAD_W:
        parts = half[HEAD_W:, :].astype(F32)
        out[HEAD_W:, :] = in_two(mine[HEAD_W:, :] + (parts[0:8] + parts[8:16]))


def merge(at, mine, half):
    (out,) = on_core(merge_kernel, [(half.shape, BF16)], at, mine, half, name="merge")
    return out


def spread_kernel(at, low, high, low1, high1, low2, high2, out):
    small = high[HEAD_W:, :]
    for r in (high1, high2):
        parts = r[HEAD_W:, :].astype(F32)
        small = small + (parts[0:8] + parts[8:16])
    tail = in_two(small)
    for n, (a, b, c) in enumerate(((low, low1, low2), (high, high1, high2))):
        total = a[:HEAD_W, :] + b[:HEAD_W, :].astype(F32) + c[:HEAD_W, :].astype(F32)
        for p in range(PLANE // 2):
            at_chip = n * (PLANE // 2) + p
            out[at_chip, :SHARE, :] = total[SHARE * p : SHARE * (p + 1)].astype(BF16)
            out[at_chip, SHARE:, :] = tail


def plane_kernel(at, pieces, out, tail):
    total = pieces[0].astype(F32)
    for p in range(1, PLANE):
        total = total + pieces[p].astype(F32)
    done = total[:SHARE].astype(BF16)
    for p in range(PLANE):
        out[p] = done
    tail[...] = in_two(total[SHARE : SHARE + 8] + total[SHARE + 8 :])


def trade(pieces):
    groups = [list(range(c, 32, 2)) for c in range(2)]
    return lax.all_to_all(pieces, "inner", 0, 0, axis_index_groups=groups)


def lay_kernel(at, body, tail, low, high):
    for p in range(PLANE // 2):
        rows = slice(SHARE * p, SHARE * (p + 1))
        low[rows, :] = body[p]
        high[rows, :] = body[PLANE // 2 + p]
    high[HEAD_W:, :] = tail[...]


def unpack_kernel(items, count, lines, at, *refs):
    pieces, refs = refs[:count], refs[count:]
    buf, sems = refs[-2:]
    if lines:
        a_param, tails, refs = refs[0], refs[1:9], refs[9:]
        lines_o, refs = refs[-7:-2], refs[:-7] + refs[-2:]
    wx_o, wa_o = refs[-4:-2]
    copies = []
    for parts, k, j, mine in items:
        owner = at[0] if mine else 1 - at[0]
        chunk = j // 2 if k is None else lax.rem(at[1] + k, 4)
        head = owner * HEADS + 2 * chunk + j % 2
        for i, out in enumerate((wx_o, wa_o)):
            n, place = len(copies), 0
            for operand, lead, first, rows in parts:
                ref = pieces[operand] if lead is None else pieces[operand].at[lead]
                buf[n, place : place + rows, :] = ref[
                    first : first + rows, HEAD_W * i : HEAD_W * (i + 1)
                ].astype(F32)
                place += rows
            copies.append(pltpu.make_async_copy(buf.at[n], out.at[head], sems.at[n]))
            copies[n].start()
    if lines:
        bx_o, ba_o, ap_o, taps_o, cb_o = lines_o
        for n, piece in enumerate(tails):
            owner = at[0] if n < 4 else 1 - at[0]
            parts = piece[piece.shape[0] - 16 :, :].astype(F32)
            small = parts[0:8] + parts[8:16]
            cols = columns(owner * HALF + lax.rem(at[1] + n % 4, 4) * BOTH, BOTH)
            bx_o[:, cols] = small[0:1]
            ba_o[:, cols] = small[1:2]
            ap_o[:, cols] = small[2:3] * jax.nn.sigmoid(a_param[:, cols])
            taps_o[:, cols] = small[3:7]
            cb_o[:, cols] = small[7:8]
    for copy in copies:
        copy.wait()


def unpack(at, pieces, items, done, lines=()):
    away = pl.BlockSpec(memory_space=pl.ANY)
    big = jax.ShapeDtypeStruct((2 * HEADS, HEAD_W, HEAD_W), F32)
    line = jax.ShapeDtypeStruct((1, WIDTH), F32)
    taps = jax.ShapeDtypeStruct((MARGIN + 1, WIDTH), F32)
    count, before = len(pieces), 1 + len(pieces) + len(lines)
    return pl.pallas_call(
        functools.partial(unpack_kernel, items, count, bool(lines)),
        in_specs=[pl.BlockSpec(memory_space=pltpu.SMEM)]
        + whole(before - 1)
        + [away] * len(done),
        out_specs=[away] * 2 + whole(5 if lines else 0),
        out_shape=[big, big] + ([line, line, line, taps, line] if lines else []),
        input_output_aliases={before + i: i for i in range(len(done))},
        scratch_shapes=[
            pltpu.VMEM((2 * len(items), HEAD_W, HEAD_W), F32),
            pltpu.SemaphoreType.DMA((2 * len(items),)),
        ],
        compiler_params=pltpu.CompilerParams(vmem_limit_bytes=VMEM_LIMIT),
        cost_estimate=CHEAP,
        name="unpack",
    )(at, *pieces, *lines, *done)


def assemble_kernel(at, own, other, fix, fix_other, out):
    mine, rest = columns(at[0] * HALF, HALF), columns((1 - at[0]) * HALF, HALF)
    out[:, mine] = own[...]
    out[:, rest] = other[...]

    @pl.when(at[0] == 1)
    def _():
        for half, lines, cols in ((own, fix, mine), (other, fix_other, rest)):
            tail = half[TOK - 16 :, :].astype(F32)
            tail = jnp.concatenate([tail[: 16 - MARGIN], lines[0:MARGIN, :].astype(F32)], 0)
            out[TOK - 16 :, cols] = tail.astype(BF16)


def on_device(conv_input, grad_out, conv_w, conv_b, w_x, b_x, w_a, b_a, a_param):
    outer, inner = lax.axis_index("outer"), lax.axis_index("inner")
    core = inner % 2
    at = jnp.stack([core, outer, inner // 8, (inner // 2) % 4]).astype(jnp.int32)
    rate = jax.nn.softplus(a_param)
    par = jnp.concatenate([conv_w, jnp.stack([conv_b, b_x, b_a, rate])], axis=0)
    u_other, g_other = swap_cores(conv_input), swap_cores(grad_out)
    ends = lax.ppermute(
        conv_input[TOK - MARGIN :, :], AXES, [(2 * chip + 1, 2 * chip + 3) for chip in range(63)]
    )
    ends, w_x, w_a = lax.optimization_barrier((ends, w_x, w_a))
    heads = [lax.dynamic_slice_in_dim(w, core * HEADS, HEADS, 0) for w in (w_x, w_a)]
    passed_on = lax.ppermute(
        ends[:, :HALF], AXES, [(2 * chip + 1, 2 * chip) for chip in range(64)]
    )
    halo = jnp.where(core == 0, passed_on, ends[:, HALF:])
    *saved, lead, total = forward_pass(
        at, u_other, g_other, conv_input, grad_out, halo, par, *heads
    )
    operands = (halo, par, *saved, *heads, lead, entering(at, total))
    gms = [None] * 4
    far_low, far_high, gms[2] = backward_chunk(2, at, *operands)
    far_low, far_high = send_on(far_low, 0, 1), send_on(far_high, 0, -1)
    right_low, right_high, gms[1] = backward_chunk(1, at, *operands)
    from_left = send_on(right_high, 0, 1)
    left_low, left_high, gms[3] = backward_chunk(3, at, *operands)
    from_right = send_on(left_low, 0, -1)
    own_low, own_high, gms[0] = backward_chunk(0, at, *operands)
    arrived = (
        send_on(merge(at, right_low, far_low), 0, 1),
        from_left,
        from_right,
        send_on(merge(at, left_high, far_high), 0, -1),
    )

    (pieces,) = on_core(
        spread_kernel,
        [((PLANE, SHARE + 16, BOTH), BF16)],
        at, own_low, own_high, *arrived,
        name="spread",
    )
    pieces, gms = lax.optimization_barrier((pieces, gms))
    traded = trade(pieces)
    own_u, send_u, edge = input_pass(at, par, gms)
    other_u = swap_cores(send_u)
    traded, own_u, other_u, edge = lax.optimization_barrier((traded, own_u, other_u, edge))
    shared, tail = on_core(
        plane_kernel,
        [((PLANE, SHARE, BOTH), BF16), ((16, BOTH), BF16)],
        at, traded,
        name="plane",
    )
    traded = trade(shared)
    low, high = on_core(
        lay_kernel,
        [((HEAD_W, BOTH), BF16), ((HEAD_W + 16, BOTH), BF16)],
        at, traded, tail,
        name="lay",
    )

    left_low, right_high = send_on(low, 0, 1), send_on(high, 0, -1)
    left_high, right_low = send_on(high, 0, 1), send_on(low, 0, -1)
    theirs = [swap_cores(low), swap_cores(high)]
    one = lambda n: ((n, None, 0, HEAD_W),)
    items = [(one(2 * c + j), 0, j, c == 0) for c in range(2) for j in range(2)]
    weights = unpack(at, [low, high] + theirs, items, ())
    edge, theirs = lax.optimization_barrier((edge, theirs))
    far = [send_on(left_low, 0, 1), send_on(right_high, 0, -1)]

    after = lax.ppermute(
        edge[MARGIN : 2 * MARGIN].astype(BF16), AXES, [(i, i - 2) for i in range(2, 128)]
    ).astype(F32)
    cols = lax.dynamic_slice(conv_w, (0, core * HALF), (4, HALF))
    fixed = []
    for m in range(MARGIN):
        line = edge[m]
        for k in range(MARGIN - m, MARGIN + 1):
            line = line + cols[k] * after[m + k - MARGIN]
        fixed.append(line)
    fix = jnp.stack(fixed).astype(BF16)
    (grad_u,) = on_core(
        assemble_kernel,
        [((TOK, WIDTH), BF16)],
        at, own_u, other_u, fix, swap_cores(fix),
        name="assemble",
    )
    first = [right_high, left_low]
    first_other = [swap_cores(piece) for piece in first]
    second = [right_low, left_high]
    items = [(one(0), 1, 1, True), (one(1), 3, 0, True), (one(2), 1, 0, True), (one(3), 3, 1, True)]
    weights = unpack(at, first + second, items, weights)
    far, second, weights, grad_u = lax.optimization_barrier((far, second, weights, grad_u))
    far_other = [swap_cores(piece) for piece in far]
    second_other = [swap_cores(piece) for piece in second]
    items = [(one(0), 2, 0, True), (one(1), 2, 1, True), (one(2), 1, 1, False), (one(3), 3, 0, False)]
    weights = unpack(at, far + first_other, items, weights)
    items = [(one(0), 2, 0, False), (one(1), 2, 1, False), (one(2), 1, 0, False), (one(3), 3, 1, False)]
    tails = [high, right_high, far[1], second[1]]
    tails += [theirs[1], first_other[0], far_other[1], second_other[1]]
    lines = (a_param.reshape(1, WIDTH), *tails)
    *weights, bx, ba, ap, taps, cb = unpack(at, far_other + second_other, items, weights, lines)
    flat = lambda line: line.reshape(WIDTH)
    return (grad_u, *weights, flat(bx), flat(ba), flat(ap), taps, flat(cb))


def solution(mesh):
    split = P(AXES, None)
    return jax.shard_map(
        on_device,
        mesh=mesh,
        in_specs=(split, split) + (P(),) * 7,
        out_specs=(split,) + (P(),) * 7,
        check_vma=False,
    )
```

```python
import functools

import jax
import jax.numpy as jnp
from jax import lax
from jax.experimental import pallas as pl
from jax.experimental.pallas import tpu as pltpu
from jax.sharding import PartitionSpec as P

AXES = ("outer", "inner")
F32, BF16 = jnp.float32, jnp.bfloat16
TOK = 128
CHIP_TOK = 256
GROUPS = CHIP_TOK // 8
WIDTH = 4096
HALF = 2048
HEAD_W = 256
HEADS = 8
PLANE = 16
SHARE = 32
BOTH = 2 * HEAD_W
MARGIN = 3
EDGE = 8 * MARGIN
ROOT_FLOOR = 2.5e-07
VMEM_LIMIT = 16 * 1024 * 1024
CHEAP = pl.CostEstimate(flops=1000, bytes_accessed=1000, transcendentals=0)


def place(index):
    return [index // 32, (index // 8) % 4, (index // 2) % 4, index % 2]


def number(coords):
    return coords[0] * 32 + coords[1] * 8 + coords[2] * 2 + coords[3]


def turned(axis, steps):
    size = 2 if axis == 3 else 4
    pairs = []
    for source in range(128):
        coords = place(source)
        coords[axis] = (coords[axis] + steps) % size
        pairs.append((source, number(coords)))
    return pairs


def send_on(value, axis, steps):
    return lax.ppermute(value, AXES, turned(axis, steps))


def swap_cores(value):
    return send_on(value, 3, 1)


def dot(a, b, dims):
    return lax.dot_general(a, b, (dims, ((), ())), preferred_element_type=F32)


def orders(core):
    row = lax.broadcasted_iota(jnp.int32, (CHIP_TOK, TOK), 0)
    col = lax.broadcasted_iota(jnp.int32, (CHIP_TOK, TOK), 1)
    token = (row % 8) * GROUPS + row // 8
    own = (token == col + core * TOK).astype(F32).astype(BF16)
    other = (token == col + (1 - core) * TOK).astype(F32).astype(BF16)
    return own, other


def wide(row, rows):
    return jnp.broadcast_to(row, (rows, row.shape[1]))


def load_conv_input(u_s, u, halo):
    sub = lax.broadcasted_iota(jnp.int32, (8, HEAD_W), 0)
    u_s[EDGE:, :] = u
    for k in range(1, MARGIN + 1):
        last = u_s[EDGE + CHIP_TOK - 8 * k : EDGE + CHIP_TOK - 8 * (k - 1), :]
        first = wide(halo[MARGIN - k : MARGIN - k + 1, :].astype(F32), 8)
        u_s[EDGE - 8 * k : EDGE - 8 * (k - 1), :] = jnp.where(
            sub == 0, first, pltpu.roll(last, 1, 0)
        )


def whole(count):
    return [pl.BlockSpec(memory_space=pltpu.VMEM)] * count


def on_core(body, shapes, *args, scratch=(), away=(), name):
    specs = [pl.BlockSpec(memory_space=pltpu.SMEM)] + whole(len(args) - 1)
    for i in away:
        specs[i] = pl.BlockSpec(memory_space=pl.ANY)
    return pl.pallas_call(
        body,
        in_specs=specs,
        out_specs=whole(len(shapes)),
        out_shape=[jax.ShapeDtypeStruct(shape, dtype) for shape, dtype in shapes],
        scratch_shapes=[
            s if not isinstance(s, tuple) else pltpu.VMEM(s[0], s[1]) for s in scratch
        ],
        compiler_params=pltpu.CompilerParams(vmem_limit_bytes=VMEM_LIMIT),
        cost_estimate=CHEAP,
        name=name,
    )(*args)


def columns(first, count=HEAD_W):
    return pl.ds(pl.multiple_of(first, count), count)


def forward_kernel(
    at, u_other, g_other, u_own, g_own, halo_in, par, w_x, w_a,
    decay_o, drive_o, quot_o, ga_o, gx_o, gk_o, mixed_o, u_o, g_o, lead_o, total_o,
    u_s, g_s, mix_s, zx_s, za_s,
):
    own, other = orders(at[0])
    step = 16

    h = pl.program_id(0)


    u = dot(own, u_own[...], ((1,), (0,))) + dot(other, u_other[...], ((1,), (0,)))
    g = dot(own, g_own[...], ((1,), (0,))) + dot(other, g_other[...], ((1,), (0,)))
    u_o[0] = u.astype(BF16)
    g_o[0] = g.astype(BF16)
    g_s[...] = g
    load_conv_input(u_s, u, halo_in[...])
    row = lambda k, rows: wide(par[k : k + 1, :], rows)
    taps = [row(k, step) for k in range(MARGIN + 1)]
    bias = row(4, step)
    for c in range(0, CHIP_TOK, step):
        mixed = bias
        for k in range(MARGIN + 1):
            mixed = mixed + taps[k] * u_s[EDGE - 8 * k + c : EDGE - 8 * k + c + step, :]
        mix_s[c : c + step, :] = mixed
        mixed_o[0, c : c + step, :] = mixed.astype(BF16)
    mixed_b = mixed_o[0]
    zx_s[...] = dot(mixed_b, w_x[0], ((1,), (0,)))
    za_s[...] = dot(mixed_b, w_a[0], ((1,), (0,)))
    b_x, b_a = row(5, step), row(6, step)
    slope = -8.0 * row(7, step)
    prod = jnp.ones((8, HEAD_W), F32)
    state = jnp.zeros((8, HEAD_W), F32)
    back = jnp.zeros((8, HEAD_W), F32)
    for c in range(0, CHIP_TOK, step):
        rows = slice(c, c + step)
        mixed = mix_s[rows, :]
        gate_x = jax.nn.sigmoid(zx_s[rows, :] + b_x)
        gate_a = jax.nn.sigmoid(za_s[rows, :] + b_a)
        x = slope * gate_a
        series = 1.0 / 120.0 + x * (1.0 / 720.0)
        for coef in (1.0 / 24.0, 1.0 / 6.0, 0.5, 1.0):
            series = coef + x * series
        less = x * series
        decay = 1.0 + less
        vari = -less * (2.0 + less)
        mult = jnp.sqrt(vari)
        gk = gate_x * mult
        drive = gk * mixed
        decay_o[0, rows, :] = decay
        drive_o[0, rows, :] = drive
        quot_o[0, rows, :] = (
            gate_x * mixed * (decay * decay) * lax.rsqrt(jnp.maximum(vari, ROOT_FLOOR))
        )
        ga_o[0, rows, :] = -8.0 * gate_a
        gx_o[0, rows, :] = gate_x
        gk_o[0, rows, :] = gk
        for q in (0, 8):
            part = decay[q : q + 8]
            prod = prod * part
            state = part * state + drive[q : q + 8]
            back = back + prod * g_s[c + q : c + q + 8, :]
    sub = lax.broadcasted_iota(jnp.int32, (8, HEAD_W), 0)
    fprod, fstate = prod, state
    bprod, bstate = prod, back
    for d in (1, 2, 4):
        up = sub >= d
        fstate = jnp.where(up, fprod * pltpu.roll(fstate, d, 0) + fstate, fstate)
        fprod = jnp.where(up, fprod * pltpu.roll(fprod, d, 0), fprod)
        down = sub < 8 - d
        bstate = jnp.where(down, bprod * pltpu.roll(bstate, 8 - d, 0) + bstate, bstate)
        bprod = jnp.where(down, bprod * pltpu.roll(bprod, 8 - d, 0), bprod)
    lead_o[0, 0:8, :] = jnp.where(sub == 0, 1.0, pltpu.roll(fprod, 1, 0))
    lead_o[0, 8:16, :] = jnp.where(sub == 0, 0.0, pltpu.roll(fstate, 1, 0))
    lead_o[0, 16:24, :] = jnp.where(sub == 7, 1.0, pltpu.roll(bprod, 7, 0))
    lead_o[0, 24:32, :] = jnp.where(sub == 7, 0.0, pltpu.roll(bstate, 7, 0))
    for i, line in enumerate((fprod[7:8], fstate[7:8], bstate[0:1])):
        for part in range(2):
            total_o[i, pl.ds(2 * h + part, 1), :] = line[:, 128 * part : 128 * part + 128]


def forward_pass(at, *inputs):
    head = lambda h, at: (0, at[0] * HEADS + h)
    saved = pl.BlockSpec((1, CHIP_TOK, HEAD_W), lambda h, at: (h, 0, 0))
    matrix = pl.BlockSpec((1, HEAD_W, HEAD_W), lambda h, at: (h, 0, 0))
    big = (HEADS, CHIP_TOK, HEAD_W)
    return pl.pallas_call(
        forward_kernel,
        grid_spec=pltpu.PrefetchScalarGridSpec(
            num_scalar_prefetch=1,
            grid=(HEADS,),
            in_specs=[pl.BlockSpec((TOK, HEAD_W), head)] * 4
            + [pl.BlockSpec((MARGIN, HEAD_W), lambda h, at: (0, h)), pl.BlockSpec((8, HEAD_W), head)]
            + [matrix] * 2,
            out_specs=[saved] * 9
            + [
                pl.BlockSpec((1, 32, HEAD_W), lambda h, at: (h, 0, 0)),
                pl.BlockSpec((3, 16, 128), lambda h, at: (0, 0, 0)),
            ],
            scratch_shapes=[pltpu.VMEM((EDGE + CHIP_TOK, HEAD_W), F32)]
            + [pltpu.VMEM((CHIP_TOK, HEAD_W), F32)] * 4,
        ),
        out_shape=[jax.ShapeDtypeStruct(big, F32)] * 6
        + [jax.ShapeDtypeStruct(big, BF16)] * 3
        + [
            jax.ShapeDtypeStruct((HEADS, 32, HEAD_W), F32),
            jax.ShapeDtypeStruct((3, 16, 128), F32),
        ],
        compiler_params=pltpu.CompilerParams(vmem_limit_bytes=VMEM_LIMIT),
        cost_estimate=CHEAP,
        name="gates",
    )(at, *inputs)


def join_kernel(axis, first, last, at, own, r1, r2, r3, *refs):
    before = None if first else refs[0]
    outs = refs if first else refs[1:]
    here = at[1 + axis]
    rows = lambda ref: [ref[i] for i in range(3)]
    t0, f0, b0 = rows(own)
    pieces = [rows(r) for r in (r1, r2, r3)]
    one, zero = jnp.ones_like(t0), jnp.zeros_like(t0)
    early = [jnp.full(t0.shape, here + k >= 4) for k in (1, 2, 3)]
    pt, pf = one, zero
    for k in range(3):
        t, f, _ = pieces[k]
        pf = jnp.where(early[k], t * pf + f, pf)
        pt = jnp.where(early[k], t * pt, pt)
    bt, bs = one, zero
    for k in (2, 1, 0):
        t, _, b = pieces[k]
        bs = jnp.where(early[k], bs, t * bs + b)
        bt = jnp.where(early[k], bt, t * bt)
    if first:
        acc = [pt, pf, bt, bs]
    else:
        ep, es, fp, fs = [before[i] for i in range(4)]
        acc = [ep * pt, ep * pf + es, fp * bt, fp * bs + fs]
    if last:
        outs[0][0] = acc[1]
        outs[0][1] = acc[3]
        return
    f = t0 * pf + f0
    for k in range(3):
        f = jnp.where(early[k], f, pieces[k][0] * f + pieces[k][1])
    b = t0 * bs + b0
    for k in (2, 1, 0):
        b = jnp.where(early[k], pieces[k][0] * b + pieces[k][2], b)
    outs[0][0] = pt * t0 * bt
    outs[0][1] = f
    outs[0][2] = b
    for i in range(4):
        outs[1][i] = acc[i]


def entering(at, total):
    acc = None
    value = total
    for axis in (2, 1, 0):
        first, last = axis == 2, axis == 0
        args = [value] + [send_on(value, axis, -k) for k in (1, 2, 3)]
        if not first:
            args.append(acc)
        shapes = [((2, 16, 128), F32)] if last else [((3, 16, 128), F32), ((4, 16, 128), F32)]
        out = on_core(
            functools.partial(join_kernel, axis, first, last), shapes, at, *args, name="join"
        )
        if last:
            return out[0]
        value, acc = out


def backward_kernel(
    k, at, halo_in, par,
    decay, drive, quot, ga, gx, gk, mixed_b, u_b, g_b, w_x, w_a, lead, carry,
    *refs,
):
    pieces, (gm_o, u_s, a_s, dx_s, da_s) = refs[:-5], refs[-5:]
    j = pl.program_id(0)
    h = 2 * lax.rem(at[1] + k, 4) + j
    load_conv_input(u_s, u_b[0].astype(F32), halo_in[...])
    row = lambda k: wide(par[k : k + 1, :], 8)
    entry = [
        wide(
            jnp.concatenate([carry[i, pl.ds(2 * h + p, 1), :] for p in range(2)], axis=1), 8
        )
        for i in range(2)
    ]
    state = lead[0, 8:16, :] + lead[0, 0:8, :] * entry[0]
    back = lead[0, 24:32, :] + lead[0, 16:24, :] * entry[1]
    for r in range(GROUPS - 2, -1, -2):
        grads = g_b[0, 8 * r : 8 * r + 16, :].astype(F32)
        for q in (1, 0):
            rows = slice(8 * (r + q), 8 * (r + q) + 8)
            adjoint = grads[8 * q : 8 * q + 8] + back
            a_s[rows, :] = adjoint
            back = decay[0, rows, :] * adjoint
    rate = row(7)
    eighth = 0.125 * rate
    zero = jnp.zeros((8, HEAD_W), F32)
    sum_x, sum_a, sum_rate = zero, zero, zero
    for r in range(0, GROUPS, 2):
        pair_x, pair_a = [], []
        for q in (r, r + 1):
            rows = slice(8 * q, 8 * q + 8)
            adjoint = a_s[rows, :]
            passed = state * decay[0, rows, :]
            drv = drive[0, rows, :]
            grad_log = adjoint * (passed - quot[0, rows, :])
            state = passed + drv
            gate = ga[0, rows, :]
            term = gate * grad_log
            dz_a = term * (rate + eighth * gate)
            dz_x = adjoint * drv * (1.0 - gx[0, rows, :])
            sum_rate = sum_rate + term
            sum_a = sum_a + dz_a
            sum_x = sum_x + dz_x
            gm_o[0, rows, :] = adjoint * gk[0, rows, :]
            pair_x.append(dz_x)
            pair_a.append(dz_a)
        rows = slice(8 * r, 8 * r + 16)
        dx_s[rows, :] = jnp.concatenate(pair_x, 0).astype(BF16)
        da_s[rows, :] = jnp.concatenate(pair_a, 0).astype(BF16)
    dz_x, dz_a = dx_s[...], da_s[...]
    gm_o[0] += dot(dz_x, w_x[0], ((1,), (1,))) + dot(dz_a, w_a[0], ((1,), (1,)))
    mixed = mixed_b[0]
    grad_w = [dot(mixed, dz, ((0,), (0,))) for dz in (dz_x, dz_a)]
    for n in range(2):

        @pl.when(j == n)
        def _(half=pieces[n]):
            half[:HEAD_W, :HEAD_W] = grad_w[0].astype(half.dtype)
            half[:HEAD_W, HEAD_W:] = grad_w[1].astype(half.dtype)

    sum_c, sum_k = zero, [zero] * (MARGIN + 1)
    for q in range(GROUPS):
        here = gm_o[0, 8 * q : 8 * q + 8, :]
        sum_c = sum_c + here
        for t in range(MARGIN + 1):
            lo = EDGE + 8 * (q - t)
            sum_k[t] = sum_k[t] + here * u_s[lo : lo + 8, :]
    sums = [sum_x, sum_a, sum_rate] + sum_k + [sum_c]
    small = jnp.concatenate([jnp.sum(s, axis=0, keepdims=True) for s in sums], 0)
    if pieces[1].dtype == BF16:
        small = in_two(small)
    pieces[1][HEAD_W:, columns(j * HEAD_W)] = small


def in_two(small):
    high = small.astype(BF16).astype(F32)
    return jnp.concatenate([high, small - high], 0).astype(BF16)


def backward_chunk(k, at, *operands):
    local = lambda j, at: 2 * lax.rem(at[1] + k, 4) + j
    outer = lambda j, at: at[0] * HEADS + local(j, at)
    saved = pl.BlockSpec((1, CHIP_TOK, HEAD_W), lambda j, at: (local(j, at), 0, 0))
    low = ((HEAD_W, BOTH), BF16 if k in (2, 3) else F32)
    high = ((HEAD_W + 16, BOTH), BF16) if k in (1, 2) else ((HEAD_W + 8, BOTH), F32)
    pieces = [low, high]
    return pl.pallas_call(
        functools.partial(backward_kernel, k),
        grid_spec=pltpu.PrefetchScalarGridSpec(
            num_scalar_prefetch=1,
            grid=(2,),
            in_specs=[
                pl.BlockSpec((MARGIN, HEAD_W), lambda j, at: (0, local(j, at))),
                pl.BlockSpec((8, HEAD_W), lambda j, at: (0, outer(j, at))),
            ]
            + [saved] * 11
            + [
                pl.BlockSpec((1, 32, HEAD_W), lambda j, at: (local(j, at), 0, 0)),
                pl.BlockSpec((2, 16, 128), lambda j, at: (0, 0, 0)),
            ],
            out_specs=[pl.BlockSpec(shape, lambda j, at: (0, 0)) for shape, _ in pieces]
            + [pl.BlockSpec((1, CHIP_TOK, HEAD_W), lambda j, at: (j, 0, 0))],
            scratch_shapes=[
                pltpu.VMEM((EDGE + CHIP_TOK, HEAD_W), F32),
                pltpu.VMEM((CHIP_TOK, HEAD_W), F32),
                pltpu.VMEM((CHIP_TOK, HEAD_W), BF16),
                pltpu.VMEM((CHIP_TOK, HEAD_W), BF16),
            ],
        ),
        out_shape=[jax.ShapeDtypeStruct(*piece) for piece in pieces]
        + [jax.ShapeDtypeStruct((2, CHIP_TOK, HEAD_W), F32)],
        compiler_params=pltpu.CompilerParams(vmem_limit_bytes=VMEM_LIMIT),
        cost_estimate=CHEAP,
        name="grads",
    )(at, *operands)


def input_kernel(at, gm0, gm1, gm2, gm3, par, own_o, send_o, edge_o, gm_s, dx_s):
    own, other = orders(at[0])
    sub = lax.broadcasted_iota(jnp.int32, (8, HEAD_W), 0)
    for k, gm in enumerate((gm0, gm1, gm2, gm3)):

        def one_head(j, _):
            h = 2 * lax.rem(at[1] + k, 4) + j
            head = at[0] * HEADS + h
            local, outer = columns(h * HEAD_W), columns(head * HEAD_W)
            for i in range(MARGIN):
                first = gm[j, 8 * i : 8 * i + 8, :]
                edge_o[MARGIN + i : MARGIN + i + 1, local] = first[0:1]
                gm_s[8 * i : 8 * i + 8, :] = jnp.where(sub == 7, 0.0, pltpu.roll(first, 7, 0))
            taps = [wide(par[t : t + 1, outer], 8) for t in range(MARGIN + 1)]
            for r in range(0, GROUPS, 2):
                pair = []
                for q in (r, r + 1):
                    grad = taps[0] * gm[j, 8 * q : 8 * q + 8, :]
                    for t in range(1, MARGIN + 1):
                        lo = 8 * (q + t)
                        if q + t < GROUPS:
                            grad = grad + taps[t] * gm[j, lo : lo + 8, :]
                        else:
                            lo -= CHIP_TOK
                            grad = grad + taps[t] * gm_s[lo : lo + 8, :]
                    if q >= GROUPS - MARGIN:
                        at_edge = q - GROUPS + MARGIN
                        edge_o[at_edge : at_edge + 1, local] = grad[7:8]
                    pair.append(grad)
                dx_s[8 * r : 8 * r + 16, :] = jnp.concatenate(pair, 0).astype(BF16)
            grad_b = dx_s[...]
            own_o[:, local] = dot(own, grad_b, ((0,), (0,))).astype(BF16)
            send_o[:, local] = dot(other, grad_b, ((0,), (0,))).astype(BF16)
            return 0

        lax.fori_loop(0, 2, one_head, 0)


def input_pass(at, par, gms):
    return on_core(
        input_kernel,
        [((TOK, HALF), BF16), ((TOK, HALF), BF16), ((8, HALF), F32)],
        at, *gms, par,
        scratch=[((EDGE, HEAD_W), F32), ((CHIP_TOK, HEAD_W), BF16)],
        name="grad_input",
    )


def merge_kernel(at, mine, half, out):
    out[:HEAD_W, :] = (mine[:HEAD_W, :] + half[:HEAD_W, :].astype(F32)).astype(BF16)
    if out.shape[0] > HEAD_W:
        parts = half[HEAD_W:, :].astype(F32)
        out[HEAD_W:, :] = in_two(mine[HEAD_W:, :] + (parts[0:8] + parts[8:16]))


def merge(at, mine, half):
    (out,) = on_core(merge_kernel, [(half.shape, BF16)], at, mine, half, name="merge")
    return out


def spread_kernel(at, low, high, low1, high1, low2, high2, out):
    small = high[HEAD_W:, :]
    for r in (high1, high2):
        parts = r[HEAD_W:, :].astype(F32)
        small = small + (parts[0:8] + parts[8:16])
    tail = in_two(small)
    for n, (a, b, c) in enumerate(((low, low1, low2), (high, high1, high2))):

        @pl.when(pl.program_id(0) == n)
        def _(a=a, b=b, c=c):
            total = a[:HEAD_W, :] + b[:HEAD_W, :].astype(F32) + c[:HEAD_W, :].astype(F32)
            for p in range(PLANE // 2):
                out[p, :SHARE, :] = total[SHARE * p : SHARE * (p + 1)].astype(BF16)
                out[p, SHARE:, :] = tail


def spread(at, *args):
    half = (PLANE // 2, SHARE + 16, BOTH)
    return pl.pallas_call(
        spread_kernel,
        grid=(2,),
        in_specs=[pl.BlockSpec(memory_space=pltpu.SMEM)] + whole(len(args)),
        out_specs=pl.BlockSpec(half, lambda n: (n, 0, 0)),
        out_shape=jax.ShapeDtypeStruct((PLANE, SHARE + 16, BOTH), BF16),
        compiler_params=pltpu.CompilerParams(vmem_limit_bytes=VMEM_LIMIT),
        cost_estimate=CHEAP,
        name="spread",
    )(at, *args)


def plane_kernel(at, pieces, out, tail):
    total = pieces[0].astype(F32)
    for p in range(1, PLANE):
        total = total + pieces[p].astype(F32)
    done = total[:SHARE].astype(BF16)
    for p in range(PLANE):
        out[p] = done
    tail[...] = in_two(total[SHARE : SHARE + 8] + total[SHARE + 8 :])


def trade(pieces):
    groups = [list(range(c, 32, 2)) for c in range(2)]
    return lax.all_to_all(pieces, "inner", 0, 0, axis_index_groups=groups)


def lay_kernel(at, body, tail, low, high):
    for p in range(PLANE // 2):
        rows = slice(SHARE * p, SHARE * (p + 1))
        low[rows, :] = body[p]
        high[rows, :] = body[PLANE // 2 + p]
    high[HEAD_W:, :] = tail[...]


def unpack_kernel(items, count, lines, at, *refs):
    pieces, refs = refs[:count], refs[count:]
    buf, sems = refs[-2:]
    if lines:
        a_param, tails, refs = refs[0], refs[1:9], refs[9:]
        lines_o, refs = refs[-7:-2], refs[:-7] + refs[-2:]
    wx_o, wa_o = refs[-4:-2]
    copies = []
    for parts, k, j, mine in items:
        owner = at[0] if mine else 1 - at[0]
        chunk = j // 2 if k is None else lax.rem(at[1] + k, 4)
        head = owner * HEADS + 2 * chunk + j % 2
        for i, out in enumerate((wx_o, wa_o)):
            n, place = len(copies), 0
            for operand, lead, first, rows in parts:
                ref = pieces[operand] if lead is None else pieces[operand].at[lead]
                buf[n, place : place + rows, :] = ref[
                    first : first + rows, HEAD_W * i : HEAD_W * (i + 1)
                ].astype(F32)
                place += rows
            copies.append(pltpu.make_async_copy(buf.at[n], out.at[head], sems.at[n]))
            copies[n].start()
    if lines:
        bx_o, ba_o, ap_o, taps_o, cb_o = lines_o
        for n, piece in enumerate(tails):
            owner = at[0] if n < 4 else 1 - at[0]
            parts = piece[piece.shape[0] - 16 :, :].astype(F32)
            small = parts[0:8] + parts[8:16]
            cols = columns(owner * HALF + lax.rem(at[1] + n % 4, 4) * BOTH, BOTH)
            bx_o[:, cols] = small[0:1]
            ba_o[:, cols] = small[1:2]
            ap_o[:, cols] = small[2:3] * jax.nn.sigmoid(a_param[:, cols])
            taps_o[:, cols] = small[3:7]
            cb_o[:, cols] = small[7:8]
    for copy in copies:
        copy.wait()


def unpack(at, pieces, items, done, lines=()):
    away = pl.BlockSpec(memory_space=pl.ANY)
    big = jax.ShapeDtypeStruct((2 * HEADS, HEAD_W, HEAD_W), F32)
    line = jax.ShapeDtypeStruct((1, WIDTH), F32)
    taps = jax.ShapeDtypeStruct((MARGIN + 1, WIDTH), F32)
    count, before = len(pieces), 1 + len(pieces) + len(lines)
    return pl.pallas_call(
        functools.partial(unpack_kernel, items, count, bool(lines)),
        in_specs=[pl.BlockSpec(memory_space=pltpu.SMEM)]
        + whole(before - 1)
        + [away] * len(done),
        out_specs=[away] * 2 + whole(5 if lines else 0),
        out_shape=[big, big] + ([line, line, line, taps, line] if lines else []),
        input_output_aliases={before + i: i for i in range(len(done))},
        scratch_shapes=[
            pltpu.VMEM((2 * len(items), HEAD_W, HEAD_W), F32),
            pltpu.SemaphoreType.DMA((2 * len(items),)),
        ],
        compiler_params=pltpu.CompilerParams(vmem_limit_bytes=VMEM_LIMIT),
        cost_estimate=CHEAP,
        name="unpack",
    )(at, *pieces, *lines, *done)


def assemble_kernel(at, own, other, fix, fix_other, out):
    mine, rest = columns(at[0] * HALF, HALF), columns((1 - at[0]) * HALF, HALF)
    out[:, mine] = own[...]
    out[:, rest] = other[...]

    @pl.when(at[0] == 1)
    def _():
        for half, lines, cols in ((own, fix, mine), (other, fix_other, rest)):
            tail = half[TOK - 16 :, :].astype(F32)
            tail = jnp.concatenate([tail[: 16 - MARGIN], lines[0:MARGIN, :].astype(F32)], 0)
            out[TOK - 16 :, cols] = tail.astype(BF16)


def on_device(conv_input, grad_out, conv_w, conv_b, w_x, b_x, w_a, b_a, a_param):
    outer, inner = lax.axis_index("outer"), lax.axis_index("inner")
    core = inner % 2
    at = jnp.stack([core, outer, inner // 8, (inner // 2) % 4]).astype(jnp.int32)
    rate = jax.nn.softplus(a_param)
    par = jnp.concatenate([conv_w, jnp.stack([conv_b, b_x, b_a, rate])], axis=0)
    last = conv_input[TOK - MARGIN :, :]
    last, u_mine, g_mine = lax.optimization_barrier((last, conv_input, grad_out))
    u_other, g_other = swap_cores(u_mine), swap_cores(g_mine)
    ends = lax.ppermute(
        last, AXES, [(2 * chip + 1, 2 * chip + 3) for chip in range(63)]
    )
    ends, w_x, w_a = lax.optimization_barrier((ends, w_x, w_a))
    heads = [lax.dynamic_slice_in_dim(w, core * HEADS, HEADS, 0) for w in (w_x, w_a)]
    passed_on = lax.ppermute(
        ends[:, :HALF], AXES, [(2 * chip + 1, 2 * chip) for chip in range(64)]
    )
    halo = jnp.where(core == 0, passed_on, ends[:, HALF:])
    *saved, lead, total = forward_pass(
        at, u_other, g_other, conv_input, grad_out, halo, par, *heads
    )
    operands = (halo, par, *saved, *heads, lead, entering(at, total))
    gms = [None] * 4
    far_low, far_high, gms[2] = backward_chunk(2, at, *operands)
    far_low, far_high = send_on(far_low, 0, 1), send_on(far_high, 0, -1)
    right_low, right_high, gms[1] = backward_chunk(1, at, *operands)
    from_left = send_on(right_high, 0, 1)
    left_low, left_high, gms[3] = backward_chunk(3, at, *operands)
    from_right = send_on(left_low, 0, -1)
    own_low, own_high, gms[0] = backward_chunk(0, at, *operands)
    arrived = (
        send_on(merge(at, right_low, far_low), 0, 1),
        from_left,
        from_right,
        send_on(merge(at, left_high, far_high), 0, -1),
    )

    pieces = spread(at, own_low, own_high, *arrived)
    pieces, gms = lax.optimization_barrier((pieces, gms))
    traded = trade(pieces)
    own_u, send_u, edge = input_pass(at, par, gms)
    other_u = swap_cores(send_u)
    traded, own_u, other_u, edge = lax.optimization_barrier((traded, own_u, other_u, edge))
    shared, tail = on_core(
        plane_kernel,
        [((PLANE, SHARE, BOTH), BF16), ((16, BOTH), BF16)],
        at, traded,
        name="plane",
    )
    traded = trade(shared)
    low, high = on_core(
        lay_kernel,
        [((HEAD_W, BOTH), BF16), ((HEAD_W + 16, BOTH), BF16)],
        at, traded, tail,
        name="lay",
    )

    left_low, right_high = send_on(low, 0, 1), send_on(high, 0, -1)
    left_high, right_low = send_on(high, 0, 1), send_on(low, 0, -1)
    theirs = [swap_cores(low), swap_cores(high)]
    one = lambda n: ((n, None, 0, HEAD_W),)
    items = [(one(2 * c + j), 0, j, c == 0) for c in range(2) for j in range(2)]
    weights = unpack(at, [low, high] + theirs, items, ())
    edge, theirs = lax.optimization_barrier((edge, theirs))
    far = [send_on(left_low, 0, 1), send_on(right_high, 0, -1)]

    after = lax.ppermute(
        edge[MARGIN : 2 * MARGIN].astype(BF16), AXES, [(i, i - 2) for i in range(2, 128)]
    ).astype(F32)
    cols = lax.dynamic_slice(conv_w, (0, core * HALF), (4, HALF))
    fixed = []
    for m in range(MARGIN):
        line = edge[m]
        for k in range(MARGIN - m, MARGIN + 1):
            line = line + cols[k] * after[m + k - MARGIN]
        fixed.append(line)
    fix = jnp.stack(fixed).astype(BF16)
    (grad_u,) = on_core(
        assemble_kernel,
        [((TOK, WIDTH), BF16)],
        at, own_u, other_u, fix, swap_cores(fix),
        name="assemble",
    )
    first = [right_high, left_low]
    first_other = [swap_cores(piece) for piece in first]
    second = [right_low, left_high]
    items = [(one(0), 1, 1, True), (one(1), 3, 0, True), (one(2), 1, 0, True), (one(3), 3, 1, True)]
    weights = unpack(at, first + second, items, weights)
    far, weights, grad_u = lax.optimization_barrier((far, weights, grad_u))
    far_other = [swap_cores(piece) for piece in far]
    second_other = [swap_cores(piece) for piece in second]
    items = [(one(0), 2, 0, True), (one(1), 2, 1, True), (one(2), 1, 1, False), (one(3), 3, 0, False)]
    weights = unpack(at, far + first_other, items, weights)
    items = [(one(0), 2, 0, False), (one(1), 2, 1, False), (one(2), 1, 0, False), (one(3), 3, 1, False)]
    tails = [high, right_high, far[1], second[1]]
    tails += [theirs[1], first_other[0], far_other[1], second_other[1]]
    lines = (a_param.reshape(1, WIDTH), *tails)
    *weights, bx, ba, ap, taps, cb = unpack(at, far_other + second_other, items, weights, lines)
    flat = lambda line: line.reshape(WIDTH)
    return (grad_u, *weights, flat(bx), flat(ba), flat(ap), taps, flat(cb))


def solution(mesh):
    split = P(AXES, None)
    return jax.shard_map(
        on_device,
        mesh=mesh,
        in_specs=(split, split) + (P(),) * 7,
        out_specs=(split,) + (P(),) * 7,
        check_vma=False,
    )
```
